32 devices in a mesh: shard: 8 (over y, x, core), rep: 4 (over z).
Axes of the slice: x: 2, y: 2, z: 4, core: 2. Of those that a mesh axis runs over, the one named last changes fastest.
Arguments:
- tokens: bfloat16 [16384, 1472], P(('shard', 'rep')), may hold values from -6 to 6
- cotangent: bfloat16 [16384, 1472], P(('shard', 'rep')), may hold values from -6 to 6
- buckets: int32 [1023], replicated, may hold values from 0 to 31
- bias_table: bfloat16 [32, 6], replicated, may hold values from -4 to 4
- attn_gain: bfloat16 [1472], P('shard'), may hold values from 0.25 to 1.75
- w_query: bfloat16 [1472, 384], P('shard'), may hold values from -0.0390625 to 0.0390625
- w_key: bfloat16 [1472, 384], P('shard'), may hold values from -0.15625 to 0.15625
- w_value: bfloat16 [1472, 384], P('shard'), may hold values from -0.15625 to 0.15625
- w_output: bfloat16 [1472, 384], P('shard'), may hold values from -1.25 to 1.25
- ffn_gain: bfloat16 [1472], P('shard'), may hold values from 0.25 to 1.75
- w_gate: bfloat16 [1472, 3584], P('shard'), may hold values from -0.15625 to 0.15625
- w_up: bfloat16 [1472, 3584], P('shard'), may hold values from -0.15625 to 0.15625
- w_down: bfloat16 [1472, 3584], P('shard'), may hold values from -0.09375 to 0.09375
Outputs:
- layer_out: bfloat16 [16384, 1472], P(('shard', 'rep'))
- grad_tokens: bfloat16 [16384, 1472], P(('shard', 'rep'))
- grad_attn_gain: float32 [1472], P('shard')
- grad_w_query: float32 [1472, 384], P('shard')
- grad_w_key: float32 [1472, 384], P('shard')
- grad_w_value: float32 [1472, 384], P('shard')
- grad_w_output: float32 [1472, 384], P('shard')
- grad_ffn_gain: float32 [1472], P('shard')
- grad_w_gate: float32 [1472, 3584], P('shard')
- grad_w_up: float32 [1472, 3584], P('shard')
- grad_w_down: float32 [1472, 3584], P('shard')
- grad_bias_table: float32 [32, 6], replicated
The draws below stay inside these ranges and needn't reach their ends.
All inputs are finite; a program needn't handle non-finite values.
Results may differ from the reference program's by a relative error of at most 0.015.
The reference program's roundings to bfloat16 on the way count: a program that leaves them out, or rounds other values in their place, can miss the bound.
Values may be sent and summed in bfloat16 or wider, within the bound.
A program may use at most 320 MiB of HBM per device.

```python
import jax
import jax.numpy as jnp
from jax import lax

D = 1472
HEADS = 6
HEAD_DIM = 64
FF = 3584
BUCKETS = 32
BLOCK = 256
TOK_DEV = 512
INNER = 384
TOKENS = 16384


def place_ends(entries, rng, least, top_value):
    spot = [jax.random.randint(jax.random.fold_in(rng, axis), (), 0, length) for axis, length in enumerate(entries.shape)]
    longest = entries.shape.index(max(entries.shape))
    beside = spot[:longest] + [(spot[longest] + 1) % entries.shape[longest]] + spot[longest + 1:]
    return entries.at[tuple(spot)].set(least).at[tuple(beside)].set(top_value)


def spiked(drawn, key, source, target, shards_of, factor):
    owner, partner = [(jnp.arange(drawn.shape[dim]) // (drawn.shape[dim] // shards_of)).reshape([-1 if axis == dim else 1 for axis in range(drawn.ndim)]) for dim in (source, target)]
    chosen = jax.random.permutation(key, shards_of)[partner]
    strong = (owner == chosen) | (owner == (partner + shards_of // 2) % shards_of)
    return jnp.where(strong, factor * drawn, drawn)


def block_scale(key, extent, shards, low, largest):
    loudness = 1.0
    for axis_at, shards_of in shards:
        heights = jax.random.uniform(jax.random.fold_in(jax.random.fold_in(key, 6), axis_at), (shards_of,), jnp.float32, low / len(shards), largest / len(shards))
        loudness = loudness * jnp.repeat(jnp.exp(heights), extent[axis_at] // shards_of).reshape((-1,) + (1,) * (len(extent) - 1 - axis_at))
    return loudness


def scatter_about(key, extent, deviation, bound, cuts=(), held_as=jnp.bfloat16):
    result = jax.random.normal(key, extent, jnp.float32) * deviation
    if len(cuts) > 0:
        result = block_scale(key, extent, cuts, -0.22, 0.18) * result
    return jnp.clip(result, min=-bound, max=bound).astype(held_as)


def bell_draw_with(rng, shape, spread, bound, cuts, heavy, dtype=jnp.bfloat16):
    values = spread * jax.random.normal(rng, shape, jnp.float32)
    if cuts:
        values = values * block_scale(rng, shape, cuts, -0.22, 0.18)
    return jnp.clip(spiked(values, jax.random.fold_in(rng, 3), *heavy), -bound, bound).astype(dtype)


def setup_inputs(seed: int = 0) -> dict:
    key_list = jax.random.split(jax.random.key(seed), 14)
    tokens = scatter_about(key_list[0], (TOKENS, D), 1.0, 6.0, ((0, 32),))
    cotangent = bell_draw_with(key_list[1], (TOKENS, D), 1.0, 6.0, ((0, 32),), (0, 1, 32, 2.75))
    buckets = place_ends(jax.random.randint(key_list[2], (2 * TOK_DEV - 1,), 0, BUCKETS), jax.random.fold_in(key_list[2], 1), 0, BUCKETS - 1).astype(jnp.int32)
    bias_table = scatter_about(key_list[3], (BUCKETS, HEADS), 1.0, 4.0)
    attn_gain = jnp.clip(1.0 + 0.15 * jax.random.normal(key_list[4], (D,), jnp.float32), 0.25, 1.75).astype(jnp.bfloat16)
    w_query = scatter_about(key_list[5], (D, INNER), (16 * D) ** -0.5, 0.0390625, ((0, 8),))
    w_key = scatter_about(key_list[6], (D, INNER), D ** -0.5, 0.15625, ((0, 8),))
    w_value = scatter_about(key_list[7], (D, INNER), D ** -0.5, 0.15625, ((0, 8),))
    w_output = scatter_about(key_list[8], (D, INNER), (INNER // 16) ** -0.5, 1.25, ((0, 8),))
    ffn_gain = jnp.clip(1.0 + 0.15 * jax.random.normal(key_list[9], (D,), jnp.float32), 0.25, 1.75).astype(jnp.bfloat16)
    w_gate = scatter_about(key_list[10], (D, FF), D ** -0.5, 0.15625, ((0, 8),))
    w_up = scatter_about(key_list[11], (D, FF), D ** -0.5, 0.15625, ((0, 8),))
    w_down = scatter_about(key_list[12], (D, FF), FF ** -0.5, 0.09375, ((0, 8),))
    return {"tokens": tokens, "cotangent": cotangent, "buckets": buckets, "bias_table": bias_table, "attn_gain": attn_gain, "w_query": w_query, "w_key": w_key, "w_value": w_value, "w_output": w_output, "ffn_gain": ffn_gain, "w_gate": w_gate, "w_up": w_up, "w_down": w_down}


@jax.custom_vjp
def low(v):
    return lax.optimization_barrier(v.astype(jnp.bfloat16)).astype(jnp.float32)

@jax.custom_vjp
def low_back(v):
    return v

def low_keep(v):
    return (low(v), None)

def low_pass(kept, grad):
    return (grad,)

def back_keep(v):
    return (v, None)

def back_low(kept, grad):
    return (low(grad),)
low.defvjp(low_keep, low_pass)
low_back.defvjp(back_keep, back_low)
norm_eps = 1e-06
masked_score = -1e+30
highest = lax.Precision.HIGHEST

def rms_norm(row_values, gain_vector):
    return row_values * lax.rsqrt(lax.optimization_barrier(jnp.mean(row_values * row_values, axis=-1, keepdims=True)) + norm_eps) * gain_vector

def layer_forward(seq_rows, weights, buckets):
    attn_gain, w_query, w_key, w_value, w_output, ffn_gain, w_gate, w_up, w_down, bias_table = weights
    length = seq_rows.shape[0]
    normed_one = low(rms_norm(seq_rows, attn_gain))

    def project(weight):
        product = jnp.dot(normed_one, weight, precision=highest)
        return low_back(low(product)).reshape(length, HEADS, HEAD_DIM)
    queries = project(w_query)
    key_rows = project(w_key)
    value_rows = project(w_value)
    offset_bias = bias_table[buckets]
    position = jnp.arange(length)
    index_grid = position[:, None] - position[None, :] + (length - 1)
    bias_grid = jnp.transpose(offset_bias[index_grid], (2, 0, 1))
    scores = jnp.einsum('qhd,khd->hqk', queries, key_rows, precision=highest) + bias_grid
    scores = low_back(scores)
    allowed = position[None, :] // BLOCK <= position[:, None] // BLOCK
    scores = jnp.where(allowed[None], scores, masked_score)
    probability = low(jax.nn.softmax(scores, axis=-1))
    mixed_rows = jnp.einsum('hqk,khd->qhd', probability, value_rows, precision=highest)
    attended = low_back(low(mixed_rows.reshape(length, HEADS * HEAD_DIM)))
    branch_one = low_back(jnp.einsum('ti,di->td', attended, w_output, precision=highest))
    middle = seq_rows + branch_one
    normed_two = low(rms_norm(middle, ffn_gain))
    gate_values = low_back(jnp.dot(normed_two, w_gate, precision=highest))
    up_values = low_back(jnp.dot(normed_two, w_up, precision=highest))
    hidden = low(jax.nn.gelu(gate_values, approximate=True) * up_values)
    branch_two = low_back(jnp.einsum('tf,df->td', hidden, w_down, precision=highest))
    return middle + branch_two

def reference(tokens, cotangent, buckets, bias_table, attn_gain, w_query, w_key, w_value, w_output, ffn_gain, w_gate, w_up, w_down):
    weights = tuple((item.astype(jnp.float32) for item in (attn_gain, w_query, w_key, w_value, w_output, ffn_gain, w_gate, w_up, w_down, bias_table)))
    seq_count = tokens.shape[0] // TOK_DEV
    token_seqs = tokens.reshape(seq_count, TOK_DEV, D).astype(jnp.float32)
    cot_seqs = cotangent.reshape(seq_count, TOK_DEV, D).astype(jnp.float32)

    def forward_seq(seq_rows, layer_weights):
        return layer_forward(seq_rows, layer_weights, buckets)

    def step(totals, seq_pair):
        seq_rows, seq_cot = seq_pair
        outputs, pullback = jax.vjp(forward_seq, seq_rows, weights)
        grad_rows, grad_weights = pullback(seq_cot)
        totals = jax.tree.map(lambda first_sum, second_sum: first_sum + second_sum, totals, grad_weights)
        return (totals, (outputs.astype(jnp.bfloat16), grad_rows.astype(jnp.bfloat16)))
    zeros_init = jax.tree.map(jnp.zeros_like, weights)
    totals, (out_seqs, grad_seqs) = lax.scan(step, zeros_init, (token_seqs, cot_seqs))
    return (out_seqs.reshape(seq_count * TOK_DEV, D), grad_seqs.reshape(seq_count * TOK_DEV, D), totals[0], totals[1], totals[2], totals[3], totals[4], totals[5], totals[6], totals[7], totals[8], totals[9])
```

```python
import jax
import jax.numpy as jnp
from jax import lax
from jax.sharding import PartitionSpec as P

BLOCK = 256


norm_eps = 1e-06
masked_score = -1e30
highest = lax.Precision.HIGHEST


def norm_local(row_values, gain_vector):
    return (
        row_values
        * lax.rsqrt(jnp.mean(row_values * row_values, axis=-1, keepdims=True) + norm_eps)
        * gain_vector
    )


def gelu_tanh(values_in):
    return jax.nn.gelu(values_in, approximate=True)


def diagonal_total(matrix):
    head_count, row_count, key_count = matrix.shape
    flipped = matrix[:, :, ::-1]
    padded = jnp.concatenate(
        [flipped, jnp.zeros((head_count, row_count, row_count), jnp.float32)], axis=2
    )
    flat_rows = padded.reshape(head_count, row_count * (key_count + row_count))
    flat_rows = flat_rows[:, : row_count * (key_count + row_count - 1)]
    return jnp.sum(flat_rows.reshape(head_count, row_count, key_count + row_count - 1), axis=1)


def toeplitz_grid(offset_bias, row_count, length):
    head_count = offset_bias.shape[0]
    span = length + row_count - 1
    flipped = offset_bias[:, ::-1]
    rotated = jnp.concatenate([flipped[:, row_count - 1 :], flipped[:, : row_count - 1]], axis=1)
    tiled = jnp.tile(rotated, (1, row_count))[:, : row_count * (span - 1)]
    return tiled.reshape(head_count, row_count, span - 1)[:, :, :length]


def body(
    tokens,
    cotangent,
    buckets,
    bias_table,
    attn_gain,
    w_query,
    w_key,
    w_value,
    w_output,
    ffn_gain,
    w_gate,
    w_up,
    w_down,
):
    length = tokens.shape[0]
    bucket_count = bias_table.shape[0]
    head_count = bias_table.shape[1]
    inner_width = w_query.shape[1]
    ff_width = w_gate.shape[1]
    owner_rows = w_query.shape[0]
    head_size = inner_width // head_count
    block_rows = min(512, length)
    block_count = length // block_rows
    residual = tokens.astype(jnp.float32)
    attn_set = (
        lax.all_gather(attn_gain, "shard", axis=0, tiled=True),
        lax.all_gather(w_query, "shard", axis=0, tiled=True),
        lax.all_gather(w_key, "shard", axis=0, tiled=True),
        lax.all_gather(w_value, "shard", axis=0, tiled=True),
        lax.all_gather(w_output, "shard", axis=0, tiled=True),
    )
    gain_one = attn_set[0].astype(jnp.float32)
    normed_one = norm_local(residual, gain_one).astype(jnp.bfloat16)

    def project(weight):
        product = jnp.dot(normed_one, weight, preferred_element_type=jnp.float32)
        return product.astype(jnp.bfloat16).reshape(length, head_count, head_size)

    queries = project(attn_set[1])
    key_rows = project(attn_set[2])
    value_rows = project(attn_set[3])
    one_hot = (buckets[:, None] == jnp.arange(bucket_count, dtype=jnp.int32)[None, :]).astype(
        jnp.float32
    )
    offset_bias = jnp.dot(one_hot, bias_table.astype(jnp.float32), precision=highest).T
    block_starts = jnp.arange(block_count, dtype=jnp.int32) * block_rows
    key_index = jnp.arange(length, dtype=jnp.int32)

    def block_scores(first_row, query_block):
        query_index = first_row + jnp.arange(block_rows, dtype=jnp.int32)
        bias_grid = toeplitz_grid(offset_bias, block_rows, length)
        scores = (
            jnp.einsum("qhd,khd->hqk", query_block, key_rows, preferred_element_type=jnp.float32)
            + bias_grid
        )
        allowed = key_index[None, :] // BLOCK <= query_index[:, None] // BLOCK
        return jnp.where(allowed[None], scores, masked_score)

    def attend(first_row):
        scores = block_scores(first_row, queries)
        row_max = jnp.max(scores, axis=-1, keepdims=True)
        exp_scores = jnp.exp(scores - row_max)
        totals = jnp.sum(exp_scores, axis=-1, keepdims=True)
        probability = (exp_scores / totals).astype(jnp.bfloat16)
        mixed_rows = jnp.einsum(
            "hqk,khd->qhd", probability, value_rows, preferred_element_type=jnp.float32
        )
        return (mixed_rows, (row_max + jnp.log(totals))[..., 0])

    mixed_blocks, log_totals = lax.map(attend, block_starts)
    attended = mixed_blocks.reshape(length, inner_width).astype(jnp.bfloat16)
    middle = residual + jnp.einsum(
        "ti,di->td", attended, attn_set[4], preferred_element_type=jnp.float32
    )
    ffn_set = (
        lax.all_gather(ffn_gain, "shard", axis=0, tiled=True),
        lax.all_gather(w_gate, "shard", axis=0, tiled=True),
        lax.all_gather(w_up, "shard", axis=0, tiled=True),
        lax.all_gather(w_down, "shard", axis=0, tiled=True),
    )
    gain_two = ffn_set[0].astype(jnp.float32)
    normed_two = norm_local(middle, gain_two).astype(jnp.bfloat16)
    gate_values = jnp.dot(normed_two, ffn_set[1], preferred_element_type=jnp.float32)
    up_values = jnp.dot(normed_two, ffn_set[2], preferred_element_type=jnp.float32)
    activated, gelu_pullback = jax.vjp(gelu_tanh, gate_values)
    hidden = (activated * up_values).astype(jnp.bfloat16)
    layer_out = (
        middle + jnp.einsum("tf,df->td", hidden, ffn_set[3], preferred_element_type=jnp.float32)
    ).astype(jnp.bfloat16)
    ffn_set = (
        lax.all_gather(ffn_gain, "shard", axis=0, tiled=True),
        lax.all_gather(w_gate, "shard", axis=0, tiled=True),
        lax.all_gather(w_up, "shard", axis=0, tiled=True),
        lax.all_gather(w_down, "shard", axis=0, tiled=True),
    )
    grad_w_down = jnp.einsum("td,tf->df", cotangent, hidden, preferred_element_type=jnp.float32)
    grad_hidden = jnp.dot(cotangent, ffn_set[3], preferred_element_type=jnp.float32)
    grad_gate = gelu_pullback(grad_hidden * up_values)[0].astype(jnp.bfloat16)
    grad_up = (grad_hidden * activated).astype(jnp.bfloat16)
    grad_w_gate = jnp.einsum("td,tf->df", normed_two, grad_gate, preferred_element_type=jnp.float32)
    grad_w_up = jnp.einsum("td,tf->df", normed_two, grad_up, preferred_element_type=jnp.float32)
    grad_normed_two = jnp.einsum(
        "tf,df->td", grad_gate, ffn_set[1], preferred_element_type=jnp.float32
    )
    grad_normed_two = grad_normed_two + jnp.einsum(
        "tf,df->td", grad_up, ffn_set[2], preferred_element_type=jnp.float32
    )
    middle_part, grad_gain_two = jax.vjp(norm_local, middle, gain_two)[1](grad_normed_two)
    grad_middle = cotangent.astype(jnp.float32) + middle_part
    ffn_shards = (
        lax.psum_scatter(grad_w_gate.astype(jnp.bfloat16), "shard", scatter_dimension=0, tiled=True),
        lax.psum_scatter(grad_w_up.astype(jnp.bfloat16), "shard", scatter_dimension=0, tiled=True),
        lax.psum_scatter(grad_w_down.astype(jnp.bfloat16), "shard", scatter_dimension=0, tiled=True),
    )
    attn_set = (
        lax.all_gather(attn_gain, "shard", axis=0, tiled=True),
        lax.all_gather(w_query, "shard", axis=0, tiled=True),
        lax.all_gather(w_key, "shard", axis=0, tiled=True),
        lax.all_gather(w_value, "shard", axis=0, tiled=True),
        lax.all_gather(w_output, "shard", axis=0, tiled=True),
    )
    grad_branch = grad_middle.astype(jnp.bfloat16)
    grad_w_output = jnp.einsum(
        "td,ti->di", grad_branch, attended, preferred_element_type=jnp.float32
    )
    grad_attended = jnp.einsum(
        "td,di->ti", grad_branch, attn_set[4], preferred_element_type=jnp.float32
    )
    grad_attended = grad_attended.astype(jnp.bfloat16).reshape(length, head_count, head_size)

    def attend_back(carried, block_input):
        grad_keys, grad_values, grad_offsets = carried
        first_row, log_total = block_input
        scores = block_scores(first_row, queries)
        probability = jnp.exp(scores - log_total[..., None])
        grad_probs = jnp.einsum(
            "qhd,khd->hqk", grad_attended, value_rows, preferred_element_type=jnp.float32
        )
        inner_sum = jnp.sum(probability * grad_probs, axis=-1, keepdims=True)
        grad_scores = (probability * (grad_probs - inner_sum)).astype(jnp.bfloat16)
        grad_values = grad_values + jnp.einsum(
            "hqk,qhd->khd",
            probability.astype(jnp.bfloat16),
            grad_attended,
            preferred_element_type=jnp.float32,
        )
        grad_keys = grad_keys + jnp.einsum(
            "hqk,qhd->khd", grad_scores, queries, preferred_element_type=jnp.float32
        )
        grad_queries = jnp.einsum(
            "hqk,khd->qhd", grad_scores, key_rows, preferred_element_type=jnp.float32
        )
        diagonal_sums = diagonal_total(grad_scores.astype(jnp.float32))
        offset_piece = grad_offsets
        grad_offsets = offset_piece + diagonal_sums
        return ((grad_keys, grad_values, grad_offsets), grad_queries)

    zero_rows = jnp.zeros((length, head_count, head_size), jnp.float32)
    zero_offsets = jnp.zeros((head_count, 2 * length - 1), jnp.float32)
    (grad_keys, grad_values, grad_offsets), query_blocks = lax.scan(
        attend_back, (zero_rows, zero_rows, zero_offsets), (block_starts, log_totals)
    )
    grad_queries = query_blocks.reshape(length, inner_width).astype(jnp.bfloat16)
    grad_keys = grad_keys.reshape(length, inner_width).astype(jnp.bfloat16)
    grad_values = grad_values.reshape(length, inner_width).astype(jnp.bfloat16)
    grad_w_query = jnp.einsum(
        "td,ti->di", normed_one, grad_queries, preferred_element_type=jnp.float32
    )
    grad_w_key = jnp.einsum("td,ti->di", normed_one, grad_keys, preferred_element_type=jnp.float32)
    grad_w_value = jnp.einsum(
        "td,ti->di", normed_one, grad_values, preferred_element_type=jnp.float32
    )
    grad_normed_one = jnp.einsum(
        "ti,di->td", grad_queries, attn_set[1], preferred_element_type=jnp.float32
    )
    grad_normed_one = grad_normed_one + jnp.einsum(
        "ti,di->td", grad_keys, attn_set[2], preferred_element_type=jnp.float32
    )
    grad_normed_one = grad_normed_one + jnp.einsum(
        "ti,di->td", grad_values, attn_set[3], preferred_element_type=jnp.float32
    )
    rows_part, grad_gain_one = jax.vjp(norm_local, residual, gain_one)[1](grad_normed_one)
    grad_tokens = (grad_middle + rows_part).astype(jnp.bfloat16)
    grad_table = jnp.dot(grad_offsets, one_hot, precision=highest).T
    owner_start = lax.axis_index("shard") * owner_rows
    attn_shards = (
        lax.psum_scatter(grad_w_query.astype(jnp.bfloat16), "shard", scatter_dimension=0, tiled=True),
        lax.psum_scatter(grad_w_key.astype(jnp.bfloat16), "shard", scatter_dimension=0, tiled=True),
        lax.psum_scatter(grad_w_value.astype(jnp.bfloat16), "shard", scatter_dimension=0, tiled=True),
        lax.psum_scatter(grad_w_output.astype(jnp.bfloat16), "shard", scatter_dimension=0, tiled=True),
    )
    summed = lax.psum(
        (
            attn_shards[0],
            attn_shards[1],
            attn_shards[2],
            attn_shards[3],
            ffn_shards[0],
            ffn_shards[1],
            ffn_shards[2],
        ),
        "rep",
    )
    small_total = lax.psum((grad_gain_one, grad_gain_two, grad_table), ("shard", "rep"))
    gain_one_own = lax.dynamic_slice_in_dim(small_total[0], owner_start, owner_rows, 0)
    gain_two_own = lax.dynamic_slice_in_dim(small_total[1], owner_start, owner_rows, 0)
    return (
        layer_out,
        grad_tokens,
        gain_one_own,
        summed[0].astype(jnp.float32),
        summed[1].astype(jnp.float32),
        summed[2].astype(jnp.float32),
        summed[3].astype(jnp.float32),
        gain_two_own,
        summed[4].astype(jnp.float32),
        summed[5].astype(jnp.float32),
        summed[6].astype(jnp.float32),
        small_total[2],
    )


def solution(mesh):
    return jax.shard_map(
        body,
        mesh=mesh,
        in_specs=(
            P(("shard", "rep"), None),
            P(("shard", "rep"), None),
            P(),
            P(),
            P("shard"),
            P("shard", None),
            P("shard", None),
            P("shard", None),
            P("shard", None),
            P("shard"),
            P("shard", None),
            P("shard", None),
            P("shard", None),
        ),
        out_specs=(
            P(("shard", "rep"), None),
            P(("shard", "rep"), None),
            P("shard"),
            P("shard", None),
            P("shard", None),
            P("shard", None),
            P("shard", None),
            P("shard"),
            P("shard", None),
            P("shard", None),
            P("shard", None),
            P(),
        ),
        check_vma=False,
    )
```

```python
import functools

import jax
import jax.numpy as jnp
from jax import lax
from jax.experimental import pallas as pl
from jax.experimental.pallas import tpu as pltpu
from jax.sharding import PartitionSpec as P

BLOCK = 256
MESH = pl.DeviceIdType.MESH
f32 = jnp.float32
bf16 = jnp.bfloat16


norm_eps = 1e-06
masked_score = -1e30
highest = lax.Precision.HIGHEST


def norm_local(row_values, gain_vector):
    return (
        row_values
        * lax.rsqrt(jnp.mean(row_values * row_values, axis=-1, keepdims=True) + norm_eps)
        * gain_vector
    )


def gelu_tanh(values_in):
    return jax.nn.gelu(values_in, approximate=True)


def diagonal_total(matrix):
    head_count, row_count, key_count = matrix.shape
    flipped = matrix[:, :, ::-1]
    padded = jnp.concatenate(
        [flipped, jnp.zeros((head_count, row_count, row_count), jnp.float32)], axis=2
    )
    flat_rows = padded.reshape(head_count, row_count * (key_count + row_count))
    flat_rows = flat_rows[:, : row_count * (key_count + row_count - 1)]
    return jnp.sum(flat_rows.reshape(head_count, row_count, key_count + row_count - 1), axis=1)


def toeplitz_grid(offset_bias, row_count, length):
    head_count = offset_bias.shape[0]
    span = length + row_count - 1
    flipped = offset_bias[:, ::-1]
    rotated = jnp.concatenate([flipped[:, row_count - 1 :], flipped[:, : row_count - 1]], axis=1)
    tiled = jnp.tile(rotated, (1, row_count))[:, : row_count * (span - 1)]
    return tiled.reshape(head_count, row_count, span - 1)[:, :, :length]


def body(
    tokens,
    cotangent,
    buckets,
    bias_table,
    attn_gain,
    w_query,
    w_key,
    w_value,
    w_output,
    ffn_gain,
    w_gate,
    w_up,
    w_down,
):
    length = tokens.shape[0]
    bucket_count = bias_table.shape[0]
    head_count = bias_table.shape[1]
    inner_width = w_query.shape[1]
    ff_width = w_gate.shape[1]
    owner_rows = w_query.shape[0]
    head_size = inner_width // head_count
    block_rows = min(512, length)
    block_count = length // block_rows
    residual = tokens.astype(jnp.float32)
    attn_set = (
        lax.all_gather(attn_gain, "shard", axis=0, tiled=True),
        lax.all_gather(w_query, "shard", axis=0, tiled=True),
        lax.all_gather(w_key, "shard", axis=0, tiled=True),
        lax.all_gather(w_value, "shard", axis=0, tiled=True),
        lax.all_gather(w_output, "shard", axis=0, tiled=True),
    )
    gain_one = attn_set[0].astype(jnp.float32)
    normed_one = norm_local(residual, gain_one).astype(jnp.bfloat16)

    def project(weight):
        product = jnp.dot(normed_one, weight, preferred_element_type=jnp.float32)
        return product.astype(jnp.bfloat16).reshape(length, head_count, head_size)

    queries = project(attn_set[1])
    key_rows = project(attn_set[2])
    value_rows = project(attn_set[3])
    one_hot = (buckets[:, None] == jnp.arange(bucket_count, dtype=jnp.int32)[None, :]).astype(
        jnp.float32
    )
    offset_bias = jnp.dot(one_hot, bias_table.astype(jnp.float32), precision=highest).T
    block_starts = jnp.arange(block_count, dtype=jnp.int32) * block_rows
    key_index = jnp.arange(length, dtype=jnp.int32)

    def block_scores(first_row, query_block):
        query_index = first_row + jnp.arange(block_rows, dtype=jnp.int32)
        bias_grid = toeplitz_grid(offset_bias, block_rows, length)
        scores = (
            jnp.einsum("qhd,khd->hqk", query_block, key_rows, preferred_element_type=jnp.float32)
            + bias_grid
        )
        allowed = key_index[None, :] // BLOCK <= query_index[:, None] // BLOCK
        return jnp.where(allowed[None], scores, masked_score)

    def attend(first_row):
        scores = block_scores(first_row, queries)
        row_max = jnp.max(scores, axis=-1, keepdims=True)
        exp_scores = jnp.exp(scores - row_max)
        totals = jnp.sum(exp_scores, axis=-1, keepdims=True)
        probability = (exp_scores / totals).astype(jnp.bfloat16)
        mixed_rows = jnp.einsum(
            "hqk,khd->qhd", probability, value_rows, preferred_element_type=jnp.float32
        )
        return (mixed_rows, (row_max + jnp.log(totals))[..., 0])

    mixed_blocks, log_totals = lax.map(attend, block_starts)
    attended = mixed_blocks.reshape(length, inner_width).astype(jnp.bfloat16)
    middle = residual + jnp.einsum(
        "ti,di->td", attended, attn_set[4], preferred_element_type=jnp.float32
    )
    ffn_set = (
        lax.all_gather(ffn_gain, "shard", axis=0, tiled=True),
        lax.all_gather(w_gate, "shard", axis=0, tiled=True),
        lax.all_gather(w_up, "shard", axis=0, tiled=True),
        lax.all_gather(w_down, "shard", axis=0, tiled=True),
    )
    gain_two = ffn_set[0].astype(jnp.float32)
    normed_two = norm_local(middle, gain_two).astype(jnp.bfloat16)
    gate_values = jnp.dot(normed_two, ffn_set[1], preferred_element_type=jnp.float32)
    up_values = jnp.dot(normed_two, ffn_set[2], preferred_element_type=jnp.float32)
    activated, gelu_pullback = jax.vjp(gelu_tanh, gate_values)
    hidden = (activated * up_values).astype(jnp.bfloat16)
    layer_out = (
        middle + jnp.einsum("tf,df->td", hidden, ffn_set[3], preferred_element_type=jnp.float32)
    ).astype(jnp.bfloat16)
    ffn_set = (
        lax.all_gather(ffn_gain, "shard", axis=0, tiled=True),
        lax.all_gather(w_gate, "shard", axis=0, tiled=True),
        lax.all_gather(w_up, "shard", axis=0, tiled=True),
        lax.all_gather(w_down, "shard", axis=0, tiled=True),
    )
    grad_w_down = jnp.einsum("td,tf->df", cotangent, hidden, preferred_element_type=jnp.float32)
    grad_hidden = jnp.dot(cotangent, ffn_set[3], preferred_element_type=jnp.float32)
    grad_gate = gelu_pullback(grad_hidden * up_values)[0].astype(jnp.bfloat16)
    grad_up = (grad_hidden * activated).astype(jnp.bfloat16)
    grad_w_gate = jnp.einsum("td,tf->df", normed_two, grad_gate, preferred_element_type=jnp.float32)
    grad_w_up = jnp.einsum("td,tf->df", normed_two, grad_up, preferred_element_type=jnp.float32)
    grad_normed_two = jnp.einsum(
        "tf,df->td", grad_gate, ffn_set[1], preferred_element_type=jnp.float32
    )
    grad_normed_two = grad_normed_two + jnp.einsum(
        "tf,df->td", grad_up, ffn_set[2], preferred_element_type=jnp.float32
    )
    middle_part, grad_gain_two = jax.vjp(norm_local, middle, gain_two)[1](grad_normed_two)
    grad_middle = cotangent.astype(jnp.float32) + middle_part
    ffn_shards = (
        lax.psum_scatter(grad_w_gate.astype(jnp.bfloat16), "shard", scatter_dimension=0, tiled=True),
        lax.psum_scatter(grad_w_up.astype(jnp.bfloat16), "shard", scatter_dimension=0, tiled=True),
        lax.psum_scatter(grad_w_down.astype(jnp.bfloat16), "shard", scatter_dimension=0, tiled=True),
    )
    attn_set = (
        lax.all_gather(attn_gain, "shard", axis=0, tiled=True),
        lax.all_gather(w_query, "shard", axis=0, tiled=True),
        lax.all_gather(w_key, "shard", axis=0, tiled=True),
        lax.all_gather(w_value, "shard", axis=0, tiled=True),
        lax.all_gather(w_output, "shard", axis=0, tiled=True),
    )
    grad_branch = grad_middle.astype(jnp.bfloat16)
    grad_w_output = jnp.einsum(
        "td,ti->di", grad_branch, attended, preferred_element_type=jnp.float32
    )
    grad_attended = jnp.einsum(
        "td,di->ti", grad_branch, attn_set[4], preferred_element_type=jnp.float32
    )
    grad_attended = grad_attended.astype(jnp.bfloat16).reshape(length, head_count, head_size)

    def attend_back(carried, block_input):
        grad_keys, grad_values, grad_offsets = carried
        first_row, log_total = block_input
        scores = block_scores(first_row, queries)
        probability = jnp.exp(scores - log_total[..., None])
        grad_probs = jnp.einsum(
            "qhd,khd->hqk", grad_attended, value_rows, preferred_element_type=jnp.float32
        )
        inner_sum = jnp.sum(probability * grad_probs, axis=-1, keepdims=True)
        grad_scores = (probability * (grad_probs - inner_sum)).astype(jnp.bfloat16)
        grad_values = grad_values + jnp.einsum(
            "hqk,qhd->khd",
            probability.astype(jnp.bfloat16),
            grad_attended,
            preferred_element_type=jnp.float32,
        )
        grad_keys = grad_keys + jnp.einsum(
            "hqk,qhd->khd", grad_scores, queries, preferred_element_type=jnp.float32
        )
        grad_queries = jnp.einsum(
            "hqk,khd->qhd", grad_scores, key_rows, preferred_element_type=jnp.float32
        )
        diagonal_sums = diagonal_total(grad_scores.astype(jnp.float32))
        offset_piece = grad_offsets
        grad_offsets = offset_piece + diagonal_sums
        return ((grad_keys, grad_values, grad_offsets), grad_queries)

    zero_rows = jnp.zeros((length, head_count, head_size), jnp.float32)
    zero_offsets = jnp.zeros((head_count, 2 * length - 1), jnp.float32)
    (grad_keys, grad_values, grad_offsets), query_blocks = lax.scan(
        attend_back, (zero_rows, zero_rows, zero_offsets), (block_starts, log_totals)
    )
    grad_queries = query_blocks.reshape(length, inner_width).astype(jnp.bfloat16)
    grad_keys = grad_keys.reshape(length, inner_width).astype(jnp.bfloat16)
    grad_values = grad_values.reshape(length, inner_width).astype(jnp.bfloat16)
    grad_w_query = jnp.einsum(
        "td,ti->di", normed_one, grad_queries, preferred_element_type=jnp.float32
    )
    grad_w_key = jnp.einsum("td,ti->di", normed_one, grad_keys, preferred_element_type=jnp.float32)
    grad_w_value = jnp.einsum(
        "td,ti->di", normed_one, grad_values, preferred_element_type=jnp.float32
    )
    grad_normed_one = jnp.einsum(
        "ti,di->td", grad_queries, attn_set[1], preferred_element_type=jnp.float32
    )
    grad_normed_one = grad_normed_one + jnp.einsum(
        "ti,di->td", grad_keys, attn_set[2], preferred_element_type=jnp.float32
    )
    grad_normed_one = grad_normed_one + jnp.einsum(
        "ti,di->td", grad_values, attn_set[3], preferred_element_type=jnp.float32
    )
    rows_part, grad_gain_one = jax.vjp(norm_local, residual, gain_one)[1](grad_normed_one)
    grad_tokens = (grad_middle + rows_part).astype(jnp.bfloat16)
    grad_table = jnp.dot(grad_offsets, one_hot, precision=highest).T
    owner_start = lax.axis_index("shard") * owner_rows
    attn_shards = (
        lax.psum_scatter(grad_w_query.astype(jnp.bfloat16), "shard", scatter_dimension=0, tiled=True),
        lax.psum_scatter(grad_w_key.astype(jnp.bfloat16), "shard", scatter_dimension=0, tiled=True),
        lax.psum_scatter(grad_w_value.astype(jnp.bfloat16), "shard", scatter_dimension=0, tiled=True),
        lax.psum_scatter(grad_w_output.astype(jnp.bfloat16), "shard", scatter_dimension=0, tiled=True),
    )
    summed = lax.psum(
        (
            attn_shards[0],
            attn_shards[1],
            attn_shards[2],
            attn_shards[3],
            ffn_shards[0],
            ffn_shards[1],
            ffn_shards[2],
        ),
        "rep",
    )
    small_total = lax.psum((grad_gain_one, grad_gain_two, grad_table), ("shard", "rep"))
    gain_one_own = lax.dynamic_slice_in_dim(small_total[0], owner_start, owner_rows, 0)
    gain_two_own = lax.dynamic_slice_in_dim(small_total[1], owner_start, owner_rows, 0)
    return (
        layer_out,
        grad_tokens,
        gain_one_own,
        summed[0].astype(jnp.float32),
        summed[1].astype(jnp.float32),
        summed[2].astype(jnp.float32),
        summed[3].astype(jnp.float32),
        gain_two_own,
        summed[4].astype(jnp.float32),
        summed[5].astype(jnp.float32),
        summed[6].astype(jnp.float32),
        small_total[2],
    )


def dot_nn(a, b):
    return lax.dot_general(a, b, (((1,), (0,)), ((), ())), preferred_element_type=f32)


def dot_nt(a, b):
    return lax.dot_general(a, b, (((1,), (1,)), ((), ())), preferred_element_type=f32)


def dot_tn(a, b):
    return lax.dot_general(a, b, (((0,), (0,)), ((), ())), preferred_element_type=f32)


def fused_kernel(
    xt_ref,
    ct_ref,
    buckets_ref,
    table_ref,
    gains_ref,
    wa_ref,
    wf_ref,
    out_ref,
    gtok_ref,
    small_ref,
    ga_ref,
    gf_ref,
    land_ref,
    gland,
    gcol,
    n1t,
    n2t,
    mid,
    acc_o,
    acc_n,
    qt,
    kt,
    vt,
    att,
    dat,
    dqt,
    dkt,
    dvt,
    wq,
    wk,
    wv,
    wo,
    wg2,
    wu2,
    wd2,
    wload,
    g,
    hid,
    dgt,
    dup,
    rc,
    rxy,
    r2,
    vbuf,
    zi,
    zm,
    ubuf,
    revb,
    onehot,
    doff,
    sms,
    smr,
    gain_s,
    gain_r,
    gsend,
    gloc,
    g1r,
    g2r,
    gpr,
    load_sem,
    e0s,
    e0r,
    e1s,
    e1r,
    e2s,
    e2r,
    zis,
    zir,
    zms,
    zmr,
    us,
    ul,
    ur,
    sss,
    ssr,
    zcredit,
    *,
    chunks,
    heads,
):
    width = xt_ref.shape[0]
    toks = xt_ref.shape[1]
    rows = gains_ref.shape[0]
    fw = wf_ref.shape[3]
    sub = fw // 3
    aw = wa_ref.shape[3]
    hs = aw // heads
    total = chunks + 2
    eps = 1e-06
    lanes = revb.shape[1]
    big = 2 * rows
    nbig = width // big

    s = lax.axis_index("shard")
    r = lax.axis_index("rep")
    c = s % 2
    x = (s // 2) % 2
    y = s // 4
    sc = s + 1 - 2 * c
    sx = s + 2 - 4 * x
    sy = s + 4 - 8 * y
    bx = sx - c
    by = sy - c
    bd = (1 - y) * 4 + (1 - x) * 2
    b_own = s - c
    mate = r + 1 - 2 * (r % 2)
    inner = (r == 1) | (r == 2)
    outer = (r == 0) | (r == 3)

    def remote(src, dst, ssem, rsem, dev):
        return pltpu.make_async_remote_copy(
            src_ref=src, dst_ref=dst, send_sem=ssem, recv_sem=rsem, device_id=dev, device_id_type=MESH
        )

    def settle(ref, sem):
        pltpu.make_async_copy(ref, ref, sem).wait()

    barrier = pltpu.get_barrier_semaphore()
    near = [(sc, r), (bx, r), (bx + 1, r), (by, r), (by + 1, r), (bd, r), (bd + 1, r), (s, mate), (sc, mate)]
    for dev in near:
        pl.semaphore_signal(barrier, inc=1, device_id=dev, device_id_type=MESH)

    @pl.when(inner)
    def _():
        pl.semaphore_signal(barrier, inc=1, device_id=(s, 3 - r), device_id_type=MESH)

    @pl.when(inner)
    def _():
        pl.semaphore_wait(barrier, len(near) + 1)

    @pl.when(outer)
    def _():
        pl.semaphore_wait(barrier, len(near))

    def place(chunk, index):
        kind, k = chunk
        if kind == "a":
            return g.at[16 + index, :, pl.ds(k * aw, aw)]
        return land_ref.at[k, index]

    def places(chunk, count):
        kind, k = chunk
        if kind == "a":
            return g.at[pl.ds(16, count), :, pl.ds(k * aw, aw)]
        return land_ref.at[k, pl.ds(0, count)]

    def own_block(chunk, half):
        kind, k = chunk
        return wa_ref.at[k, half] if kind == "a" else wf_ref.at[half, k]

    def at(chunk):
        kind, k = chunk
        return k if kind == "a" else k + 2

    def gather_send(chunk):
        i = at(chunk)
        for half in (0, 1):
            src = own_block(chunk, half)
            dst = place(chunk, half * 8 + s)
            remote(src, dst, gsend.at[i], g1r.at[i], (bx + half, r)).start()
            remote(src, dst, gsend.at[i], g1r.at[i], (by + half, r)).start()
        for half in (0, 1):
            src = own_block(chunk, half)
            dst = place(chunk, half * 8 + s)
            remote(src, dst, gsend.at[i], gpr.at[i], (sc, r)).start()
            pltpu.make_async_copy(src, dst, gloc.at[i]).start()

    def gather_forward(chunk):
        i = at(chunk)
        settle(places(chunk, 4), g1r.at[i])
        one = place(chunk, c * 8 + bx)
        two = place(chunk, c * 8 + by + 1)
        remote(one, one, gsend.at[i], g2r.at[i], (sy, r)).start()
        remote(two, two, gsend.at[i], g2r.at[i], (sx, r)).start()
        for b in (bx, bx + 1, by, by + 1):
            spot = place(chunk, c * 8 + b)
            remote(spot, spot, gsend.at[i], gpr.at[i], (sc, r)).start()

    def gather_swap(chunk):
        i = at(chunk)
        settle(places(chunk, 2), g2r.at[i])
        for b in (bd, bd + 1):
            spot = place(chunk, c * 8 + b)
            remote(spot, spot, gsend.at[i], gpr.at[i], (sc, r)).start()

    def gather_done(chunk):
        i = at(chunk)
        settle(places(chunk, 8), gpr.at[i])
        settle(places(chunk, 2), gloc.at[i])

    def gather_sent(chunk):
        settle(places(chunk, 14), gsend.at[at(chunk)])

    def cut(ref, w):
        return ref if w == fw else ref.at[:, :, pl.ds(0, w)]

    def cut1(ref, index, w):
        return ref.at[index] if w == fw else ref.at[index, :, pl.ds(0, w)]

    def span(ref, start, count, w):
        return ref.at[pl.ds(start, count)] if w == fw else ref.at[pl.ds(start, count), :, pl.ds(0, w)]

    def get(ref, index, w):
        return ref[index] if w == fw else ref[index, :, 0:w]

    def put(ref, index, w, value):
        if w == fw:
            ref[index] = value
        else:
            ref[index, :, 0:w] = value

    def add_to(dst, i, src, j, w):
        value = get(dst, i, w).astype(f32) + get(src, j, w).astype(f32)
        put(dst, i, w, value.astype(bf16))

    def core_send(n, w):
        slot = n % 2
        remote(
            span(g, slot * 16 + (1 - c) * 8, 8, w), span(rc, slot * 8, 8, w), e0s.at[n], e0r.at[n], (sc, r)
        ).start()

    def plane_send(n, w):
        slot = n % 2
        base = slot * 16 + c * 8
        settle(span(rc, slot * 8, 8, w), e0r.at[n])

        @pl.loop(0, 8)
        def _(b):
            add_to(g, base + b, rc, slot * 8 + b, w)

        for k in (0, 1):
            remote(
                cut1(g, base + 4 * k + 2 * (1 - x), w), cut1(rxy, slot * 4 + k, w), e1s.at[n], e1r.at[n], (sx, r)
            ).start()
            remote(
                cut1(g, base + 4 * (1 - y) + 2 * k + 1, w),
                cut1(rxy, slot * 4 + 2 + k, w),
                e1s.at[n],
                e1r.at[n],
                (sy, r),
            ).start()

    def plane_turn(n, w):
        slot = n % 2
        base = slot * 16 + c * 8
        settle(span(rxy, slot * 4, 4, w), e1r.at[n])
        first = base + 4 * (1 - y) + 2 * x
        second = base + 4 * y + 2 * (1 - x) + 1
        mine = base + b_own
        add_to(g, first, rxy, slot * 4 + 1 - y, w)
        add_to(g, second, rxy, slot * 4 + 2 + 1 - x, w)
        add_to(g, mine, rxy, slot * 4 + y, w)
        add_to(g, mine + 1, rxy, slot * 4 + 2 + x, w)
        remote(cut1(g, first, w), cut1(r2, slot * 2, w), e2s.at[n], e2r.at[n], (sy, r)).start()
        remote(cut1(g, second, w), cut1(r2, slot * 2 + 1, w), e2s.at[n], e2r.at[n], (sx, r)).start()

    def rep_send(n, w):
        slot = n % 2
        base = slot * 16 + c * 8
        settle(span(r2, slot * 2, 2, w), e2r.at[n])
        if isinstance(n, int):
            if n >= 2:
                pl.when(outer)(functools.partial(rep_free, n))
        else:
            pl.when(outer & (n >= 2))(functools.partial(rep_free, n))
        for j in (0, 1):
            value = get(g, base + b_own + j, w).astype(f32) + get(r2, slot * 2 + j, w).astype(f32)
            put(vbuf, slot * 2 + j, w, value.astype(bf16))

        @pl.when(outer)
        def _():
            remote(
                span(vbuf, slot * 2, 2, w), span(zi, slot * 2, 2, w), zis.at[n], zir.at[n], (s, mate)
            ).start()

        settle(span(g, slot * 16, 8, w), e0s.at[n])
        settle(span(rxy, slot * 4, 4, w), e1s.at[n])
        settle(span(r2, slot * 2, 2, w), e2s.at[n])

    def width_of(n):
        return fw if not isinstance(n, int) or n < chunks else aw

    def rep_free(n):
        earlier = n - 2
        slot = n % 2
        settle(span(vbuf, slot * 2, 2, width_of(earlier)), zis.at[earlier])
        pl.semaphore_wait(zcredit, 1)

    def rep_turn(n, w):
        slot = n % 2

        @pl.when(inner)
        def _():
            settle(span(zi, slot * 2, 2, w), zir.at[n])
            for j in (0, 1):
                add_to(vbuf, slot * 2 + j, zi, slot * 2 + j, w)

            def credit():
                pl.semaphore_signal(zcredit, inc=1, device_id=(s, mate), device_id_type=MESH)

            if isinstance(n, int):
                if n + 2 < total:
                    credit()
            else:
                credit()
            remote(
                span(vbuf, slot * 2, 2, w), span(zm, slot * 2, 2, w), zms.at[n], zmr.at[n], (s, 3 - r)
            ).start()

    def result(n, half):
        if isinstance(n, int) and n >= chunks:
            return ga_ref.at[total - 1 - n, half]
        return gf_ref.at[n, half]

    def u_free(n, w):
        slot = n % 2
        for k in (0, 1, 2):
            settle(cut1(ubuf, slot * 2, w), us.at[n, k])
        settle(cut1(ubuf, slot * 2, w), ul.at[n])

    def rep_last(n, w):
        slot = n % 2

        @pl.when(inner)
        def _():
            settle(span(zm, slot * 2, 2, w), zmr.at[n])
            if isinstance(n, int):
                if n >= 2:
                    u_free(n - 2, width_of(n - 2))
            else:
                pl.when(n >= 2)(lambda: u_free(n - 2, w))
            for j in (0, 1):
                value = get(vbuf, slot * 2 + j, w).astype(f32) + get(zm, slot * 2 + j, w).astype(f32)
                put(ubuf, slot * 2 + j, w, value.astype(bf16))
            keep = cut1(ubuf, slot * 2 + c, w)
            give = cut1(ubuf, slot * 2 + 1 - c, w)
            target = result(n, c)
            pltpu.make_async_copy(keep, target, ul.at[n]).start()
            remote(keep, target, us.at[n, 0], ur.at[n, c], (s, mate)).start()
            remote(give, target, us.at[n, 1], ur.at[n, c], (sc, mate)).start()
            remote(give, target, us.at[n, 2], ur.at[n, c], (sc, r)).start()
            settle(span(vbuf, slot * 2, 2, w), zms.at[n])

    def small_send(step):
        if step < 3:
            dev = ((sc, r), (sx, r), (sy, r))[step]
            remote(sms.at[step], smr.at[step], sss.at[step], ssr.at[step], dev).start()
        elif step == 3:

            @pl.when(outer)
            def _():
                remote(sms.at[3], smr.at[3], sss.at[3], ssr.at[3], (s, mate)).start()
        elif step == 4:

            @pl.when(inner)
            def _():
                remote(sms.at[4], smr.at[4], sss.at[4], ssr.at[4], (s, 3 - r)).start()
        else:

            @pl.when(inner)
            def _():
                remote(sms.at[5], smr.at[5], sss.at[5], ssr.at[5], (s, mate)).start()

    def small_step(step):
        def take():
            settle(smr.at[step], ssr.at[step])
            settle(sms.at[step], sss.at[step])
            if step < 2:
                sms[step + 1] = sms[step] + smr[step]
            elif step == 2:
                sms[3] = sms[2] + smr[2]

        if step < 3:
            take()
            small_send(step + 1)
        elif step == 3:

            @pl.when(inner)
            def _():
                settle(smr.at[3], ssr.at[3])
                sms[4] = sms[3] + smr[3]

            @pl.when(outer)
            def _():
                settle(sms.at[3], sss.at[3])

            small_send(4)
        elif step == 4:

            @pl.when(inner)
            def _():
                settle(smr.at[4], ssr.at[4])
                settle(sms.at[4], sss.at[4])
                sms[5] = sms[4] + smr[4]
                small_ref[...] = sms[5]

            small_send(5)
        else:

            @pl.when(inner)
            def _():
                settle(sms.at[5], sss.at[5])

            @pl.when(outer)
            def _():
                settle(smr.at[5], ssr.at[5])
                small_ref[...] = smr[5]

    tile = 64
    tiles = width // tile

    def over_rows(body, start):
        def step(i, carry):
            return body(pl.ds(pl.multiple_of(i * tile, tile), tile), carry)

        return lax.fori_loop(0, tiles, step, start)

    def fold(value):
        return jnp.sum(value.reshape(tile // 8, 8, toks), axis=0)

    zero8 = jnp.zeros((8, toks), f32)

    gather_send(("a", 0))
    gdst = gland.at[s]
    for k, dev in enumerate([(sc, r), (bx, r), (bx + 1, r), (by, r), (by + 1, r), (bd, r), (bd + 1, r)]):
        remote(gains_ref, gdst, gain_s, gain_r, dev).start()
    pltpu.make_async_copy(gains_ref, gdst, load_sem.at[1]).start()
    gather_send(("a", 1))
    gather_send(("f", 0))

    def square_sum(sl, acc):
        v = xt_ref[sl, :].astype(f32)
        return acc + fold(v * v)

    ssum = jnp.sum(over_rows(square_sum, zero8), axis=0, keepdims=True)
    r1 = lax.rsqrt(ssum * (1.0 / width) + eps)

    bucket_index = lax.broadcasted_iota(jnp.int32, (table_ref.shape[1], lanes), 0)
    rev_hot = (bucket_index == buckets_ref[0:1, :]).astype(bf16)
    onehot[...] = (bucket_index == buckets_ref[1:2, :]).astype(bf16)
    revb[...] = dot_nn(table_ref[...], rev_hot)

    settle(gland.at[pl.ds(0, 7)], gain_r)
    settle(gland.at[0], load_sem.at[1])
    for b in range(8):
        gcol[rows * b : rows * (b + 1), :] = gland[b].astype(f32)

    def norm_one(sl, carry):
        v = xt_ref[sl, :].astype(f32)
        n1t[sl, :] = (v * r1 * gcol[sl, 0:1]).astype(bf16)
        return carry

    gather_forward(("a", 0))
    over_rows(norm_one, 0)
    gather_swap(("a", 0))
    gather_forward(("a", 1))
    gather_send(("f", 1))

    def compact(dst, half, col):
        @pl.loop(0, nbig)
        def _(i):
            both = jnp.concatenate(
                [
                    g[16 + half * 8 + 2 * i, :, col : col + aw].astype(f32),
                    g[16 + half * 8 + 2 * i + 1, :, col : col + aw].astype(f32),
                ],
                axis=0,
            )
            dst[pl.ds(pl.multiple_of(i * 2 * rows, 16), 2 * rows), :] = both.astype(bf16)

    gather_done(("a", 0))
    compact(wq, 0, 0)
    qt[...] = dot_tn(wq[...], n1t[...]).astype(bf16)
    compact(wk, 1, 0)
    kt[...] = dot_tn(wk[...], n1t[...]).astype(bf16)
    gather_swap(("a", 1))
    gather_done(("a", 1))
    compact(wv, 0, aw)
    vt[...] = dot_tn(wv[...], n1t[...]).astype(bf16)
    compact(wo, 1, aw)
    gather_forward(("f", 0))
    gather_send(("f", 2))

    half_tok = toks // 2

    def softmax_block(h, head, block):
        keys = half_tok * (block + 1)
        low = half_tok * block
        row = jnp.broadcast_to(revb[pl.ds(h, 1), :], (half_tok, lanes))
        bias = pltpu.roll(row, (low + 1 - toks) % lanes, 1, stride=1, stride_axis=0)[:, :keys]
        scores = dot_tn(qt[head, low : low + half_tok], kt[head, 0:keys]) + bias
        e = jnp.exp(scores - jnp.max(scores, axis=1, keepdims=True))
        return e * (1.0 / jnp.sum(e, axis=1, keepdims=True)), low, keys

    def attend(h, carry):
        head = pl.ds(pl.multiple_of(h * hs, hs), hs)
        for block in (0, 1):
            p, low, keys = softmax_block(h, head, block)
            att[head, low : low + half_tok] = dot_nt(vt[head, 0:keys], p.astype(bf16)).astype(bf16)
        return carry

    lax.fori_loop(0, heads // 2, attend, 0)
    gather_swap(("f", 0))
    gather_forward(("f", 1))
    lax.fori_loop(heads // 2, heads, attend, 0)

    def branch_one(i, acc):
        sl = pl.ds(pl.multiple_of(i * big, 16), big)
        m = xt_ref[sl, :].astype(f32) + dot_nn(wo[sl, :], att[...])
        mid[sl, :] = m
        return acc + jnp.sum((m * m).reshape(big // 8, 8, toks), axis=0)

    ssum = jnp.sum(lax.fori_loop(0, nbig, branch_one, zero8), axis=0, keepdims=True)
    r2n = lax.rsqrt(ssum * (1.0 / width) + eps)

    def norm_two(sl, carry):
        m = mid[sl, :]
        n2t[sl, :] = (m * r2n * gcol[sl, 1:2]).astype(bf16)
        acc_o[sl, :] = m
        acc_n[sl, :] = jnp.zeros((tile, toks), f32)
        return carry

    over_rows(norm_two, 0)

    tok_tile = toks // 2

    def ffn_chunk(t):
        slot = t % 2
        parts = [(half, k) for half in (0, 1) for k in (0, 1, 2)]

        def load(p):
            half, k = parts[p]
            return pltpu.make_async_copy(
                land_ref.at[t, pl.ds(half * 8, 8), :, pl.ds(k * sub, sub)],
                wload.at[pl.ds((p % 2) * 8, 8)],
                load_sem.at[p % 2],
            )

        load(0).start()
        for p, (half, k) in enumerate(parts):
            if p + 1 < len(parts):
                load(p + 1).start()
            load(p).wait()
            dst = (wg2, wu2, wd2)[k]

            @pl.loop(0, nbig)
            def _(i):
                base = (p % 2) * 8 + 2 * i
                both = jnp.concatenate([wload[base].astype(f32), wload[base + 1].astype(f32)], axis=0)
                sl = pl.ds(pl.multiple_of(i * big, 16), big)
                dst[sl, half * sub : (half + 1) * sub] = both.astype(bf16)

        @pl.loop(0, toks // tok_tile)
        def _(m):
            sl = pl.ds(pl.multiple_of(m * tok_tile, tok_tile), tok_tile)
            gate = dot_tn(n2t[:, sl], wg2[...])
            up = dot_tn(n2t[:, sl], wu2[...])
            gh = dot_tn(ct_ref[:, sl], wd2[...])
            k0 = 0.7978845608028654
            k1 = 0.044715
            sq = gate * gate
            th = jnp.tanh(k0 * (gate + k1 * (sq * gate)))
            half_one = 0.5 * (1.0 + th)
            act = gate * half_one
            slope = half_one + 0.5 * gate * (1.0 - th * th) * (k0 * (1.0 + 3.0 * k1 * sq))
            hid[sl, :] = (act * up).astype(bf16)
            dgt[sl, :] = (gh * up * slope).astype(bf16)
            dup[sl, :] = (gh * act).astype(bf16)

        @pl.loop(0, nbig)
        def _(i):
            sl = pl.ds(pl.multiple_of(i * big, 16), big)
            acc_o[sl, :] += dot_nt(wd2[sl, :], hid[...])
            acc_n[sl, :] += dot_nt(wg2[sl, :], dgt[...]) + dot_nt(wu2[sl, :], dup[...])
            for k, value in enumerate(
                (dot_nn(n2t[sl, :], dgt[...]), dot_nn(n2t[sl, :], dup[...]), dot_nn(ct_ref[sl, :], hid[...]))
            ):
                for half in (0, 1):
                    for j in (0, 1):
                        g[slot * 16 + half * 8 + 2 * i + j, :, k * sub : (k + 1) * sub] = value[
                            rows * j : rows * (j + 1), half * sub : (half + 1) * sub
                        ].astype(bf16)

    def ffn_step(t, carry):
        pl.when(t + 1 < chunks)(lambda: gather_swap(("f", t + 1)))
        pl.when(t + 2 < chunks)(lambda: gather_forward(("f", t + 2)))
        pl.when(t + 3 < chunks)(lambda: gather_send(("f", t + 3)))
        pl.when(t >= 3)(lambda: rep_turn(t - 3, fw))
        pl.when(t >= 2)(lambda: rep_send(t - 2, fw))
        gather_done(("f", t))
        ffn_chunk(t)
        core_send(t, fw)
        pl.when(t >= 3)(lambda: rep_last(t - 3, fw))
        pl.when(t >= 1)(lambda: plane_turn(t - 1, fw))
        plane_send(t, fw)
        return carry

    gather_sent(("a", 0))
    gather_sent(("a", 1))
    lax.fori_loop(0, chunks, ffn_step, 0)

    nv = chunks
    nq = chunks + 1
    rep_turn(nv - 3, fw)
    rep_send(nv - 2, fw)
    pick = lax.broadcasted_iota(jnp.int32, (8, toks), 0)

    def token_sums(row):
        chosen = (pick == row).astype(bf16)
        return dot_nt(chosen, wg2[...]) + dot_nt(chosen, wu2[...])

    def second_mean(sl, acc):
        return acc + fold(gcol[sl, 1:2] * acc_n[sl, :] * mid[sl, :])

    back = jnp.sum(over_rows(second_mean, zero8), axis=0, keepdims=True) * (1.0 / width)
    back = back * (r2n * r2n * r2n)

    def second_norm(sl, carry):
        m = mid[sl, :]
        gn = acc_n[sl, :]
        out_ref[sl, :] = acc_o[sl, :].astype(bf16)
        v = gn * m * r2n
        hi = v.astype(bf16)
        wg2[sl, :] = hi
        wu2[sl, :] = (v - hi.astype(f32)).astype(bf16)
        gm = ct_ref[sl, :].astype(f32) + r2n * gcol[sl, 1:2] * gn - m * back
        acc_n[sl, :] = gm
        n2t[sl, :] = gm.astype(bf16)
        return carry

    over_rows(second_norm, 0)
    sms[0] = jnp.zeros(sms.shape[1:], f32)
    sms[0, :, 0:width] = token_sums(1)
    rep_last(nv - 3, fw)
    plane_turn(nv - 1, fw)

    dat[...] = dot_tn(wo[...], n2t[...]).astype(bf16)

    def weight_grad(n, half, left, right):
        @pl.loop(0, nbig)
        def _(i):
            sl = pl.ds(pl.multiple_of(i * big, 16), big)
            value = dot_nt(left[sl, :], right[...])
            for j in (0, 1):
                g[(n % 2) * 16 + half * 8 + 2 * i + j, :, 0:aw] = value[rows * j : rows * (j + 1), :].astype(bf16)

    weight_grad(nv, 1, n2t, att)
    flip = (
        lax.broadcasted_iota(jnp.int32, (toks, toks), 0) + lax.broadcasted_iota(jnp.int32, (toks, toks), 1)
        == toks - 1
    )
    hid[...] = flip.astype(bf16)
    doff[...] = jnp.zeros(doff.shape, f32)

    def attend_back(h, carry):
        head = pl.ds(pl.multiple_of(h * hs, hs), hs)
        grad_v = []
        grad_k = []
        offsets = jnp.zeros((1, lanes), f32)
        for block in (0, 1):
            p, low, keys = softmax_block(h, head, block)
            q_rows = qt[head, low : low + half_tok]
            a_rows = dat[head, low : low + half_tok]
            grad_p = dot_tn(a_rows, vt[head, 0:keys])
            ds = (p * (grad_p - jnp.sum(p * grad_p, axis=1, keepdims=True))).astype(bf16)
            grad_v.append(dot_nn(a_rows, p.astype(bf16)))
            grad_k.append(dot_nn(q_rows, ds))
            dqt[head, low : low + half_tok] = dot_nt(kt[head, 0:keys], ds).astype(bf16)
            turned = dot_nn(ds, hid[0:keys, toks - keys : toks])
            padded = jnp.concatenate([turned, jnp.zeros((half_tok, lanes - keys), f32)], axis=1)
            lined = pltpu.roll(padded, half_tok, 1, stride=1, stride_axis=0)
            offsets = offsets + jnp.sum(lined, axis=0, keepdims=True)
        for dst, parts in ((dvt, grad_v), (dkt, grad_k)):
            dst[head, 0:half_tok] = (parts[0] + parts[1][:, 0:half_tok]).astype(bf16)
            dst[head, half_tok:toks] = parts[1][:, half_tok:toks].astype(bf16)
        doff[pl.ds(h, 1), :] = offsets
        return carry

    lax.fori_loop(0, heads // 2, attend_back, 0)
    rep_turn(nv - 2, fw)
    rep_send(nv - 1, fw)
    lax.fori_loop(heads // 2, heads, attend_back, 0)
    rep_last(nv - 2, fw)
    rep_turn(nv - 1, fw)
    weight_grad(nv, 0, n1t, dvt)
    core_send(nv, aw)
    weight_grad(nq, 0, n1t, dqt)
    weight_grad(nq, 1, n1t, dkt)
    plane_send(nv, aw)
    core_send(nq, aw)
    rep_last(nv - 1, fw)
    plane_send(nq, aw)

    def first_back(i, acc):
        sl = pl.ds(pl.multiple_of(i * big, 16), big)
        gn = dot_nn(wq[sl, :], dqt[...]) + dot_nn(wk[sl, :], dkt[...]) + dot_nn(wv[sl, :], dvt[...])
        acc_o[sl, :] = gn
        v = gcol[sl, 0:1] * gn * xt_ref[sl, :].astype(f32)
        return acc + jnp.sum(v.reshape(big // 8, 8, toks), axis=0)

    back = jnp.sum(lax.fori_loop(0, nbig, first_back, zero8), axis=0, keepdims=True) * (1.0 / width)
    back = back * (r1 * r1 * r1)
    plane_turn(nv, aw)

    def first_norm(sl, carry):
        v = xt_ref[sl, :].astype(f32)
        gn = acc_o[sl, :]
        prod = gn * v * r1
        hi = prod.astype(bf16)
        wg2[sl, :] = hi
        wu2[sl, :] = (prod - hi.astype(f32)).astype(bf16)
        gtok_ref[sl, :] = (acc_n[sl, :] + r1 * gcol[sl, 0:1] * gn - v * back).astype(bf16)
        return carry

    over_rows(first_norm, 0)
    sms[0, :, 0:width] += token_sums(0)
    rest = doff[...]
    table = jnp.zeros((8, onehot.shape[0]), f32)
    for _ in range(3):
        part = rest.astype(bf16)
        table = table + dot_nt(part, onehot[...])
        rest = rest - part.astype(f32)
    sms[0, :, sms.shape[2] - onehot.shape[0] : sms.shape[2]] = table
    small_send(0)
    plane_turn(nq, aw)
    small_step(0)
    rep_send(nv, aw)
    small_step(1)
    rep_send(nq, aw)
    small_step(2)
    rep_turn(nv, aw)
    small_step(3)
    rep_last(nv, aw)
    rep_turn(nq, aw)
    small_step(4)
    rep_last(nq, aw)
    small_step(5)

    settle(gland.at[pl.ds(0, 7)], gain_s)
    lax.fori_loop(0, chunks, lambda k, carry: (gather_sent(("f", k)), carry)[1], 0)

    @pl.when(outer)
    def _():
        for n in (nv, nq):
            settle(span(vbuf, (n % 2) * 2, 2, aw), zis.at[n])
        for n in range(total):
            for half in (0, 1):
                settle(result(n, half), ur.at[n, half])

    @pl.when(inner)
    def _():
        for n in (nv, nq):
            u_free(n, aw)
        for n in range(total):
            settle(result(n, 0), ur.at[n, 1 - c])


def fused(tokens, cotangent, buckets, bias_table, gains, wa, wf):
    toks, width = tokens.shape
    heads = bias_table.shape[1]
    chunks, rows, fw = wf.shape[1:]
    aw = wa.shape[3]
    sub = fw // 3
    total = chunks + 2
    lanes = 2 * toks
    small_lanes = (width + 127) // 128 * 128 + 128
    padded = jnp.concatenate([buckets, jnp.full((1,), -1, jnp.int32)])
    turned = jnp.concatenate([buckets[::-1], jnp.full((1,), -1, jnp.int32)])
    bucket_rows = jnp.concatenate([turned[None], padded[None], jnp.full((6, lanes), -1, jnp.int32)])
    table = jnp.pad(bias_table.T, ((0, 8 - heads), (0, 128 - bias_table.shape[0])))
    vm = pl.BlockSpec(memory_space=pltpu.VMEM)
    hbm = pl.BlockSpec(memory_space=pltpu.HBM)
    dma = pltpu.SemaphoreType.DMA
    tok = lambda kind: pltpu.VMEM((width, toks), kind)
    inner_rows = pltpu.VMEM((aw, toks), bf16)
    blocks = lambda count: pltpu.VMEM((count, rows, fw), bf16)
    return pl.pallas_call(
        functools.partial(fused_kernel, chunks=chunks, heads=heads),
        out_shape=(
            jax.ShapeDtypeStruct((width, toks), bf16),
            jax.ShapeDtypeStruct((width, toks), bf16),
            jax.ShapeDtypeStruct((8, small_lanes), f32),
            jax.ShapeDtypeStruct((2, 2, rows, aw), bf16),
            jax.ShapeDtypeStruct((chunks, 2, rows, fw), bf16),
            jax.ShapeDtypeStruct((chunks, 16, rows, fw), bf16),
        ),
        in_specs=[vm, vm, vm, vm, vm, hbm, hbm],
        out_specs=(vm, vm, vm, hbm, hbm, hbm),
        scratch_shapes=[
            pltpu.VMEM((8, rows, 128), bf16),
            pltpu.VMEM((width, 128), f32),
            tok(bf16),
            tok(bf16),
            tok(f32),
            tok(f32),
            tok(f32),
            *([inner_rows] * 8),
            *([pltpu.VMEM((width, aw), bf16)] * 4),
            *([pltpu.VMEM((width, 2 * sub), bf16)] * 3),
            pltpu.VMEM((16, rows, sub), bf16),
            blocks(32),
            *([pltpu.VMEM((toks, 2 * sub), bf16)] * 3),
            blocks(16),
            blocks(8),
            *([blocks(4)] * 5),
            pltpu.VMEM((8, lanes), f32),
            pltpu.VMEM((128, lanes), bf16),
            pltpu.VMEM((8, lanes), f32),
            pltpu.VMEM((6, 8, small_lanes), f32),
            pltpu.VMEM((6, 8, small_lanes), f32),
            dma(()),
            dma(()),
            *([dma((total,))] * 5),
            dma((2,)),
            *([dma((total,))] * 10),
            dma((total, 3)),
            dma((total,)),
            dma((total, 2)),
            dma((6,)),
            dma((6,)),
            pltpu.SemaphoreType.REGULAR,
        ],
        compiler_params=pltpu.CompilerParams(
            collective_id=0, has_side_effects=True, vmem_limit_bytes=60 * 2**20
        ),
        cost_estimate=pl.CostEstimate(flops=57 * 10**9, bytes_accessed=10**8, transcendentals=10**7),
    )(tokens.T, cotangent.T, bucket_rows, table, gains, wa, wf)


def fused_body(
    tokens,
    cotangent,
    buckets,
    bias_table,
    attn_gain,
    w_query,
    w_key,
    w_value,
    w_output,
    ffn_gain,
    w_gate,
    w_up,
    w_down,
):
    rows, inner_width = w_query.shape
    ff_width = w_gate.shape[1]
    sub = 256
    chunks = ff_width // (2 * sub)
    wa = jnp.stack([w_query, w_key, w_value, w_output]).reshape(2, 2, rows, inner_width)
    wf = jnp.stack([w_gate, w_up, w_down]).reshape(3, rows, chunks, 2, sub)
    wf = wf.transpose(3, 2, 1, 0, 4).reshape(2, chunks, rows, 3 * sub)
    gains = jnp.pad(jnp.stack([attn_gain, ffn_gain], axis=1), ((0, 0), (0, 126)))
    out, gtok, small, ga, gf, _ = fused(tokens, cotangent, buckets, bias_table, gains, wa, wf)
    ga = ga.astype(f32)
    gf = gf.reshape(chunks, 2, rows, 3, sub).astype(f32).transpose(3, 2, 0, 1, 4).reshape(3, rows, ff_width)
    own = lax.dynamic_slice(small, (0, lax.axis_index("shard") * rows), (2, rows))
    table = small[0 : bias_table.shape[1], small.shape[1] - 128 :][:, 0 : bias_table.shape[0]].T
    return (
        out.T,
        gtok.T,
        own[0],
        ga[0, 0],
        ga[0, 1],
        ga[1, 0],
        ga[1, 1],
        own[1],
        gf[0],
        gf[1],
        gf[2],
        table,
    )


def solution(mesh):
    chosen = body
    if mesh.shape["shard"] == 8 and mesh.shape["rep"] == 4:
        chosen = fused_body
    return jax.shard_map(
        chosen,
        mesh=mesh,
        in_specs=(
            P(("shard", "rep"), None),
            P(("shard", "rep"), None),
            P(),
            P(),
            P("shard"),
            P("shard", None),
            P("shard", None),
            P("shard", None),
            P("shard", None),
            P("shard"),
            P("shard", None),
            P("shard", None),
            P("shard", None),
        ),
        out_specs=(
            P(("shard", "rep"), None),
            P(("shard", "rep"), None),
            P("shard"),
            P("shard", None),
            P("shard", None),
            P("shard", None),
            P("shard", None),
            P("shard"),
            P("shard", None),
            P("shard", None),
            P("shard", None),
            P(),
        ),
        check_vma=False,
    )
```

```python
import functools

import jax
import jax.numpy as jnp
from jax import lax
from jax.experimental import pallas as pl
from jax.experimental.pallas import tpu as pltpu
from jax.sharding import PartitionSpec as P

BLOCK = 256
MESH = pl.DeviceIdType.MESH
f32 = jnp.float32
bf16 = jnp.bfloat16


norm_eps = 1e-06
masked_score = -1e30
highest = lax.Precision.HIGHEST


def norm_local(row_values, gain_vector):
    return (
        row_values
        * lax.rsqrt(jnp.mean(row_values * row_values, axis=-1, keepdims=True) + norm_eps)
        * gain_vector
    )


def gelu_tanh(values_in):
    return jax.nn.gelu(values_in, approximate=True)


def diagonal_total(matrix):
    head_count, row_count, key_count = matrix.shape
    flipped = matrix[:, :, ::-1]
    padded = jnp.concatenate(
        [flipped, jnp.zeros((head_count, row_count, row_count), jnp.float32)], axis=2
    )
    flat_rows = padded.reshape(head_count, row_count * (key_count + row_count))
    flat_rows = flat_rows[:, : row_count * (key_count + row_count - 1)]
    return jnp.sum(flat_rows.reshape(head_count, row_count, key_count + row_count - 1), axis=1)


def toeplitz_grid(offset_bias, row_count, length):
    head_count = offset_bias.shape[0]
    span = length + row_count - 1
    flipped = offset_bias[:, ::-1]
    rotated = jnp.concatenate([flipped[:, row_count - 1 :], flipped[:, : row_count - 1]], axis=1)
    tiled = jnp.tile(rotated, (1, row_count))[:, : row_count * (span - 1)]
    return tiled.reshape(head_count, row_count, span - 1)[:, :, :length]


def body(
    tokens,
    cotangent,
    buckets,
    bias_table,
    attn_gain,
    w_query,
    w_key,
    w_value,
    w_output,
    ffn_gain,
    w_gate,
    w_up,
    w_down,
):
    length = tokens.shape[0]
    bucket_count = bias_table.shape[0]
    head_count = bias_table.shape[1]
    inner_width = w_query.shape[1]
    ff_width = w_gate.shape[1]
    owner_rows = w_query.shape[0]
    head_size = inner_width // head_count
    block_rows = min(512, length)
    block_count = length // block_rows
    residual = tokens.astype(jnp.float32)
    attn_set = (
        lax.all_gather(attn_gain, "shard", axis=0, tiled=True),
        lax.all_gather(w_query, "shard", axis=0, tiled=True),
        lax.all_gather(w_key, "shard", axis=0, tiled=True),
        lax.all_gather(w_value, "shard", axis=0, tiled=True),
        lax.all_gather(w_output, "shard", axis=0, tiled=True),
    )
    gain_one = attn_set[0].astype(jnp.float32)
    normed_one = norm_local(residual, gain_one).astype(jnp.bfloat16)

    def project(weight):
        product = jnp.dot(normed_one, weight, preferred_element_type=jnp.float32)
        return product.astype(jnp.bfloat16).reshape(length, head_count, head_size)

    queries = project(attn_set[1])
    key_rows = project(attn_set[2])
    value_rows = project(attn_set[3])
    one_hot = (buckets[:, None] == jnp.arange(bucket_count, dtype=jnp.int32)[None, :]).astype(
        jnp.float32
    )
    offset_bias = jnp.dot(one_hot, bias_table.astype(jnp.float32), precision=highest).T
    block_starts = jnp.arange(block_count, dtype=jnp.int32) * block_rows
    key_index = jnp.arange(length, dtype=jnp.int32)

    def block_scores(first_row, query_block):
        query_index = first_row + jnp.arange(block_rows, dtype=jnp.int32)
        bias_grid = toeplitz_grid(offset_bias, block_rows, length)
        scores = (
            jnp.einsum("qhd,khd->hqk", query_block, key_rows, preferred_element_type=jnp.float32)
            + bias_grid
        )
        allowed = key_index[None, :] // BLOCK <= query_index[:, None] // BLOCK
        return jnp.where(allowed[None], scores, masked_score)

    def attend(first_row):
        scores = block_scores(first_row, queries)
        row_max = jnp.max(scores, axis=-1, keepdims=True)
        exp_scores = jnp.exp(scores - row_max)
        totals = jnp.sum(exp_scores, axis=-1, keepdims=True)
        probability = (exp_scores / totals).astype(jnp.bfloat16)
        mixed_rows = jnp.einsum(
            "hqk,khd->qhd", probability, value_rows, preferred_element_type=jnp.float32
        )
        return (mixed_rows, (row_max + jnp.log(totals))[..., 0])

    mixed_blocks, log_totals = lax.map(attend, block_starts)
    attended = mixed_blocks.reshape(length, inner_width).astype(jnp.bfloat16)
    middle = residual + jnp.einsum(
        "ti,di->td", attended, attn_set[4], preferred_element_type=jnp.float32
    )
    ffn_set = (
        lax.all_gather(ffn_gain, "shard", axis=0, tiled=True),
        lax.all_gather(w_gate, "shard", axis=0, tiled=True),
        lax.all_gather(w_up, "shard", axis=0, tiled=True),
        lax.all_gather(w_down, "shard", axis=0, tiled=True),
    )
    gain_two = ffn_set[0].astype(jnp.float32)
    normed_two = norm_local(middle, gain_two).astype(jnp.bfloat16)
    gate_values = jnp.dot(normed_two, ffn_set[1], preferred_element_type=jnp.float32)
    up_values = jnp.dot(normed_two, ffn_set[2], preferred_element_type=jnp.float32)
    activated, gelu_pullback = jax.vjp(gelu_tanh, gate_values)
    hidden = (activated * up_values).astype(jnp.bfloat16)
    layer_out = (
        middle + jnp.einsum("tf,df->td", hidden, ffn_set[3], preferred_element_type=jnp.float32)
    ).astype(jnp.bfloat16)
    ffn_set = (
        lax.all_gather(ffn_gain, "shard", axis=0, tiled=True),
        lax.all_gather(w_gate, "shard", axis=0, tiled=True),
        lax.all_gather(w_up, "shard", axis=0, tiled=True),
        lax.all_gather(w_down, "shard", axis=0, tiled=True),
    )
    grad_w_down = jnp.einsum("td,tf->df", cotangent, hidden, preferred_element_type=jnp.float32)
    grad_hidden = jnp.dot(cotangent, ffn_set[3], preferred_element_type=jnp.float32)
    grad_gate = gelu_pullback(grad_hidden * up_values)[0].astype(jnp.bfloat16)
    grad_up = (grad_hidden * activated).astype(jnp.bfloat16)
    grad_w_gate = jnp.einsum("td,tf->df", normed_two, grad_gate, preferred_element_type=jnp.float32)
    grad_w_up = jnp.einsum("td,tf->df", normed_two, grad_up, preferred_element_type=jnp.float32)
    grad_normed_two = jnp.einsum(
        "tf,df->td", grad_gate, ffn_set[1], preferred_element_type=jnp.float32
    )
    grad_normed_two = grad_normed_two + jnp.einsum(
        "tf,df->td", grad_up, ffn_set[2], preferred_element_type=jnp.float32
    )
    middle_part, grad_gain_two = jax.vjp(norm_local, middle, gain_two)[1](grad_normed_two)
    grad_middle = cotangent.astype(jnp.float32) + middle_part
    ffn_shards = (
        lax.psum_scatter(grad_w_gate.astype(jnp.bfloat16), "shard", scatter_dimension=0, tiled=True),
        lax.psum_scatter(grad_w_up.astype(jnp.bfloat16), "shard", scatter_dimension=0, tiled=True),
        lax.psum_scatter(grad_w_down.astype(jnp.bfloat16), "shard", scatter_dimension=0, tiled=True),
    )
    attn_set = (
        lax.all_gather(attn_gain, "shard", axis=0, tiled=True),
        lax.all_gather(w_query, "shard", axis=0, tiled=True),
        lax.all_gather(w_key, "shard", axis=0, tiled=True),
        lax.all_gather(w_value, "shard", axis=0, tiled=True),
        lax.all_gather(w_output, "shard", axis=0, tiled=True),
    )
    grad_branch = grad_middle.astype(jnp.bfloat16)
    grad_w_output = jnp.einsum(
        "td,ti->di", grad_branch, attended, preferred_element_type=jnp.float32
    )
    grad_attended = jnp.einsum(
        "td,di->ti", grad_branch, attn_set[4], preferred_element_type=jnp.float32
    )
    grad_attended = grad_attended.astype(jnp.bfloat16).reshape(length, head_count, head_size)

    def attend_back(carried, block_input):
        grad_keys, grad_values, grad_offsets = carried
        first_row, log_total = block_input
        scores = block_scores(first_row, queries)
        probability = jnp.exp(scores - log_total[..., None])
        grad_probs = jnp.einsum(
            "qhd,khd->hqk", grad_attended, value_rows, preferred_element_type=jnp.float32
        )
        inner_sum = jnp.sum(probability * grad_probs, axis=-1, keepdims=True)
        grad_scores = (probability * (grad_probs - inner_sum)).astype(jnp.bfloat16)
        grad_values = grad_values + jnp.einsum(
            "hqk,qhd->khd",
            probability.astype(jnp.bfloat16),
            grad_attended,
            preferred_element_type=jnp.float32,
        )
        grad_keys = grad_keys + jnp.einsum(
            "hqk,qhd->khd", grad_scores, queries, preferred_element_type=jnp.float32
        )
        grad_queries = jnp.einsum(
            "hqk,khd->qhd", grad_scores, key_rows, preferred_element_type=jnp.float32
        )
        diagonal_sums = diagonal_total(grad_scores.astype(jnp.float32))
        offset_piece = grad_offsets
        grad_offsets = offset_piece + diagonal_sums
        return ((grad_keys, grad_values, grad_offsets), grad_queries)

    zero_rows = jnp.zeros((length, head_count, head_size), jnp.float32)
    zero_offsets = jnp.zeros((head_count, 2 * length - 1), jnp.float32)
    (grad_keys, grad_values, grad_offsets), query_blocks = lax.scan(
        attend_back, (zero_rows, zero_rows, zero_offsets), (block_starts, log_totals)
    )
    grad_queries = query_blocks.reshape(length, inner_width).astype(jnp.bfloat16)
    grad_keys = grad_keys.reshape(length, inner_width).astype(jnp.bfloat16)
    grad_values = grad_values.reshape(length, inner_width).astype(jnp.bfloat16)
    grad_w_query = jnp.einsum(
        "td,ti->di", normed_one, grad_queries, preferred_element_type=jnp.float32
    )
    grad_w_key = jnp.einsum("td,ti->di", normed_one, grad_keys, preferred_element_type=jnp.float32)
    grad_w_value = jnp.einsum(
        "td,ti->di", normed_one, grad_values, preferred_element_type=jnp.float32
    )
    grad_normed_one = jnp.einsum(
        "ti,di->td", grad_queries, attn_set[1], preferred_element_type=jnp.float32
    )
    grad_normed_one = grad_normed_one + jnp.einsum(
        "ti,di->td", grad_keys, attn_set[2], preferred_element_type=jnp.float32
    )
    grad_normed_one = grad_normed_one + jnp.einsum(
        "ti,di->td", grad_values, attn_set[3], preferred_element_type=jnp.float32
    )
    rows_part, grad_gain_one = jax.vjp(norm_local, residual, gain_one)[1](grad_normed_one)
    grad_tokens = (grad_middle + rows_part).astype(jnp.bfloat16)
    grad_table = jnp.dot(grad_offsets, one_hot, precision=highest).T
    owner_start = lax.axis_index("shard") * owner_rows
    attn_shards = (
        lax.psum_scatter(grad_w_query.astype(jnp.bfloat16), "shard", scatter_dimension=0, tiled=True),
        lax.psum_scatter(grad_w_key.astype(jnp.bfloat16), "shard", scatter_dimension=0, tiled=True),
        lax.psum_scatter(grad_w_value.astype(jnp.bfloat16), "shard", scatter_dimension=0, tiled=True),
        lax.psum_scatter(grad_w_output.astype(jnp.bfloat16), "shard", scatter_dimension=0, tiled=True),
    )
    summed = lax.psum(
        (
            attn_shards[0],
            attn_shards[1],
            attn_shards[2],
            attn_shards[3],
            ffn_shards[0],
            ffn_shards[1],
            ffn_shards[2],
        ),
        "rep",
    )
    small_total = lax.psum((grad_gain_one, grad_gain_two, grad_table), ("shard", "rep"))
    gain_one_own = lax.dynamic_slice_in_dim(small_total[0], owner_start, owner_rows, 0)
    gain_two_own = lax.dynamic_slice_in_dim(small_total[1], owner_start, owner_rows, 0)
    return (
        layer_out,
        grad_tokens,
        gain_one_own,
        summed[0].astype(jnp.float32),
        summed[1].astype(jnp.float32),
        summed[2].astype(jnp.float32),
        summed[3].astype(jnp.float32),
        gain_two_own,
        summed[4].astype(jnp.float32),
        summed[5].astype(jnp.float32),
        summed[6].astype(jnp.float32),
        small_total[2],
    )


def dot_nn(a, b):
    return lax.dot_general(a, b, (((1,), (0,)), ((), ())), preferred_element_type=f32)


def dot_nt(a, b):
    return lax.dot_general(a, b, (((1,), (1,)), ((), ())), preferred_element_type=f32)


def dot_tn(a, b):
    return lax.dot_general(a, b, (((0,), (0,)), ((), ())), preferred_element_type=f32)


def fused_kernel(
    xt_ref,
    ct_ref,
    buckets_ref,
    table_ref,
    gains_ref,
    wq_ref,
    wk_ref,
    wv_ref,
    wo_ref,
    wg_ref,
    wu_ref,
    wd_ref,
    out_ref,
    gtok_ref,
    small_ref,
    gq_ref,
    gk_ref,
    gv_ref,
    go_ref,
    gg_ref,
    gu_ref,
    gd_ref,
    land_ref,
    gland,
    gcol,
    n1t,
    n2t,
    mid,
    acc_o,
    acc_n,
    qt,
    kt,
    vt,
    att,
    dat,
    dqt,
    dkt,
    dvt,
    wq,
    wk,
    wv,
    wo,
    wg2,
    wu2,
    wd2,
    wload,
    g,
    hid,
    dgt,
    dup,
    rc,
    rxy,
    r2,
    vbuf,
    zi,
    zm,
    ubuf,
    revb,
    onehot,
    doff,
    sms,
    smr,
    gain_s,
    gain_r,
    gsend,
    gloc,
    g1r,
    g2r,
    gpr,
    load_sem,
    e0s,
    e0r,
    e1s,
    e1r,
    e2s,
    e2r,
    zis,
    zir,
    zms,
    zmr,
    us,
    ul,
    ur,
    sss,
    ssr,
    zcredit,
    *,
    chunks,
    heads,
):
    width = xt_ref.shape[0]
    toks = xt_ref.shape[1]
    rows = gains_ref.shape[0]
    fw = land_ref.shape[3]
    sub = fw // 3
    aw = wq_ref.shape[1]
    hs = aw // heads
    total = chunks + 2
    eps = 1e-06
    lanes = revb.shape[1]
    big = 2 * rows
    nbig = width // big

    s = lax.axis_index("shard")
    r = lax.axis_index("rep")
    c = s % 2
    x = (s // 2) % 2
    y = s // 4
    sc = s + 1 - 2 * c
    sx = s + 2 - 4 * x
    sy = s + 4 - 8 * y
    bx = sx - c
    by = sy - c
    bd = (1 - y) * 4 + (1 - x) * 2
    b_own = s - c
    mate = r + 1 - 2 * (r % 2)
    inner = (r == 1) | (r == 2)
    outer = (r == 0) | (r == 3)

    def remote(src, dst, ssem, rsem, dev):
        return pltpu.make_async_remote_copy(
            src_ref=src, dst_ref=dst, send_sem=ssem, recv_sem=rsem, device_id=dev, device_id_type=MESH
        )

    def settle(ref, sem):
        pltpu.make_async_copy(ref, ref, sem).wait()

    barrier = pltpu.get_barrier_semaphore()
    near = [(sc, r), (bx, r), (bx + 1, r), (by, r), (by + 1, r), (bd, r), (bd + 1, r), (s, mate), (sc, mate)]
    for dev in near:
        pl.semaphore_signal(barrier, inc=1, device_id=dev, device_id_type=MESH)

    @pl.when(inner)
    def _():
        pl.semaphore_signal(barrier, inc=1, device_id=(s, 3 - r), device_id_type=MESH)

    @pl.when(inner)
    def _():
        pl.semaphore_wait(barrier, len(near) + 1)

    @pl.when(outer)
    def _():
        pl.semaphore_wait(barrier, len(near))

    def place(chunk, index):
        kind, k = chunk
        if kind == "a":
            return g.at[16 + index, :, pl.ds(k * aw, aw)]
        return land_ref.at[k, index]

    def places(chunk, count):
        kind, k = chunk
        if kind == "a":
            return g.at[pl.ds(16, count), :, pl.ds(k * aw, aw)]
        return land_ref.at[k, pl.ds(0, count)]

    def columns(k, half):
        return pl.ds(pl.multiple_of((2 * k + half) * sub, sub), sub)

    def own_parts(chunk, half):
        kind, k = chunk
        dst = place(chunk, half * 8 + s)
        if kind == "a":
            return [(((wq_ref, wk_ref), (wv_ref, wo_ref))[k][half], dst)]
        return [
            (ref.at[:, columns(k, half)], dst.at[:, pl.ds(j * sub, sub)]) for j, ref in enumerate((wg_ref, wu_ref, wd_ref))
        ]

    def at(chunk):
        kind, k = chunk
        return k if kind == "a" else k + 2

    def gather_send(chunk):
        i = at(chunk)
        for half in (0, 1):
            for src, dst in own_parts(chunk, half):
                remote(src, dst, gsend.at[i], g1r.at[i], (bx + half, r)).start()
                remote(src, dst, gsend.at[i], g1r.at[i], (by + half, r)).start()
        for half in (0, 1):
            for src, dst in own_parts(chunk, half):
                remote(src, dst, gsend.at[i], gpr.at[i], (sc, r)).start()
                pltpu.make_async_copy(src, dst, gloc.at[i]).start()

    def gather_forward(chunk):
        i = at(chunk)
        settle(places(chunk, 4), g1r.at[i])
        one = place(chunk, c * 8 + bx)
        two = place(chunk, c * 8 + by + 1)
        remote(one, one, gsend.at[i], g2r.at[i], (sy, r)).start()
        remote(two, two, gsend.at[i], g2r.at[i], (sx, r)).start()
        for b in (bx, bx + 1, by, by + 1):
            spot = place(chunk, c * 8 + b)
            remote(spot, spot, gsend.at[i], gpr.at[i], (sc, r)).start()

    def gather_swap(chunk):
        i = at(chunk)
        settle(places(chunk, 2), g2r.at[i])
        for b in (bd, bd + 1):
            spot = place(chunk, c * 8 + b)
            remote(spot, spot, gsend.at[i], gpr.at[i], (sc, r)).start()

    def gather_done(chunk):
        i = at(chunk)
        settle(places(chunk, 8), gpr.at[i])
        settle(places(chunk, 2), gloc.at[i])

    def gather_sent(chunk):
        settle(places(chunk, 14), gsend.at[at(chunk)])

    def cut(ref, w):
        return ref if w == fw else ref.at[:, :, pl.ds(0, w)]

    def cut1(ref, index, w):
        return ref.at[index] if w == fw else ref.at[index, :, pl.ds(0, w)]

    def span(ref, start, count, w):
        return ref.at[pl.ds(start, count)] if w == fw else ref.at[pl.ds(start, count), :, pl.ds(0, w)]

    def get(ref, index, w):
        return ref[index] if w == fw else ref[index, :, 0:w]

    def put(ref, index, w, value):
        if w == fw:
            ref[index] = value
        else:
            ref[index, :, 0:w] = value

    def add_to(dst, i, src, j, w):
        value = get(dst, i, w).astype(f32) + get(src, j, w).astype(f32)
        put(dst, i, w, value.astype(bf16))

    def core_send(n, w):
        slot = n % 2
        remote(
            span(g, slot * 16 + (1 - c) * 8, 8, w), span(rc, slot * 8, 8, w), e0s.at[n], e0r.at[n], (sc, r)
        ).start()

    def plane_send(n, w):
        slot = n % 2
        base = slot * 16 + c * 8
        settle(span(rc, slot * 8, 8, w), e0r.at[n])

        @pl.loop(0, 8)
        def _(b):
            add_to(g, base + b, rc, slot * 8 + b, w)

        for k in (0, 1):
            remote(
                cut1(g, base + 4 * k + 2 * (1 - x), w), cut1(rxy, slot * 4 + k, w), e1s.at[n], e1r.at[n], (sx, r)
            ).start()
            remote(
                cut1(g, base + 4 * (1 - y) + 2 * k + 1, w),
                cut1(rxy, slot * 4 + 2 + k, w),
                e1s.at[n],
                e1r.at[n],
                (sy, r),
            ).start()

    def plane_turn(n, w):
        slot = n % 2
        base = slot * 16 + c * 8
        settle(span(rxy, slot * 4, 4, w), e1r.at[n])
        first = base + 4 * (1 - y) + 2 * x
        second = base + 4 * y + 2 * (1 - x) + 1
        mine = base + b_own
        add_to(g, first, rxy, slot * 4 + 1 - y, w)
        add_to(g, second, rxy, slot * 4 + 2 + 1 - x, w)
        add_to(g, mine, rxy, slot * 4 + y, w)
        add_to(g, mine + 1, rxy, slot * 4 + 2 + x, w)
        remote(cut1(g, first, w), cut1(r2, slot * 2, w), e2s.at[n], e2r.at[n], (sy, r)).start()
        remote(cut1(g, second, w), cut1(r2, slot * 2 + 1, w), e2s.at[n], e2r.at[n], (sx, r)).start()

    def rep_send(n, w):
        slot = n % 2
        base = slot * 16 + c * 8
        settle(span(r2, slot * 2, 2, w), e2r.at[n])
        if isinstance(n, int):
            if n >= 2:
                pl.when(outer)(functools.partial(rep_free, n))
        else:
            pl.when(outer & (n >= 2))(functools.partial(rep_free, n))
        for j in (0, 1):
            value = get(g, base + b_own + j, w).astype(f32) + get(r2, slot * 2 + j, w).astype(f32)
            put(vbuf, slot * 2 + j, w, value.astype(bf16))

        @pl.when(outer)
        def _():
            remote(
                span(vbuf, slot * 2, 2, w), span(zi, slot * 2, 2, w), zis.at[n], zir.at[n], (s, mate)
            ).start()

        settle(span(g, slot * 16, 8, w), e0s.at[n])
        settle(span(rxy, slot * 4, 4, w), e1s.at[n])
        settle(span(r2, slot * 2, 2, w), e2s.at[n])

    def width_of(n):
        return fw if not isinstance(n, int) or n < chunks else aw

    def rep_free(n):
        earlier = n - 2
        slot = n % 2
        settle(span(vbuf, slot * 2, 2, width_of(earlier)), zis.at[earlier])
        pl.semaphore_wait(zcredit, 1)

    def rep_turn(n, w):
        slot = n % 2

        @pl.when(inner)
        def _():
            settle(span(zi, slot * 2, 2, w), zir.at[n])
            for j in (0, 1):
                add_to(vbuf, slot * 2 + j, zi, slot * 2 + j, w)

            def credit():
                pl.semaphore_signal(zcredit, inc=1, device_id=(s, mate), device_id_type=MESH)

            if isinstance(n, int):
                if n + 2 < total:
                    credit()
            else:
                credit()
            remote(
                span(vbuf, slot * 2, 2, w), span(zm, slot * 2, 2, w), zms.at[n], zmr.at[n], (s, 3 - r)
            ).start()

    def result(n, half, block):
        if isinstance(n, int) and n >= chunks:
            return [(block, ((gv_ref, go_ref), (gq_ref, gk_ref))[n - chunks][half])]
        return [
            (block.at[:, pl.ds(j * sub, sub)], ref.at[:, columns(n, half)])
            for j, ref in enumerate((gg_ref, gu_ref, gd_ref))
        ]

    def u_free(n, w):
        slot = n % 2
        for k in (0, 1, 2):
            settle(cut1(ubuf, slot * 2, w), us.at[n, k])
        settle(cut1(ubuf, slot * 2, w), ul.at[n])

    def rep_last(n, w):
        slot = n % 2

        @pl.when(inner)
        def _():
            settle(span(zm, slot * 2, 2, w), zmr.at[n])
            if isinstance(n, int):
                if n >= 2:
                    u_free(n - 2, width_of(n - 2))
            else:
                pl.when(n >= 2)(lambda: u_free(n - 2, w))
            for j in (0, 1):
                value = get(vbuf, slot * 2 + j, w).astype(f32) + get(zm, slot * 2 + j, w).astype(f32)
                put(ubuf, slot * 2 + j, w, value.astype(bf16))
            keep = cut1(ubuf, slot * 2 + c, w)
            give = cut1(ubuf, slot * 2 + 1 - c, w)

            def finish(half):
                for src, dst in result(n, half, keep):
                    remote(src, dst, us.at[n, 0], ur.at[n, half], (s, mate)).start()
                    pltpu.make_async_copy(src, dst, ul.at[n]).start()
                for src, dst in result(n, half, give):
                    remote(src, dst, us.at[n, 1], ur.at[n, half], (sc, mate)).start()
                    remote(src, dst, us.at[n, 2], ur.at[n, half], (sc, r)).start()

            if w == fw:
                finish(c)
            else:
                pl.when(c == 0)(lambda: finish(0))
                pl.when(c == 1)(lambda: finish(1))
            settle(span(vbuf, slot * 2, 2, w), zms.at[n])

    def small_send(step):
        if step < 3:
            dev = ((sc, r), (sx, r), (sy, r))[step]
            remote(sms.at[step], smr.at[step], sss.at[step], ssr.at[step], dev).start()
        elif step == 3:

            @pl.when(outer)
            def _():
                remote(sms.at[3], smr.at[3], sss.at[3], ssr.at[3], (s, mate)).start()
        elif step == 4:

            @pl.when(inner)
            def _():
                remote(sms.at[4], smr.at[4], sss.at[4], ssr.at[4], (s, 3 - r)).start()
        else:

            @pl.when(inner)
            def _():
                remote(sms.at[5], smr.at[5], sss.at[5], ssr.at[5], (s, mate)).start()

    def small_step(step):
        def take():
            settle(smr.at[step], ssr.at[step])
            settle(sms.at[step], sss.at[step])
            if step < 2:
                sms[step + 1] = sms[step] + smr[step]
            elif step == 2:
                sms[3] = sms[2] + smr[2]

        if step < 3:
            take()
            small_send(step + 1)
        elif step == 3:

            @pl.when(inner)
            def _():
                settle(smr.at[3], ssr.at[3])
                sms[4] = sms[3] + smr[3]

            @pl.when(outer)
            def _():
                settle(sms.at[3], sss.at[3])

            small_send(4)
        elif step == 4:

            @pl.when(inner)
            def _():
                settle(smr.at[4], ssr.at[4])
                settle(sms.at[4], sss.at[4])
                sms[5] = sms[4] + smr[4]
                small_ref[...] = sms[5]

            small_send(5)
        else:

            @pl.when(inner)
            def _():
                settle(sms.at[5], sss.at[5])

            @pl.when(outer)
            def _():
                settle(smr.at[5], ssr.at[5])
                small_ref[...] = smr[5]

    tile = 64
    tiles = width // tile

    def over_rows(body, start):
        def step(i, carry):
            return body(pl.ds(pl.multiple_of(i * tile, tile), tile), carry)

        return lax.fori_loop(0, tiles, step, start)

    def fold(value):
        return jnp.sum(value.reshape(tile // 8, 8, toks), axis=0)

    zero8 = jnp.zeros((8, toks), f32)

    gather_send(("a", 0))
    gdst = gland.at[s]
    for k, dev in enumerate([(sc, r), (bx, r), (bx + 1, r), (by, r), (by + 1, r), (bd, r), (bd + 1, r)]):
        remote(gains_ref, gdst, gain_s, gain_r, dev).start()
    pltpu.make_async_copy(gains_ref, gdst, load_sem.at[1]).start()
    gather_send(("a", 1))
    gather_send(("f", 0))

    def square_sum(sl, acc):
        v = xt_ref[sl, :].astype(f32)
        return acc + fold(v * v)

    ssum = jnp.sum(over_rows(square_sum, zero8), axis=0, keepdims=True)
    r1 = lax.rsqrt(ssum * (1.0 / width) + eps)

    bucket_index = lax.broadcasted_iota(jnp.int32, (table_ref.shape[1], lanes), 0)
    rev_hot = (bucket_index == buckets_ref[0:1, :]).astype(bf16)
    onehot[...] = (bucket_index == buckets_ref[1:2, :]).astype(bf16)
    revb[...] = dot_nn(table_ref[...], rev_hot)

    settle(gland.at[pl.ds(0, 7)], gain_r)
    settle(gland.at[0], load_sem.at[1])
    for b in range(8):
        gcol[rows * b : rows * (b + 1), :] = gland[b].astype(f32)

    def norm_one(sl, carry):
        v = xt_ref[sl, :].astype(f32)
        n1t[sl, :] = (v * r1 * gcol[sl, 0:1]).astype(bf16)
        return carry

    gather_forward(("a", 0))
    over_rows(norm_one, 0)
    gather_swap(("a", 0))
    gather_forward(("a", 1))
    gather_send(("f", 1))

    def compact(dst, half, col):
        @pl.loop(0, nbig)
        def _(i):
            both = jnp.concatenate(
                [
                    g[16 + half * 8 + 2 * i, :, col : col + aw].astype(f32),
                    g[16 + half * 8 + 2 * i + 1, :, col : col + aw].astype(f32),
                ],
                axis=0,
            )
            dst[pl.ds(pl.multiple_of(i * 2 * rows, 16), 2 * rows), :] = both.astype(bf16)

    gather_done(("a", 0))
    compact(wq, 0, 0)
    qt[...] = dot_tn(wq[...], n1t[...]).astype(bf16)
    compact(wk, 1, 0)
    kt[...] = dot_tn(wk[...], n1t[...]).astype(bf16)
    gather_swap(("a", 1))
    gather_done(("a", 1))
    compact(wv, 0, aw)
    vt[...] = dot_tn(wv[...], n1t[...]).astype(bf16)
    compact(wo, 1, aw)
    gather_forward(("f", 0))
    gather_send(("f", 2))

    half_tok = toks // 2

    def softmax_block(h, head, block):
        keys = half_tok * (block + 1)
        low = half_tok * block
        row = jnp.broadcast_to(revb[pl.ds(h, 1), :], (half_tok, lanes))
        bias = pltpu.roll(row, (low + 1 - toks) % lanes, 1, stride=1, stride_axis=0)[:, :keys]
        scores = dot_tn(qt[head, low : low + half_tok], kt[head, 0:keys]) + bias
        e = jnp.exp(scores - jnp.max(scores, axis=1, keepdims=True))
        return e * (1.0 / jnp.sum(e, axis=1, keepdims=True)), low, keys

    def attend(h, carry):
        head = pl.ds(pl.multiple_of(h * hs, hs), hs)
        for block in (0, 1):
            p, low, keys = softmax_block(h, head, block)
            att[head, low : low + half_tok] = dot_nt(vt[head, 0:keys], p.astype(bf16)).astype(bf16)
        return carry

    lax.fori_loop(0, heads // 2, attend, 0)
    gather_swap(("f", 0))
    gather_forward(("f", 1))
    lax.fori_loop(heads // 2, heads, attend, 0)

    def branch_one(i, acc):
        sl = pl.ds(pl.multiple_of(i * big, 16), big)
        m = xt_ref[sl, :].astype(f32) + dot_nn(wo[sl, :], att[...])
        mid[sl, :] = m
        return acc + jnp.sum((m * m).reshape(big // 8, 8, toks), axis=0)

    ssum = jnp.sum(lax.fori_loop(0, nbig, branch_one, zero8), axis=0, keepdims=True)
    r2n = lax.rsqrt(ssum * (1.0 / width) + eps)

    def norm_two(sl, carry):
        m = mid[sl, :]
        n2t[sl, :] = (m * r2n * gcol[sl, 1:2]).astype(bf16)
        acc_o[sl, :] = m
        acc_n[sl, :] = jnp.zeros((tile, toks), f32)
        return carry

    over_rows(norm_two, 0)

    tok_tile = toks // 2

    def ffn_chunk(t):
        slot = t % 2
        parts = [(half, k) for half in (0, 1) for k in (0, 1, 2)]

        def load(p):
            half, k = parts[p]
            return pltpu.make_async_copy(
                land_ref.at[t, pl.ds(half * 8, 8), :, pl.ds(k * sub, sub)],
                wload.at[pl.ds((p % 2) * 8, 8)],
                load_sem.at[p % 2],
            )

        load(0).start()
        for p, (half, k) in enumerate(parts):
            if p + 1 < len(parts):
                load(p + 1).start()
            load(p).wait()
            dst = (wg2, wu2, wd2)[k]

            @pl.loop(0, nbig)
            def _(i):
                base = (p % 2) * 8 + 2 * i
                both = jnp.concatenate([wload[base].astype(f32), wload[base + 1].astype(f32)], axis=0)
                sl = pl.ds(pl.multiple_of(i * big, 16), big)
                dst[sl, half * sub : (half + 1) * sub] = both.astype(bf16)

        @pl.loop(0, toks // tok_tile)
        def _(m):
            sl = pl.ds(pl.multiple_of(m * tok_tile, tok_tile), tok_tile)
            gate = dot_tn(n2t[:, sl], wg2[...])
            up = dot_tn(n2t[:, sl], wu2[...])
            gh = dot_tn(ct_ref[:, sl], wd2[...])
            k0 = 0.7978845608028654
            k1 = 0.044715
            sq = gate * gate
            th = jnp.tanh(k0 * (gate + k1 * (sq * gate)))
            half_one = 0.5 * (1.0 + th)
            act = gate * half_one
            slope = half_one + 0.5 * gate * (1.0 - th * th) * (k0 * (1.0 + 3.0 * k1 * sq))
            hid[sl, :] = (act * up).astype(bf16)
            dgt[sl, :] = (gh * up * slope).astype(bf16)
            dup[sl, :] = (gh * act).astype(bf16)

        @pl.loop(0, nbig)
        def _(i):
            sl = pl.ds(pl.multiple_of(i * big, 16), big)
            acc_o[sl, :] += dot_nt(wd2[sl, :], hid[...])
            acc_n[sl, :] += dot_nt(wg2[sl, :], dgt[...]) + dot_nt(wu2[sl, :], dup[...])
            for k, value in enumerate(
                (dot_nn(n2t[sl, :], dgt[...]), dot_nn(n2t[sl, :], dup[...]), dot_nn(ct_ref[sl, :], hid[...]))
            ):
                for half in (0, 1):
                    for j in (0, 1):
                        g[slot * 16 + half * 8 + 2 * i + j, :, k * sub : (k + 1) * sub] = value[
                            rows * j : rows * (j + 1), half * sub : (half + 1) * sub
                        ].astype(bf16)

    def ffn_step(t, carry):
        pl.when(t + 1 < chunks)(lambda: gather_swap(("f", t + 1)))
        pl.when(t + 2 < chunks)(lambda: gather_forward(("f", t + 2)))
        pl.when(t + 3 < chunks)(lambda: gather_send(("f", t + 3)))
        pl.when(t >= 3)(lambda: rep_turn(t - 3, fw))
        pl.when(t >= 2)(lambda: rep_send(t - 2, fw))
        gather_done(("f", t))
        ffn_chunk(t)
        core_send(t, fw)
        pl.when(t >= 3)(lambda: rep_last(t - 3, fw))
        pl.when(t >= 1)(lambda: plane_turn(t - 1, fw))
        plane_send(t, fw)
        return carry

    gather_sent(("a", 0))
    gather_sent(("a", 1))
    lax.fori_loop(0, chunks, ffn_step, 0)

    nv = chunks
    nq = chunks + 1
    rep_turn(nv - 3, fw)
    rep_send(nv - 2, fw)
    pick = lax.broadcasted_iota(jnp.int32, (8, toks), 0)

    def token_sums(row):
        chosen = (pick == row).astype(bf16)
        return dot_nt(chosen, wg2[...]) + dot_nt(chosen, wu2[...])

    def second_mean(sl, acc):
        return acc + fold(gcol[sl, 1:2] * acc_n[sl, :] * mid[sl, :])

    back = jnp.sum(over_rows(second_mean, zero8), axis=0, keepdims=True) * (1.0 / width)
    back = back * (r2n * r2n * r2n)

    def second_norm(sl, carry):
        m = mid[sl, :]
        gn = acc_n[sl, :]
        out_ref[sl, :] = acc_o[sl, :].astype(bf16)
        v = gn * m * r2n
        hi = v.astype(bf16)
        wg2[sl, :] = hi
        wu2[sl, :] = (v - hi.astype(f32)).astype(bf16)
        gm = ct_ref[sl, :].astype(f32) + r2n * gcol[sl, 1:2] * gn - m * back
        acc_n[sl, :] = gm
        n2t[sl, :] = gm.astype(bf16)
        return carry

    over_rows(second_norm, 0)
    sms[0] = jnp.zeros(sms.shape[1:], f32)
    sms[0, :, 0:width] = token_sums(1)
    rep_last(nv - 3, fw)
    plane_turn(nv - 1, fw)

    dat[...] = dot_tn(wo[...], n2t[...]).astype(bf16)

    def weight_grad(n, half, left, right):
        @pl.loop(0, nbig)
        def _(i):
            sl = pl.ds(pl.multiple_of(i * big, 16), big)
            value = dot_nt(left[sl, :], right[...])
            for j in (0, 1):
                g[(n % 2) * 16 + half * 8 + 2 * i + j, :, 0:aw] = value[rows * j : rows * (j + 1), :].astype(bf16)

    weight_grad(nv, 1, n2t, att)
    flip = (
        lax.broadcasted_iota(jnp.int32, (toks, toks), 0) + lax.broadcasted_iota(jnp.int32, (toks, toks), 1)
        == toks - 1
    )
    hid[...] = flip.astype(bf16)
    doff[...] = jnp.zeros(doff.shape, f32)

    def attend_back(h, carry):
        head = pl.ds(pl.multiple_of(h * hs, hs), hs)
        grad_v = []
        grad_k = []
        offsets = jnp.zeros((1, lanes), f32)
        for block in (0, 1):
            p, low, keys = softmax_block(h, head, block)
            q_rows = qt[head, low : low + half_tok]
            a_rows = dat[head, low : low + half_tok]
            grad_p = dot_tn(a_rows, vt[head, 0:keys])
            ds = (p * (grad_p - jnp.sum(p * grad_p, axis=1, keepdims=True))).astype(bf16)
            grad_v.append(dot_nn(a_rows, p.astype(bf16)))
            grad_k.append(dot_nn(q_rows, ds))
            dqt[head, low : low + half_tok] = dot_nt(kt[head, 0:keys], ds).astype(bf16)
            turned = dot_nn(ds, hid[0:keys, toks - keys : toks])
            padded = jnp.concatenate([turned, jnp.zeros((half_tok, lanes - keys), f32)], axis=1)
            lined = pltpu.roll(padded, half_tok, 1, stride=1, stride_axis=0)
            offsets = offsets + jnp.sum(lined, axis=0, keepdims=True)
        for dst, parts in ((dvt, grad_v), (dkt, grad_k)):
            dst[head, 0:half_tok] = (parts[0] + parts[1][:, 0:half_tok]).astype(bf16)
            dst[head, half_tok:toks] = parts[1][:, half_tok:toks].astype(bf16)
        doff[pl.ds(h, 1), :] = offsets
        return carry

    lax.fori_loop(0, heads // 2, attend_back, 0)
    rep_turn(nv - 2, fw)
    rep_send(nv - 1, fw)
    lax.fori_loop(heads // 2, heads, attend_back, 0)
    rep_last(nv - 2, fw)
    rep_turn(nv - 1, fw)
    weight_grad(nv, 0, n1t, dvt)
    core_send(nv, aw)
    weight_grad(nq, 0, n1t, dqt)
    weight_grad(nq, 1, n1t, dkt)
    plane_send(nv, aw)
    core_send(nq, aw)
    rep_last(nv - 1, fw)
    plane_send(nq, aw)

    def first_back(i, acc):
        sl = pl.ds(pl.multiple_of(i * big, 16), big)
        gn = dot_nn(wq[sl, :], dqt[...]) + dot_nn(wk[sl, :], dkt[...]) + dot_nn(wv[sl, :], dvt[...])
        acc_o[sl, :] = gn
        v = gcol[sl, 0:1] * gn * xt_ref[sl, :].astype(f32)
        return acc + jnp.sum(v.reshape(big // 8, 8, toks), axis=0)

    back = jnp.sum(lax.fori_loop(0, nbig, first_back, zero8), axis=0, keepdims=True) * (1.0 / width)
    back = back * (r1 * r1 * r1)
    plane_turn(nv, aw)

    def first_norm(sl, carry):
        v = xt_ref[sl, :].astype(f32)
        gn = acc_o[sl, :]
        prod = gn * v * r1
        hi = prod.astype(bf16)
        wg2[sl, :] = hi
        wu2[sl, :] = (prod - hi.astype(f32)).astype(bf16)
        gtok_ref[sl, :] = (acc_n[sl, :] + r1 * gcol[sl, 0:1] * gn - v * back).astype(bf16)
        return carry

    over_rows(first_norm, 0)
    sms[0, :, 0:width] += token_sums(0)
    rest = doff[...]
    table = jnp.zeros((8, onehot.shape[0]), f32)
    for _ in range(3):
        part = rest.astype(bf16)
        table = table + dot_nt(part, onehot[...])
        rest = rest - part.astype(f32)
    sms[0, :, sms.shape[2] - onehot.shape[0] : sms.shape[2]] = table
    small_send(0)
    plane_turn(nq, aw)
    small_step(0)
    rep_send(nv, aw)
    small_step(1)
    rep_send(nq, aw)
    small_step(2)
    rep_turn(nv, aw)
    small_step(3)
    rep_last(nv, aw)
    rep_turn(nq, aw)
    small_step(4)
    rep_last(nq, aw)
    small_step(5)

    settle(gland.at[pl.ds(0, 7)], gain_s)
    lax.fori_loop(0, chunks, lambda k, carry: (gather_sent(("f", k)), carry)[1], 0)

    @pl.when(outer)
    def _():
        for n in (nv, nq):
            settle(span(vbuf, (n % 2) * 2, 2, aw), zis.at[n])
        for n in range(total):
            for half in (0, 1):
                settle(cut1(ubuf, 0, width_of(n)), ur.at[n, half])

    @pl.when(inner)
    def _():
        for n in (nv, nq):
            u_free(n, aw)
        for n in range(total):
            settle(cut1(ubuf, 0, width_of(n)), ur.at[n, 1 - c])


def fused(tokens, cotangent, buckets, bias_table, gains, weights):
    toks, width = tokens.shape
    heads = bias_table.shape[1]
    rows, aw = weights[0].shape
    ff = weights[4].shape[1]
    sub = 256
    fw = 3 * sub
    chunks = ff // (2 * sub)
    total = chunks + 2
    lanes = 2 * toks
    small_lanes = (width + 127) // 128 * 128 + 128
    padded = jnp.concatenate([buckets, jnp.full((1,), -1, jnp.int32)])
    turned = jnp.concatenate([buckets[::-1], jnp.full((1,), -1, jnp.int32)])
    bucket_rows = jnp.concatenate([turned[None], padded[None], jnp.full((6, lanes), -1, jnp.int32)])
    table = jnp.pad(bias_table.T, ((0, 8 - heads), (0, 128 - bias_table.shape[0])))
    vm = pl.BlockSpec(memory_space=pltpu.VMEM)
    hbm = pl.BlockSpec(memory_space=pltpu.HBM)
    dma = pltpu.SemaphoreType.DMA
    tok = lambda kind: pltpu.VMEM((width, toks), kind)
    inner_rows = pltpu.VMEM((aw, toks), bf16)
    blocks = lambda count: pltpu.VMEM((count, rows, fw), bf16)
    return pl.pallas_call(
        functools.partial(fused_kernel, chunks=chunks, heads=heads),
        out_shape=(
            jax.ShapeDtypeStruct((width, toks), bf16),
            jax.ShapeDtypeStruct((width, toks), bf16),
            jax.ShapeDtypeStruct((8, small_lanes), f32),
            *([jax.ShapeDtypeStruct((rows, aw), bf16)] * 4),
            *([jax.ShapeDtypeStruct((rows, ff), bf16)] * 3),
            jax.ShapeDtypeStruct((chunks, 16, rows, fw), bf16),
        ),
        in_specs=[vm] * 5 + [hbm] * 7,
        out_specs=[vm] * 3 + [hbm] * 8,
        scratch_shapes=[
            pltpu.VMEM((8, rows, 128), bf16),
            pltpu.VMEM((width, 128), f32),
            tok(bf16),
            tok(bf16),
            tok(f32),
            tok(f32),
            tok(f32),
            *([inner_rows] * 8),
            *([pltpu.VMEM((width, aw), bf16)] * 4),
            *([pltpu.VMEM((width, 2 * sub), bf16)] * 3),
            pltpu.VMEM((16, rows, sub), bf16),
            blocks(32),
            *([pltpu.VMEM((toks, 2 * sub), bf16)] * 3),
            blocks(16),
            blocks(8),
            *([blocks(4)] * 5),
            pltpu.VMEM((8, lanes), f32),
            pltpu.VMEM((128, lanes), bf16),
            pltpu.VMEM((8, lanes), f32),
            pltpu.VMEM((6, 8, small_lanes), f32),
            pltpu.VMEM((6, 8, small_lanes), f32),
            dma(()),
            dma(()),
            *([dma((total,))] * 5),
            dma((2,)),
            *([dma((total,))] * 10),
            dma((total, 3)),
            dma((total,)),
            dma((total, 2)),
            dma((6,)),
            dma((6,)),
            pltpu.SemaphoreType.REGULAR,
        ],
        compiler_params=pltpu.CompilerParams(
            collective_id=0, has_side_effects=True, vmem_limit_bytes=60 * 2**20
        ),
        cost_estimate=pl.CostEstimate(flops=57 * 10**9, bytes_accessed=10**8, transcendentals=10**7),
    )(tokens.T, cotangent.T, bucket_rows, table, gains, *weights)


def fused_body(
    tokens,
    cotangent,
    buckets,
    bias_table,
    attn_gain,
    w_query,
    w_key,
    w_value,
    w_output,
    ffn_gain,
    w_gate,
    w_up,
    w_down,
):
    rows = w_query.shape[0]
    gains = jnp.pad(jnp.stack([attn_gain, ffn_gain], axis=1), ((0, 0), (0, 126)))
    weights = (w_query, w_key, w_value, w_output, w_gate, w_up, w_down)
    out, gtok, small, *grads = fused(tokens, cotangent, buckets, bias_table, gains, weights)
    grads = [grad.astype(f32) for grad in grads[:7]]
    own = lax.dynamic_slice(small, (0, lax.axis_index("shard") * rows), (2, rows))
    table = small[0 : bias_table.shape[1], small.shape[1] - 128 :][:, 0 : bias_table.shape[0]].T
    return (out.T, gtok.T, own[0], *grads[:4], own[1], *grads[4:], table)


def solution(mesh):
    chosen = body
    if mesh.shape["shard"] == 8 and mesh.shape["rep"] == 4:
        chosen = fused_body
    return jax.shard_map(
        chosen,
        mesh=mesh,
        in_specs=(
            P(("shard", "rep"), None),
            P(("shard", "rep"), None),
            P(),
            P(),
            P("shard"),
            P("shard", None),
            P("shard", None),
            P("shard", None),
            P("shard", None),
            P("shard"),
            P("shard", None),
            P("shard", None),
            P("shard", None),
        ),
        out_specs=(
            P(("shard", "rep"), None),
            P(("shard", "rep"), None),
            P("shard"),
            P("shard", None),
            P("shard", None),
            P("shard", None),
            P("shard", None),
            P("shard"),
            P("shard", None),
            P("shard", None),
            P("shard", None),
            P(),
        ),
        check_vma=False,
    )
```

```python
import functools

import jax
import jax.numpy as jnp
from jax import lax
from jax.experimental import pallas as pl
from jax.experimental.pallas import tpu as pltpu
from jax.sharding import PartitionSpec as P

BLOCK = 256
MESH = pl.DeviceIdType.MESH
f32 = jnp.float32
bf16 = jnp.bfloat16


norm_eps = 1e-06
masked_score = -1e30
highest = lax.Precision.HIGHEST


def norm_local(row_values, gain_vector):
    return (
        row_values
        * lax.rsqrt(jnp.mean(row_values * row_values, axis=-1, keepdims=True) + norm_eps)
        * gain_vector
    )


def gelu_tanh(values_in):
    return jax.nn.gelu(values_in, approximate=True)


def diagonal_total(matrix):
    head_count, row_count, key_count = matrix.shape
    flipped = matrix[:, :, ::-1]
    padded = jnp.concatenate(
        [flipped, jnp.zeros((head_count, row_count, row_count), jnp.float32)], axis=2
    )
    flat_rows = padded.reshape(head_count, row_count * (key_count + row_count))
    flat_rows = flat_rows[:, : row_count * (key_count + row_count - 1)]
    return jnp.sum(flat_rows.reshape(head_count, row_count, key_count + row_count - 1), axis=1)


def toeplitz_grid(offset_bias, row_count, length):
    head_count = offset_bias.shape[0]
    span = length + row_count - 1
    flipped = offset_bias[:, ::-1]
    rotated = jnp.concatenate([flipped[:, row_count - 1 :], flipped[:, : row_count - 1]], axis=1)
    tiled = jnp.tile(rotated, (1, row_count))[:, : row_count * (span - 1)]
    return tiled.reshape(head_count, row_count, span - 1)[:, :, :length]


def body(
    tokens,
    cotangent,
    buckets,
    bias_table,
    attn_gain,
    w_query,
    w_key,
    w_value,
    w_output,
    ffn_gain,
    w_gate,
    w_up,
    w_down,
):
    length = tokens.shape[0]
    bucket_count = bias_table.shape[0]
    head_count = bias_table.shape[1]
    inner_width = w_query.shape[1]
    ff_width = w_gate.shape[1]
    owner_rows = w_query.shape[0]
    head_size = inner_width // head_count
    block_rows = min(512, length)
    block_count = length // block_rows
    residual = tokens.astype(jnp.float32)
    attn_set = (
        lax.all_gather(attn_gain, "shard", axis=0, tiled=True),
        lax.all_gather(w_query, "shard", axis=0, tiled=True),
        lax.all_gather(w_key, "shard", axis=0, tiled=True),
        lax.all_gather(w_value, "shard", axis=0, tiled=True),
        lax.all_gather(w_output, "shard", axis=0, tiled=True),
    )
    gain_one = attn_set[0].astype(jnp.float32)
    normed_one = norm_local(residual, gain_one).astype(jnp.bfloat16)

    def project(weight):
        product = jnp.dot(normed_one, weight, preferred_element_type=jnp.float32)
        return product.astype(jnp.bfloat16).reshape(length, head_count, head_size)

    queries = project(attn_set[1])
    key_rows = project(attn_set[2])
    value_rows = project(attn_set[3])
    one_hot = (buckets[:, None] == jnp.arange(bucket_count, dtype=jnp.int32)[None, :]).astype(
        jnp.float32
    )
    offset_bias = jnp.dot(one_hot, bias_table.astype(jnp.float32), precision=highest).T
    block_starts = jnp.arange(block_count, dtype=jnp.int32) * block_rows
    key_index = jnp.arange(length, dtype=jnp.int32)

    def block_scores(first_row, query_block):
        query_index = first_row + jnp.arange(block_rows, dtype=jnp.int32)
        bias_grid = toeplitz_grid(offset_bias, block_rows, length)
        scores = (
            jnp.einsum("qhd,khd->hqk", query_block, key_rows, preferred_element_type=jnp.float32)
            + bias_grid
        )
        allowed = key_index[None, :] // BLOCK <= query_index[:, None] // BLOCK
        return jnp.where(allowed[None], scores, masked_score)

    def attend(first_row):
        scores = block_scores(first_row, queries)
        row_max = jnp.max(scores, axis=-1, keepdims=True)
        exp_scores = jnp.exp(scores - row_max)
        totals = jnp.sum(exp_scores, axis=-1, keepdims=True)
        probability = (exp_scores / totals).astype(jnp.bfloat16)
        mixed_rows = jnp.einsum(
            "hqk,khd->qhd", probability, value_rows, preferred_element_type=jnp.float32
        )
        return (mixed_rows, (row_max + jnp.log(totals))[..., 0])

    mixed_blocks, log_totals = lax.map(attend, block_starts)
    attended = mixed_blocks.reshape(length, inner_width).astype(jnp.bfloat16)
    middle = residual + jnp.einsum(
        "ti,di->td", attended, attn_set[4], preferred_element_type=jnp.float32
    )
    ffn_set = (
        lax.all_gather(ffn_gain, "shard", axis=0, tiled=True),
        lax.all_gather(w_gate, "shard", axis=0, tiled=True),
        lax.all_gather(w_up, "shard", axis=0, tiled=True),
        lax.all_gather(w_down, "shard", axis=0, tiled=True),
    )
    gain_two = ffn_set[0].astype(jnp.float32)
    normed_two = norm_local(middle, gain_two).astype(jnp.bfloat16)
    gate_values = jnp.dot(normed_two, ffn_set[1], preferred_element_type=jnp.float32)
    up_values = jnp.dot(normed_two, ffn_set[2], preferred_element_type=jnp.float32)
    activated, gelu_pullback = jax.vjp(gelu_tanh, gate_values)
    hidden = (activated * up_values).astype(jnp.bfloat16)
    layer_out = (
        middle + jnp.einsum("tf,df->td", hidden, ffn_set[3], preferred_element_type=jnp.float32)
    ).astype(jnp.bfloat16)
    ffn_set = (
        lax.all_gather(ffn_gain, "shard", axis=0, tiled=True),
        lax.all_gather(w_gate, "shard", axis=0, tiled=True),
        lax.all_gather(w_up, "shard", axis=0, tiled=True),
        lax.all_gather(w_down, "shard", axis=0, tiled=True),
    )
    grad_w_down = jnp.einsum("td,tf->df", cotangent, hidden, preferred_element_type=jnp.float32)
    grad_hidden = jnp.dot(cotangent, ffn_set[3], preferred_element_type=jnp.float32)
    grad_gate = gelu_pullback(grad_hidden * up_values)[0].astype(jnp.bfloat16)
    grad_up = (grad_hidden * activated).astype(jnp.bfloat16)
    grad_w_gate = jnp.einsum("td,tf->df", normed_two, grad_gate, preferred_element_type=jnp.float32)
    grad_w_up = jnp.einsum("td,tf->df", normed_two, grad_up, preferred_element_type=jnp.float32)
    grad_normed_two = jnp.einsum(
        "tf,df->td", grad_gate, ffn_set[1], preferred_element_type=jnp.float32
    )
    grad_normed_two = grad_normed_two + jnp.einsum(
        "tf,df->td", grad_up, ffn_set[2], preferred_element_type=jnp.float32
    )
    middle_part, grad_gain_two = jax.vjp(norm_local, middle, gain_two)[1](grad_normed_two)
    grad_middle = cotangent.astype(jnp.float32) + middle_part
    ffn_shards = (
        lax.psum_scatter(grad_w_gate.astype(jnp.bfloat16), "shard", scatter_dimension=0, tiled=True),
        lax.psum_scatter(grad_w_up.astype(jnp.bfloat16), "shard", scatter_dimension=0, tiled=True),
        lax.psum_scatter(grad_w_down.astype(jnp.bfloat16), "shard", scatter_dimension=0, tiled=True),
    )
    attn_set = (
        lax.all_gather(attn_gain, "shard", axis=0, tiled=True),
        lax.all_gather(w_query, "shard", axis=0, tiled=True),
        lax.all_gather(w_key, "shard", axis=0, tiled=True),
        lax.all_gather(w_value, "shard", axis=0, tiled=True),
        lax.all_gather(w_output, "shard", axis=0, tiled=True),
    )
    grad_branch = grad_middle.astype(jnp.bfloat16)
    grad_w_output = jnp.einsum(
        "td,ti->di", grad_branch, attended, preferred_element_type=jnp.float32
    )
    grad_attended = jnp.einsum(
        "td,di->ti", grad_branch, attn_set[4], preferred_element_type=jnp.float32
    )
    grad_attended = grad_attended.astype(jnp.bfloat16).reshape(length, head_count, head_size)

    def attend_back(carried, block_input):
        grad_keys, grad_values, grad_offsets = carried
        first_row, log_total = block_input
        scores = block_scores(first_row, queries)
        probability = jnp.exp(scores - log_total[..., None])
        grad_probs = jnp.einsum(
            "qhd,khd->hqk", grad_attended, value_rows, preferred_element_type=jnp.float32
        )
        inner_sum = jnp.sum(probability * grad_probs, axis=-1, keepdims=True)
        grad_scores = (probability * (grad_probs - inner_sum)).astype(jnp.bfloat16)
        grad_values = grad_values + jnp.einsum(
            "hqk,qhd->khd",
            probability.astype(jnp.bfloat16),
            grad_attended,
            preferred_element_type=jnp.float32,
        )
        grad_keys = grad_keys + jnp.einsum(
            "hqk,qhd->khd", grad_scores, queries, preferred_element_type=jnp.float32
        )
        grad_queries = jnp.einsum(
            "hqk,khd->qhd", grad_scores, key_rows, preferred_element_type=jnp.float32
        )
        diagonal_sums = diagonal_total(grad_scores.astype(jnp.float32))
        offset_piece = grad_offsets
        grad_offsets = offset_piece + diagonal_sums
        return ((grad_keys, grad_values, grad_offsets), grad_queries)

    zero_rows = jnp.zeros((length, head_count, head_size), jnp.float32)
    zero_offsets = jnp.zeros((head_count, 2 * length - 1), jnp.float32)
    (grad_keys, grad_values, grad_offsets), query_blocks = lax.scan(
        attend_back, (zero_rows, zero_rows, zero_offsets), (block_starts, log_totals)
    )
    grad_queries = query_blocks.reshape(length, inner_width).astype(jnp.bfloat16)
    grad_keys = grad_keys.reshape(length, inner_width).astype(jnp.bfloat16)
    grad_values = grad_values.reshape(length, inner_width).astype(jnp.bfloat16)
    grad_w_query = jnp.einsum(
        "td,ti->di", normed_one, grad_queries, preferred_element_type=jnp.float32
    )
    grad_w_key = jnp.einsum("td,ti->di", normed_one, grad_keys, preferred_element_type=jnp.float32)
    grad_w_value = jnp.einsum(
        "td,ti->di", normed_one, grad_values, preferred_element_type=jnp.float32
    )
    grad_normed_one = jnp.einsum(
        "ti,di->td", grad_queries, attn_set[1], preferred_element_type=jnp.float32
    )
    grad_normed_one = grad_normed_one + jnp.einsum(
        "ti,di->td", grad_keys, attn_set[2], preferred_element_type=jnp.float32
    )
    grad_normed_one = grad_normed_one + jnp.einsum(
        "ti,di->td", grad_values, attn_set[3], preferred_element_type=jnp.float32
    )
    rows_part, grad_gain_one = jax.vjp(norm_local, residual, gain_one)[1](grad_normed_one)
    grad_tokens = (grad_middle + rows_part).astype(jnp.bfloat16)
    grad_table = jnp.dot(grad_offsets, one_hot, precision=highest).T
    owner_start = lax.axis_index("shard") * owner_rows
    attn_shards = (
        lax.psum_scatter(grad_w_query.astype(jnp.bfloat16), "shard", scatter_dimension=0, tiled=True),
        lax.psum_scatter(grad_w_key.astype(jnp.bfloat16), "shard", scatter_dimension=0, tiled=True),
        lax.psum_scatter(grad_w_value.astype(jnp.bfloat16), "shard", scatter_dimension=0, tiled=True),
        lax.psum_scatter(grad_w_output.astype(jnp.bfloat16), "shard", scatter_dimension=0, tiled=True),
    )
    summed = lax.psum(
        (
            attn_shards[0],
            attn_shards[1],
            attn_shards[2],
            attn_shards[3],
            ffn_shards[0],
            ffn_shards[1],
            ffn_shards[2],
        ),
        "rep",
    )
    small_total = lax.psum((grad_gain_one, grad_gain_two, grad_table), ("shard", "rep"))
    gain_one_own = lax.dynamic_slice_in_dim(small_total[0], owner_start, owner_rows, 0)
    gain_two_own = lax.dynamic_slice_in_dim(small_total[1], owner_start, owner_rows, 0)
    return (
        layer_out,
        grad_tokens,
        gain_one_own,
        summed[0].astype(jnp.float32),
        summed[1].astype(jnp.float32),
        summed[2].astype(jnp.float32),
        summed[3].astype(jnp.float32),
        gain_two_own,
        summed[4].astype(jnp.float32),
        summed[5].astype(jnp.float32),
        summed[6].astype(jnp.float32),
        small_total[2],
    )

HEAD_SLOTS = 7
TAIL_SLOTS = 12
HELPED = (1, 2, 4, 5)
SLOTS = {
    "send": (0, 0, 1, 2, 2, 4, 6),
    "forward": (1, 1, 5, 7, 8, 10, 16),
    "swap": (2, 3, 7, 10, 11, 12, 18),
    "get_forward": (2, 6, 11, 12, 14, 15, 18),
    "get_swap": (5, 6, 11, 12, 14, 16, 19),
    "turn": (10, 12, 15, 16, 18, 20, 23, 26, 28),
    "rep": (13, 15, 16, 18, 21, 22, 24, 28, 30),
    "mid": (15, 16, 18, 20, 22, 24, 25, 30, 31),
    "last": (16, 18, 20, 22, 24, 25, 28, 31, 32),
}


def dot_nn(a, b):
    return lax.dot_general(a, b, (((1,), (0,)), ((), ())), preferred_element_type=f32)


def dot_nt(a, b):
    return lax.dot_general(a, b, (((1,), (1,)), ((), ())), preferred_element_type=f32)


def dot_tn(a, b):
    return lax.dot_general(a, b, (((0,), (0,)), ((), ())), preferred_element_type=f32)


def fused_kernel(
    xt_ref,
    ct_ref,
    buckets_ref,
    table_ref,
    gains_ref,
    wq_ref,
    wk_ref,
    wv_ref,
    wo_ref,
    wg_ref,
    wu_ref,
    wd_ref,
    out_ref,
    gtok_ref,
    small_ref,
    gq_ref,
    gk_ref,
    gv_ref,
    go_ref,
    gg_ref,
    gu_ref,
    gd_ref,
    land_ref,
    sum_ref,
    hop_ref,
    turn_ref,
    gland,
    gcol,
    n1t,
    n2t,
    mid,
    acc_o,
    acc_n,
    qt,
    kt,
    vt,
    att,
    dat,
    dqt,
    dkt,
    dvt,
    wq,
    wk,
    wv,
    wo,
    wg2,
    wu2,
    wd2,
    wload,
    g,
    hid,
    dgt,
    dup,
    rc,
    stage_t,
    stage_v,
    vbuf,
    zi,
    zm,
    ubuf,
    revb,
    onehot,
    doff,
    sms,
    smr,
    gain_s,
    gain_r,
    gsend,
    gloc,
    g1r,
    g2r,
    gpr,
    load_sem,
    e0s,
    e0r,
    sum_sem,
    stage_sem,
    e1s,
    e1r,
    e2s,
    e2r,
    zis,
    zir,
    zms,
    zmr,
    us,
    ul,
    ur,
    sss,
    ssr,
    zcredit,
    *,
    chunks,
    heads,
):
    width = xt_ref.shape[0]
    toks = xt_ref.shape[1]
    rows = gains_ref.shape[0]
    fw = land_ref.shape[2]
    sub = fw // 3
    aw = wq_ref.shape[1]
    hs = aw // heads
    total = chunks + 2
    eps = 1e-06
    lanes = revb.shape[1]
    big = 2 * rows
    nbig = width // big

    s = lax.axis_index("shard")
    r = lax.axis_index("rep")
    c = s % 2
    x = (s // 2) % 2
    y = s // 4
    sc = s + 1 - 2 * c
    sx = s + 2 - 4 * x
    sy = s + 4 - 8 * y
    bx = sx - c
    by = sy - c
    bd = (1 - y) * 4 + (1 - x) * 2
    b_own = s - c
    mate = r + 1 - 2 * (r % 2)
    inner = (r == 1) | (r == 2)
    outer = (r == 0) | (r == 3)

    def remote(src, dst, ssem, rsem, dev):
        return pltpu.make_async_remote_copy(
            src_ref=src, dst_ref=dst, send_sem=ssem, recv_sem=rsem, device_id=dev, device_id_type=MESH
        )

    def settle(ref, sem):
        pltpu.make_async_copy(ref, ref, sem).wait()

    barrier = pltpu.get_barrier_semaphore()
    near = [(sc, r), (bx, r), (bx + 1, r), (by, r), (by + 1, r), (bd, r), (bd + 1, r), (s, mate), (sc, mate)]
    for dev in near:
        pl.semaphore_signal(barrier, inc=1, device_id=dev, device_id_type=MESH)

    @pl.when(inner)
    def _():
        pl.semaphore_signal(barrier, inc=1, device_id=(s, 3 - r), device_id_type=MESH)

    @pl.when(inner)
    def _():
        pl.semaphore_wait(barrier, len(near) + 1)

    @pl.when(outer)
    def _():
        pl.semaphore_wait(barrier, len(near))

    def place(chunk, index):
        kind, k = chunk
        if kind == "a":
            return g.at[16 + index, :, pl.ds(k * aw, aw)]
        return land_ref.at[k * 16 + index]

    def places(chunk, count):
        kind, k = chunk
        if kind == "a":
            return g.at[pl.ds(16, count), :, pl.ds(k * aw, aw)]
        return land_ref.at[pl.ds(0, count)]

    def any_of(value, options):
        return functools.reduce(jnp.logical_or, [value == option for option in options], jnp.bool_(False))

    def helped(chunk):
        kind, k = chunk
        return False if kind == "a" else any_of(k, HELPED)

    def active(chunk):
        kind, k = chunk
        return True if kind == "a" else jnp.logical_not(any_of(k, HELPED)) | (r % 2 == k % 2)

    def when(condition, then):
        if condition is True:
            then()
        elif condition is not False:
            pl.when(condition)(then)

    def columns(k, half):
        return pl.ds(pl.multiple_of((2 * k + half) * sub, sub), sub)

    def own_parts(chunk, half):
        kind, k = chunk
        dst = place(chunk, half * 8 + s)
        if kind == "a":
            return [(((wq_ref, wk_ref), (wv_ref, wo_ref))[k][half], dst)]
        return [
            (ref.at[:, columns(k, half)], dst.at[:, pl.ds(j * sub, sub)]) for j, ref in enumerate((wg_ref, wu_ref, wd_ref))
        ]

    def at(chunk):
        kind, k = chunk
        return k if kind == "a" else k + 2

    def gather_send(chunk):
        i = at(chunk)

        def cross():
            for half in (0, 1):
                for src, dst in own_parts(chunk, half):
                    remote(src, dst, gsend.at[i], g1r.at[i], (bx + half, r)).start()
                    remote(src, dst, gsend.at[i], g1r.at[i], (by + half, r)).start()

        when(active(chunk), cross)
        for half in (0, 1):
            for src, dst in own_parts(chunk, half):
                remote(src, dst, gsend.at[i], gpr.at[i], (sc, r)).start()
                pltpu.make_async_copy(src, dst, gloc.at[i]).start()

    def hand_over(chunk, blocks, sem):
        i = at(chunk)

        def hand():
            for b in blocks:
                spot = place(chunk, c * 8 + b)
                remote(spot, spot, gsend.at[i], sem.at[i], (s, mate)).start()

        if chunk[0] == "f":
            pl.when(helped(chunk) & active(chunk))(hand)
        for b in blocks:
            spot = place(chunk, c * 8 + b)
            remote(spot, spot, gsend.at[i], gpr.at[i], (sc, r)).start()

    def gather_forward(chunk):
        i = at(chunk)
        settle(places(chunk, 4), g1r.at[i])

        def cross():
            one = place(chunk, c * 8 + bx)
            two = place(chunk, c * 8 + by + 1)
            remote(one, one, gsend.at[i], g2r.at[i], (sy, r)).start()
            remote(two, two, gsend.at[i], g2r.at[i], (sx, r)).start()

        when(active(chunk), cross)
        hand_over(chunk, (bx, bx + 1, by, by + 1), g1r)

    def gather_swap(chunk):
        settle(places(chunk, 2), g2r.at[at(chunk)])
        hand_over(chunk, (bd, bd + 1), g2r)

    def gather_done(chunk):
        i = at(chunk)
        settle(places(chunk, 8), gpr.at[i])
        settle(places(chunk, 2), gloc.at[i])

    def gather_sent(chunk):
        i = at(chunk)
        does = active(chunk)
        if does is True:
            settle(places(chunk, 14), gsend.at[i])
            return
        pl.when(does & helped(chunk))(lambda: settle(places(chunk, 20), gsend.at[i]))
        pl.when(does & jnp.logical_not(helped(chunk)))(lambda: settle(places(chunk, 14), gsend.at[i]))
        pl.when(jnp.logical_not(does))(lambda: settle(places(chunk, 8), gsend.at[i]))

    def ahead(stage, k, mine):
        chunk = ("f", k)
        does = active(chunk) if mine else jnp.logical_not(active(chunk))
        pl.when((k < chunks) & does)(lambda: stage(chunk))

    def cut(ref, w):
        return ref if w == fw else ref.at[:, :, pl.ds(0, w)]

    def cut1(ref, index, w):
        return ref.at[index] if w == fw else ref.at[index, :, pl.ds(0, w)]

    def span(ref, start, count, w):
        return ref.at[pl.ds(start, count)] if w == fw else ref.at[pl.ds(start, count), :, pl.ds(0, w)]

    def get(ref, index, w):
        return ref[index] if w == fw else ref[index, :, 0:w]

    def put(ref, index, w, value):
        if w == fw:
            ref[index] = value
        else:
            ref[index, :, 0:w] = value

    def add_to(dst, i, src, j, w):
        value = get(dst, i, w).astype(f32) + get(src, j, w).astype(f32)
        put(dst, i, w, value.astype(bf16))

    def core_part(n, b, count, w):
        slot = n % 2
        remote(
            span(g, slot * 16 + (1 - c) * 8 + b, count, w), span(rc, slot * 8 + b, count, w), e0s.at[n], e0r.at[n], (sc, r)
        ).start()

    def plane_send(n, w):
        slot = n % 2
        base = slot * 16 + c * 8
        settle(span(rc, slot * 8, 8, w), e0r.at[n])
        order = []
        for k, kx, ky in ((0, 1 - y, 1 - x), (1, y, x)):
            order.append((4 * kx + 2 * (1 - x), sx, 2 * k))
            order.append((4 * (1 - y) + 2 * ky + 1, sy, 2 * k + 1))
        order += [(b, None, None) for b in (4 * (1 - y) + 2 * x, 4 * y + 2 * (1 - x) + 1, b_own, b_own + 1)]

        def store(i):
            b = order[i][0]
            return pltpu.make_async_copy(cut1(g, base + b, w), cut1(sum_ref, n * 8 + b, w), sum_sem.at[i])

        for i, (b, _, _) in enumerate(order):
            add_to(g, base + b, rc, slot * 8 + b, w)
            store(i).start()
        for i, (b, dev, spot) in enumerate(order):
            store(i).wait()
            if dev is not None:
                remote(
                    cut1(sum_ref, n * 8 + b, w), cut1(hop_ref, n * 4 + spot, w), e1s.at[n], e1r.at[n, spot // 2], (dev, r)
                ).start()

    def slot_free(n):
        settle(span(g, 0, 8, width_of(n)), e0s.at[n])

    def turn_free(n):
        settle(span(turn_ref, 0, 2, width_of(n)), e2s.at[n])

    def guarded(n, least, then):
        if isinstance(n, int):
            if n >= least:
                then()
        else:
            pl.when(n >= least)(then)

    def turn_loads(n, w):
        base = (n % 2) * 4
        first = n * 8 + 4 * (1 - y) + 2 * x
        second = n * 8 + 4 * y + 2 * (1 - x) + 1
        return [
            pltpu.make_async_copy(cut1(sum_ref, first, w), cut1(stage_t, base, w), stage_sem.at[0]),
            pltpu.make_async_copy(cut1(sum_ref, second, w), cut1(stage_t, base + 1, w), stage_sem.at[1]),
            pltpu.make_async_copy(span(hop_ref, n * 4, 2, w), span(stage_t, base + 2, 2, w), stage_sem.at[2]),
        ]

    def turn_start(n, w):
        guarded(n, 2, lambda: turn_free(n - 2))
        settle(span(hop_ref, 0, 2, w), e1r.at[n, 0])
        for load in turn_loads(n, w):
            load.start()

    def turn_end(n, w):
        base = (n % 2) * 4
        for load in turn_loads(n, w):
            load.wait()
        for j, dev in ((0, sy), (1, sx)):
            add_to(stage_t, base + j, stage_t, base + 2 + j, w)
            remote(cut1(stage_t, base + j, w), cut1(turn_ref, n * 2 + j, w), e2s.at[n], e2r.at[n], (dev, r)).start()

    def rep_loads(n, w):
        return [
            pltpu.make_async_copy(span(sum_ref, n * 8 + b_own, 2, w), span(stage_v, 0, 2, w), stage_sem.at[3]),
            pltpu.make_async_copy(span(hop_ref, n * 4 + 2, 2, w), span(stage_v, 2, 2, w), stage_sem.at[4]),
            pltpu.make_async_copy(span(turn_ref, n * 2, 2, w), span(stage_v, 4, 2, w), stage_sem.at[5]),
        ]

    def rep_start(n, w):
        settle(span(hop_ref, 0, 2, w), e1r.at[n, 1])
        settle(span(turn_ref, 0, 2, w), e2r.at[n])
        for load in rep_loads(n, w):
            load.start()

    def rep_end(n, w):
        slot = n % 2
        if isinstance(n, int):
            if n >= 2:
                pl.when(outer)(functools.partial(rep_free, n))
        else:
            pl.when(outer & (n >= 2))(functools.partial(rep_free, n))
        for load in rep_loads(n, w):
            load.wait()
        for j in (0, 1):
            value = get(stage_v, j, w).astype(f32) + get(stage_v, 2 + j, w).astype(f32)
            value = value + get(stage_v, 4 + j, w).astype(f32)
            put(vbuf, slot * 2 + j, w, value.astype(bf16))

        @pl.when(outer)
        def _():
            remote(
                span(vbuf, slot * 2, 2, w), span(zi, slot * 2, 2, w), zis.at[n], zir.at[n], (s, mate)
            ).start()

    def width_of(n):
        return fw if not isinstance(n, int) or n < chunks else aw

    def rep_free(n):
        earlier = n - 2
        slot = n % 2
        settle(span(vbuf, slot * 2, 2, width_of(earlier)), zis.at[earlier])
        pl.semaphore_wait(zcredit, 1)

    def rep_turn(n, w):
        slot = n % 2

        @pl.when(inner)
        def _():
            settle(span(zi, slot * 2, 2, w), zir.at[n])
            for j in (0, 1):
                add_to(vbuf, slot * 2 + j, zi, slot * 2 + j, w)

            def credit():
                pl.semaphore_signal(zcredit, inc=1, device_id=(s, mate), device_id_type=MESH)

            if isinstance(n, int):
                if n + 2 < total:
                    credit()
            else:
                credit()
            remote(
                span(vbuf, slot * 2, 2, w), span(zm, slot * 2, 2, w), zms.at[n], zmr.at[n], (s, 3 - r)
            ).start()

    def result(n, half, block):
        if isinstance(n, int) and n >= chunks:
            return [(block, ((gv_ref, go_ref), (gq_ref, gk_ref))[n - chunks][half])]
        return [
            (block.at[:, pl.ds(j * sub, sub)], ref.at[:, columns(n, half)])
            for j, ref in enumerate((gg_ref, gu_ref, gd_ref))
        ]

    def u_free(n, w):
        slot = n % 2
        for k in (0, 1, 2):
            settle(cut1(ubuf, slot * 2, w), us.at[n, k])
        settle(cut1(ubuf, slot * 2, w), ul.at[n])

    def rep_last(n, w):
        slot = n % 2

        @pl.when(inner)
        def _():
            settle(span(zm, slot * 2, 2, w), zmr.at[n])
            if isinstance(n, int):
                if n >= 2:
                    u_free(n - 2, width_of(n - 2))
            else:
                pl.when(n >= 2)(lambda: u_free(n - 2, w))
            for j in (0, 1):
                value = get(vbuf, slot * 2 + j, w).astype(f32) + get(zm, slot * 2 + j, w).astype(f32)
                put(ubuf, slot * 2 + j, w, value.astype(bf16))
            keep = cut1(ubuf, slot * 2 + c, w)
            give = cut1(ubuf, slot * 2 + 1 - c, w)

            def finish(half):
                for src, dst in result(n, half, keep):
                    remote(src, dst, us.at[n, 0], ur.at[n, half], (s, mate)).start()
                    pltpu.make_async_copy(src, dst, ul.at[n]).start()
                for src, dst in result(n, half, give):
                    remote(src, dst, us.at[n, 1], ur.at[n, half], (sc, mate)).start()
                    remote(src, dst, us.at[n, 2], ur.at[n, half], (sc, r)).start()

            if w == fw:
                finish(c)
            else:
                pl.when(c == 0)(lambda: finish(0))
                pl.when(c == 1)(lambda: finish(1))
            settle(span(vbuf, slot * 2, 2, w), zms.at[n])

    def gathers(stage, mine):
        return lambda k: ahead(stage, k, mine)

    def reduces(stage):
        return lambda n: stage(n, width_of(n))

    order = (
        ("swap", gathers(gather_swap, True)),
        ("forward", gathers(gather_forward, True)),
        ("send", lambda k: gather_send(("f", k))),
        ("turn", reduces(turn_start)),
        ("last", reduces(rep_last)),
        ("mid", reduces(rep_turn)),
        ("turn", reduces(turn_end)),
        ("rep", reduces(rep_start)),
        ("get_forward", gathers(gather_forward, False)),
        ("get_swap", gathers(gather_swap, False)),
        ("rep", reduces(rep_end)),
    )
    loop_at = HEAD_SLOTS
    tail_at = HEAD_SLOTS + 2 * chunks

    def do(slot):
        for name, stage in order:
            for n, spot in enumerate(SLOTS[name]):
                if spot == slot:
                    stage(n)

    def do_in_loop(t, side):
        for name, stage in order:
            pairs = [
                ((spot - loop_at) // 2, n)
                for n, spot in enumerate(SLOTS[name])
                if loop_at <= spot < tail_at and (spot - loop_at) % 2 == side
            ]
            if pairs:
                n = sum([jnp.where(t == step, number, 0) for step, number in pairs], jnp.int32(0))
                pl.when(any_of(t, [step for step, _ in pairs]))(functools.partial(stage, n))

    def small_send(step):
        if step < 3:
            dev = ((sc, r), (sx, r), (sy, r))[step]
            remote(sms.at[step], smr.at[step], sss.at[step], ssr.at[step], dev).start()
        elif step == 3:

            @pl.when(outer)
            def _():
                remote(sms.at[3], smr.at[3], sss.at[3], ssr.at[3], (s, mate)).start()
        elif step == 4:

            @pl.when(inner)
            def _():
                remote(sms.at[4], smr.at[4], sss.at[4], ssr.at[4], (s, 3 - r)).start()
        else:

            @pl.when(inner)
            def _():
                remote(sms.at[5], smr.at[5], sss.at[5], ssr.at[5], (s, mate)).start()

    def small_step(step):
        def take():
            settle(smr.at[step], ssr.at[step])
            settle(sms.at[step], sss.at[step])
            if step < 2:
                sms[step + 1] = sms[step] + smr[step]
            elif step == 2:
                sms[3] = sms[2] + smr[2]

        if step < 3:
            take()
            small_send(step + 1)
        elif step == 3:

            @pl.when(inner)
            def _():
                settle(smr.at[3], ssr.at[3])
                sms[4] = sms[3] + smr[3]

            @pl.when(outer)
            def _():
                settle(sms.at[3], sss.at[3])

            small_send(4)
        elif step == 4:

            @pl.when(inner)
            def _():
                settle(smr.at[4], ssr.at[4])
                settle(sms.at[4], sss.at[4])
                sms[5] = sms[4] + smr[4]
                small_ref[...] = sms[5]

            small_send(5)
        else:

            @pl.when(inner)
            def _():
                settle(sms.at[5], sss.at[5])

            @pl.when(outer)
            def _():
                settle(smr.at[5], ssr.at[5])
                small_ref[...] = smr[5]

    tile = 64
    tiles = width // tile

    def over_rows(body, start):
        def step(i, carry):
            return body(pl.ds(pl.multiple_of(i * tile, tile), tile), carry)

        return lax.fori_loop(0, tiles, step, start)

    def fold(value):
        return jnp.sum(value.reshape(tile // 8, 8, toks), axis=0)

    zero8 = jnp.zeros((8, toks), f32)

    gather_send(("a", 0))
    gdst = gland.at[s]
    for k, dev in enumerate([(sc, r), (bx, r), (bx + 1, r), (by, r), (by + 1, r), (bd, r), (bd + 1, r)]):
        remote(gains_ref, gdst, gain_s, gain_r, dev).start()
    pltpu.make_async_copy(gains_ref, gdst, load_sem.at[1]).start()
    gather_send(("a", 1))
    do(0)

    def square_sum(sl, acc):
        v = xt_ref[sl, :].astype(f32)
        return acc + fold(v * v)

    ssum = jnp.sum(over_rows(square_sum, zero8), axis=0, keepdims=True)
    r1 = lax.rsqrt(ssum * (1.0 / width) + eps)

    bucket_index = lax.broadcasted_iota(jnp.int32, (table_ref.shape[1], lanes), 0)
    rev_hot = (bucket_index == buckets_ref[0:1, :]).astype(bf16)
    onehot[...] = (bucket_index == buckets_ref[1:2, :]).astype(bf16)
    revb[...] = dot_nn(table_ref[...], rev_hot)

    settle(gland.at[pl.ds(0, 7)], gain_r)
    settle(gland.at[0], load_sem.at[1])
    for b in range(8):
        gcol[rows * b : rows * (b + 1), :] = gland[b].astype(f32)

    def norm_one(sl, carry):
        v = xt_ref[sl, :].astype(f32)
        n1t[sl, :] = (v * r1 * gcol[sl, 0:1]).astype(bf16)
        return carry

    gather_forward(("a", 0))
    do(1)
    over_rows(norm_one, 0)
    gather_swap(("a", 0))
    gather_forward(("a", 1))
    do(2)

    def compact(dst, half, col):
        @pl.loop(0, nbig)
        def _(i):
            both = jnp.concatenate(
                [
                    g[16 + half * 8 + 2 * i, :, col : col + aw].astype(f32),
                    g[16 + half * 8 + 2 * i + 1, :, col : col + aw].astype(f32),
                ],
                axis=0,
            )
            dst[pl.ds(pl.multiple_of(i * 2 * rows, 16), 2 * rows), :] = both.astype(bf16)

    gather_done(("a", 0))
    compact(wq, 0, 0)
    qt[...] = dot_tn(wq[...], n1t[...]).astype(bf16)
    compact(wk, 1, 0)
    kt[...] = dot_tn(wk[...], n1t[...]).astype(bf16)
    gather_swap(("a", 1))
    do(3)
    gather_done(("a", 1))
    compact(wv, 0, aw)
    vt[...] = dot_tn(wv[...], n1t[...]).astype(bf16)
    compact(wo, 1, aw)
    do(4)

    half_tok = toks // 2

    def softmax_block(h, head, block):
        keys = half_tok * (block + 1)
        low = half_tok * block
        row = jnp.broadcast_to(revb[pl.ds(h, 1), :], (half_tok, lanes))
        bias = pltpu.roll(row, (low + 1 - toks) % lanes, 1, stride=1, stride_axis=0)[:, :keys]
        scores = dot_tn(qt[head, low : low + half_tok], kt[head, 0:keys]) + bias
        e = jnp.exp(scores - jnp.max(scores, axis=1, keepdims=True))
        return e * (1.0 / jnp.sum(e, axis=1, keepdims=True)), low, keys

    def attend(h, carry):
        head = pl.ds(pl.multiple_of(h * hs, hs), hs)
        for block in (0, 1):
            p, low, keys = softmax_block(h, head, block)
            att[head, low : low + half_tok] = dot_nt(vt[head, 0:keys], p.astype(bf16)).astype(bf16)
        return carry

    lax.fori_loop(0, heads // 2, attend, 0)
    do(5)
    lax.fori_loop(heads // 2, heads, attend, 0)
    do(6)

    def branch_one(i, acc):
        sl = pl.ds(pl.multiple_of(i * big, 16), big)
        m = xt_ref[sl, :].astype(f32) + dot_nn(wo[sl, :], att[...])
        mid[sl, :] = m
        return acc + jnp.sum((m * m).reshape(big // 8, 8, toks), axis=0)

    ssum = jnp.sum(lax.fori_loop(0, nbig, branch_one, zero8), axis=0, keepdims=True)
    r2n = lax.rsqrt(ssum * (1.0 / width) + eps)

    def norm_two(sl, carry):
        m = mid[sl, :]
        n2t[sl, :] = (m * r2n * gcol[sl, 1:2]).astype(bf16)
        acc_o[sl, :] = m
        acc_n[sl, :] = jnp.zeros((tile, toks), f32)
        return carry

    over_rows(norm_two, 0)

    tok_tile = toks // 2

    def ffn_chunk(t):
        slot = t % 2
        parts = [(half, k) for half in (0, 1) for k in (0, 1, 2)]

        def load(p):
            half, k = parts[p]
            return pltpu.make_async_copy(
                land_ref.at[pl.ds(t * 16 + half * 8, 8), :, pl.ds(k * sub, sub)],
                wload.at[pl.ds((p % 2) * 8, 8)],
                load_sem.at[p % 2],
            )

        load(0).start()
        for p, (half, k) in enumerate(parts):
            if p + 1 < len(parts):
                load(p + 1).start()
            load(p).wait()
            dst = (wg2, wu2, wd2)[k]

            @pl.loop(0, nbig)
            def _(i):
                base = (p % 2) * 8 + 2 * i
                both = jnp.concatenate([wload[base].astype(f32), wload[base + 1].astype(f32)], axis=0)
                sl = pl.ds(pl.multiple_of(i * big, 16), big)
                dst[sl, half * sub : (half + 1) * sub] = both.astype(bf16)

        @pl.loop(0, toks // tok_tile)
        def _(m):
            sl = pl.ds(pl.multiple_of(m * tok_tile, tok_tile), tok_tile)
            gate = dot_tn(n2t[:, sl], wg2[...])
            up = dot_tn(n2t[:, sl], wu2[...])
            gh = dot_tn(ct_ref[:, sl], wd2[...])
            k0 = 0.7978845608028654
            k1 = 0.044715
            sq = gate * gate
            th = jnp.tanh(k0 * (gate + k1 * (sq * gate)))
            half_one = 0.5 * (1.0 + th)
            act = gate * half_one
            slope = half_one + 0.5 * gate * (1.0 - th * th) * (k0 * (1.0 + 3.0 * k1 * sq))
            hid[sl, :] = (act * up).astype(bf16)
            dgt[sl, :] = (gh * up * slope).astype(bf16)
            dup[sl, :] = (gh * act).astype(bf16)

        @pl.loop(0, nbig)
        def _(i):
            sl = pl.ds(pl.multiple_of(i * big, 16), big)
            acc_o[sl, :] += dot_nt(wd2[sl, :], hid[...])
            acc_n[sl, :] += dot_nt(wg2[sl, :], dgt[...]) + dot_nt(wu2[sl, :], dup[...])
            for k, value in enumerate(
                (dot_nn(n2t[sl, :], dgt[...]), dot_nn(n2t[sl, :], dup[...]), dot_nn(ct_ref[sl, :], hid[...]))
            ):
                for half in (0, 1):
                    for j in (0, 1):
                        g[slot * 16 + half * 8 + 2 * i + j, :, k * sub : (k + 1) * sub] = value[
                            rows * j : rows * (j + 1), half * sub : (half + 1) * sub
                        ].astype(bf16)
            core_part(t, 2 * i, 2, fw)

    def ffn_step(t, carry):
        do_in_loop(t, 0)
        pl.when(t >= 2)(lambda: slot_free(t - 2))
        gather_done(("f", t))
        ffn_chunk(t)
        do_in_loop(t, 1)
        plane_send(t, fw)
        return carry

    gather_sent(("a", 0))
    gather_sent(("a", 1))
    lax.fori_loop(0, chunks, ffn_step, 0)

    nv = chunks
    nq = chunks + 1
    do(tail_at)
    pick = lax.broadcasted_iota(jnp.int32, (8, toks), 0)

    def token_sums(row):
        chosen = (pick == row).astype(bf16)
        return dot_nt(chosen, wg2[...]) + dot_nt(chosen, wu2[...])

    def second_mean(sl, acc):
        return acc + fold(gcol[sl, 1:2] * acc_n[sl, :] * mid[sl, :])

    back = jnp.sum(over_rows(second_mean, zero8), axis=0, keepdims=True) * (1.0 / width)
    back = back * (r2n * r2n * r2n)

    def second_norm(sl, carry):
        m = mid[sl, :]
        gn = acc_n[sl, :]
        out_ref[sl, :] = acc_o[sl, :].astype(bf16)
        v = gn * m * r2n
        hi = v.astype(bf16)
        wg2[sl, :] = hi
        wu2[sl, :] = (v - hi.astype(f32)).astype(bf16)
        gm = ct_ref[sl, :].astype(f32) + r2n * gcol[sl, 1:2] * gn - m * back
        acc_n[sl, :] = gm
        n2t[sl, :] = gm.astype(bf16)
        return carry

    over_rows(second_norm, 0)
    sms[0] = jnp.zeros(sms.shape[1:], f32)
    sms[0, :, 0:width] = token_sums(1)
    do(tail_at + 1)

    dat[...] = dot_tn(wo[...], n2t[...]).astype(bf16)

    def weight_grad(n, half, left, right):
        @pl.loop(0, nbig)
        def _(i):
            sl = pl.ds(pl.multiple_of(i * big, 16), big)
            value = dot_nt(left[sl, :], right[...])
            for j in (0, 1):
                g[(n % 2) * 16 + half * 8 + 2 * i + j, :, 0:aw] = value[rows * j : rows * (j + 1), :].astype(bf16)

    slot_free(5)
    weight_grad(nv, 1, n2t, att)
    do(tail_at + 2)
    flip = (
        lax.broadcasted_iota(jnp.int32, (toks, toks), 0) + lax.broadcasted_iota(jnp.int32, (toks, toks), 1)
        == toks - 1
    )
    hid[...] = flip.astype(bf16)
    doff[...] = jnp.zeros(doff.shape, f32)

    def attend_back(h, carry):
        head = pl.ds(pl.multiple_of(h * hs, hs), hs)
        grad_v = []
        grad_k = []
        offsets = jnp.zeros((1, lanes), f32)
        for block in (0, 1):
            p, low, keys = softmax_block(h, head, block)
            q_rows = qt[head, low : low + half_tok]
            a_rows = dat[head, low : low + half_tok]
            grad_p = dot_tn(a_rows, vt[head, 0:keys])
            ds = (p * (grad_p - jnp.sum(p * grad_p, axis=1, keepdims=True))).astype(bf16)
            grad_v.append(dot_nn(a_rows, p.astype(bf16)))
            grad_k.append(dot_nn(q_rows, ds))
            dqt[head, low : low + half_tok] = dot_nt(kt[head, 0:keys], ds).astype(bf16)
            turned = dot_nn(ds, hid[0:keys, toks - keys : toks])
            padded = jnp.concatenate([turned, jnp.zeros((half_tok, lanes - keys), f32)], axis=1)
            lined = pltpu.roll(padded, half_tok, 1, stride=1, stride_axis=0)
            offsets = offsets + jnp.sum(lined, axis=0, keepdims=True)
        for dst, parts in ((dvt, grad_v), (dkt, grad_k)):
            dst[head, 0:half_tok] = (parts[0] + parts[1][:, 0:half_tok]).astype(bf16)
            dst[head, half_tok:toks] = parts[1][:, half_tok:toks].astype(bf16)
        doff[pl.ds(h, 1), :] = offsets
        return carry

    lax.fori_loop(0, heads // 2, attend_back, 0)
    do(tail_at + 3)
    lax.fori_loop(heads // 2, heads, attend_back, 0)
    weight_grad(nv, 0, n1t, dvt)
    core_part(nv, 0, 8, aw)
    slot_free(6)
    weight_grad(nq, 0, n1t, dqt)
    weight_grad(nq, 1, n1t, dkt)
    plane_send(nv, aw)
    core_part(nq, 0, 8, aw)
    do(tail_at + 4)
    plane_send(nq, aw)
    do(tail_at + 5)

    def first_back(i, acc):
        sl = pl.ds(pl.multiple_of(i * big, 16), big)
        gn = dot_nn(wq[sl, :], dqt[...]) + dot_nn(wk[sl, :], dkt[...]) + dot_nn(wv[sl, :], dvt[...])
        acc_o[sl, :] = gn
        v = gcol[sl, 0:1] * gn * xt_ref[sl, :].astype(f32)
        return acc + jnp.sum(v.reshape(big // 8, 8, toks), axis=0)

    back = jnp.sum(lax.fori_loop(0, nbig, first_back, zero8), axis=0, keepdims=True) * (1.0 / width)
    back = back * (r1 * r1 * r1)
    do(tail_at + 6)

    def first_norm(sl, carry):
        v = xt_ref[sl, :].astype(f32)
        gn = acc_o[sl, :]
        prod = gn * v * r1
        hi = prod.astype(bf16)
        wg2[sl, :] = hi
        wu2[sl, :] = (prod - hi.astype(f32)).astype(bf16)
        gtok_ref[sl, :] = (acc_n[sl, :] + r1 * gcol[sl, 0:1] * gn - v * back).astype(bf16)
        return carry

    over_rows(first_norm, 0)
    sms[0, :, 0:width] += token_sums(0)
    rest = doff[...]
    table = jnp.zeros((8, onehot.shape[0]), f32)
    for _ in range(3):
        part = rest.astype(bf16)
        table = table + dot_nt(part, onehot[...])
        rest = rest - part.astype(f32)
    sms[0, :, sms.shape[2] - onehot.shape[0] : sms.shape[2]] = table
    small_send(0)
    for k in range(7, TAIL_SLOTS):
        do(tail_at + k)
        for step in {7: (0,), 8: (1,), 9: (2, 3), 10: (4, 5)}.get(k, ()):
            small_step(step)

    settle(gland.at[pl.ds(0, 7)], gain_s)
    slot_free(nv)
    slot_free(nq)
    turn_free(nv)
    turn_free(nq)
    for n in range(total):
        settle(span(hop_ref, 0, 4, width_of(n)), e1s.at[n])
    lax.fori_loop(0, chunks, lambda k, carry: (gather_sent(("f", k)), carry)[1], 0)

    @pl.when(outer)
    def _():
        for n in (nv, nq):
            settle(span(vbuf, (n % 2) * 2, 2, aw), zis.at[n])
        for n in range(total):
            for half in (0, 1):
                settle(cut1(ubuf, 0, width_of(n)), ur.at[n, half])

    @pl.when(inner)
    def _():
        for n in (nv, nq):
            u_free(n, aw)
        for n in range(total):
            settle(cut1(ubuf, 0, width_of(n)), ur.at[n, 1 - c])


def fused(tokens, cotangent, buckets, bias_table, gains, weights):
    toks, width = tokens.shape
    heads = bias_table.shape[1]
    rows, aw = weights[0].shape
    ff = weights[4].shape[1]
    sub = 256
    fw = 3 * sub
    chunks = ff // (2 * sub)
    total = chunks + 2
    lanes = 2 * toks
    small_lanes = (width + 127) // 128 * 128 + 128
    padded = jnp.concatenate([buckets, jnp.full((1,), -1, jnp.int32)])
    turned = jnp.concatenate([buckets[::-1], jnp.full((1,), -1, jnp.int32)])
    bucket_rows = jnp.concatenate([turned[None], padded[None], jnp.full((6, lanes), -1, jnp.int32)])
    table = jnp.pad(bias_table.T, ((0, 8 - heads), (0, 128 - bias_table.shape[0])))
    vm = pl.BlockSpec(memory_space=pltpu.VMEM)
    hbm = pl.BlockSpec(memory_space=pltpu.HBM)
    dma = pltpu.SemaphoreType.DMA
    tok = lambda kind: pltpu.VMEM((width, toks), kind)
    inner_rows = pltpu.VMEM((aw, toks), bf16)
    blocks = lambda count: pltpu.VMEM((count, rows, fw), bf16)
    return pl.pallas_call(
        functools.partial(fused_kernel, chunks=chunks, heads=heads),
        out_shape=(
            jax.ShapeDtypeStruct((width, toks), bf16),
            jax.ShapeDtypeStruct((width, toks), bf16),
            jax.ShapeDtypeStruct((8, small_lanes), f32),
            *([jax.ShapeDtypeStruct((rows, aw), bf16)] * 4),
            *([jax.ShapeDtypeStruct((rows, ff), bf16)] * 3),
            jax.ShapeDtypeStruct((chunks * 16, rows, fw), bf16),
            jax.ShapeDtypeStruct((total * 8, rows, fw), bf16),
            jax.ShapeDtypeStruct((total * 4, rows, fw), bf16),
            jax.ShapeDtypeStruct((total * 2, rows, fw), bf16),
        ),
        in_specs=[vm] * 5 + [hbm] * 7,
        out_specs=[vm] * 3 + [hbm] * 11,
        scratch_shapes=[
            pltpu.VMEM((8, rows, 128), bf16),
            pltpu.VMEM((width, 128), f32),
            tok(bf16),
            tok(bf16),
            tok(f32),
            tok(f32),
            tok(f32),
            *([inner_rows] * 8),
            *([pltpu.VMEM((width, aw), bf16)] * 4),
            *([pltpu.VMEM((width, 2 * sub), bf16)] * 3),
            pltpu.VMEM((16, rows, sub), bf16),
            blocks(32),
            *([pltpu.VMEM((toks, 2 * sub), bf16)] * 3),
            blocks(16),
            blocks(8),
            blocks(6),
            *([blocks(4)] * 4),
            pltpu.VMEM((8, lanes), f32),
            pltpu.VMEM((128, lanes), bf16),
            pltpu.VMEM((8, lanes), f32),
            pltpu.VMEM((6, 8, small_lanes), f32),
            pltpu.VMEM((6, 8, small_lanes), f32),
            dma(()),
            dma(()),
            *([dma((total,))] * 5),
            dma((2,)),
            *([dma((total,))] * 2),
            dma((8,)),
            dma((6,)),
            dma((total,)),
            dma((total, 2)),
            *([dma((total,))] * 6),
            dma((total, 3)),
            dma((total,)),
            dma((total, 2)),
            dma((6,)),
            dma((6,)),
            pltpu.SemaphoreType.REGULAR,
        ],
        compiler_params=pltpu.CompilerParams(
            collective_id=0, has_side_effects=True, vmem_limit_bytes=60 * 2**20
        ),
        cost_estimate=pl.CostEstimate(flops=57 * 10**9, bytes_accessed=10**8, transcendentals=10**7),
    )(tokens.T, cotangent.T, bucket_rows, table, gains, *weights)


def fused_body(
    tokens,
    cotangent,
    buckets,
    bias_table,
    attn_gain,
    w_query,
    w_key,
    w_value,
    w_output,
    ffn_gain,
    w_gate,
    w_up,
    w_down,
):
    rows = w_query.shape[0]
    gains = jnp.pad(jnp.stack([attn_gain, ffn_gain], axis=1), ((0, 0), (0, 126)))
    weights = (w_query, w_key, w_value, w_output, w_gate, w_up, w_down)
    out, gtok, small, *grads = fused(tokens, cotangent, buckets, bias_table, gains, weights)
    grads = [grad.astype(f32) for grad in grads[:7]]
    own = lax.dynamic_slice(small, (0, lax.axis_index("shard") * rows), (2, rows))
    table = small[0 : bias_table.shape[1], small.shape[1] - 128 :][:, 0 : bias_table.shape[0]].T
    return (out.T, gtok.T, own[0], *grads[:4], own[1], *grads[4:], table)


def solution(mesh):
    chosen = body
    if mesh.shape["shard"] == 8 and mesh.shape["rep"] == 4:
        chosen = fused_body
    return jax.shard_map(
        chosen,
        mesh=mesh,
        in_specs=(
            P(("shard", "rep"), None),
            P(("shard", "rep"), None),
            P(),
            P(),
            P("shard"),
            P("shard", None),
            P("shard", None),
            P("shard", None),
            P("shard", None),
            P("shard"),
            P("shard", None),
            P("shard", None),
            P("shard", None),
        ),
        out_specs=(
            P(("shard", "rep"), None),
            P(("shard", "rep"), None),
            P("shard"),
            P("shard", None),
            P("shard", None),
            P("shard", None),
            P("shard", None),
            P("shard"),
            P("shard", None),
            P("shard", None),
            P("shard", None),
            P(),
        ),
        check_vma=False,
    )
```

```python
import functools

import jax
import jax.numpy as jnp
from jax import lax
from jax.experimental import pallas as pl
from jax.experimental.pallas import tpu as pltpu
from jax.sharding import PartitionSpec as P

BLOCK = 256
MESH = pl.DeviceIdType.MESH
f32 = jnp.float32
bf16 = jnp.bfloat16


norm_eps = 1e-06
masked_score = -1e30
highest = lax.Precision.HIGHEST


def norm_local(row_values, gain_vector):
    return (
        row_values
        * lax.rsqrt(jnp.mean(row_values * row_values, axis=-1, keepdims=True) + norm_eps)
        * gain_vector
    )


def gelu_tanh(values_in):
    return jax.nn.gelu(values_in, approximate=True)


def diagonal_total(matrix):
    head_count, row_count, key_count = matrix.shape
    flipped = matrix[:, :, ::-1]
    padded = jnp.concatenate(
        [flipped, jnp.zeros((head_count, row_count, row_count), jnp.float32)], axis=2
    )
    flat_rows = padded.reshape(head_count, row_count * (key_count + row_count))
    flat_rows = flat_rows[:, : row_count * (key_count + row_count - 1)]
    return jnp.sum(flat_rows.reshape(head_count, row_count, key_count + row_count - 1), axis=1)


def toeplitz_grid(offset_bias, row_count, length):
    head_count = offset_bias.shape[0]
    span = length + row_count - 1
    flipped = offset_bias[:, ::-1]
    rotated = jnp.concatenate([flipped[:, row_count - 1 :], flipped[:, : row_count - 1]], axis=1)
    tiled = jnp.tile(rotated, (1, row_count))[:, : row_count * (span - 1)]
    return tiled.reshape(head_count, row_count, span - 1)[:, :, :length]


def body(
    tokens,
    cotangent,
    buckets,
    bias_table,
    attn_gain,
    w_query,
    w_key,
    w_value,
    w_output,
    ffn_gain,
    w_gate,
    w_up,
    w_down,
):
    length = tokens.shape[0]
    bucket_count = bias_table.shape[0]
    head_count = bias_table.shape[1]
    inner_width = w_query.shape[1]
    ff_width = w_gate.shape[1]
    owner_rows = w_query.shape[0]
    head_size = inner_width // head_count
    block_rows = min(512, length)
    block_count = length // block_rows
    residual = tokens.astype(jnp.float32)
    attn_set = (
        lax.all_gather(attn_gain, "shard", axis=0, tiled=True),
        lax.all_gather(w_query, "shard", axis=0, tiled=True),
        lax.all_gather(w_key, "shard", axis=0, tiled=True),
        lax.all_gather(w_value, "shard", axis=0, tiled=True),
        lax.all_gather(w_output, "shard", axis=0, tiled=True),
    )
    gain_one = attn_set[0].astype(jnp.float32)
    normed_one = norm_local(residual, gain_one).astype(jnp.bfloat16)

    def project(weight):
        product = jnp.dot(normed_one, weight, preferred_element_type=jnp.float32)
        return product.astype(jnp.bfloat16).reshape(length, head_count, head_size)

    queries = project(attn_set[1])
    key_rows = project(attn_set[2])
    value_rows = project(attn_set[3])
    one_hot = (buckets[:, None] == jnp.arange(bucket_count, dtype=jnp.int32)[None, :]).astype(
        jnp.float32
    )
    offset_bias = jnp.dot(one_hot, bias_table.astype(jnp.float32), precision=highest).T
    block_starts = jnp.arange(block_count, dtype=jnp.int32) * block_rows
    key_index = jnp.arange(length, dtype=jnp.int32)

    def block_scores(first_row, query_block):
        query_index = first_row + jnp.arange(block_rows, dtype=jnp.int32)
        bias_grid = toeplitz_grid(offset_bias, block_rows, length)
        scores = (
            jnp.einsum("qhd,khd->hqk", query_block, key_rows, preferred_element_type=jnp.float32)
            + bias_grid
        )
        allowed = key_index[None, :] // BLOCK <= query_index[:, None] // BLOCK
        return jnp.where(allowed[None], scores, masked_score)

    def attend(first_row):
        scores = block_scores(first_row, queries)
        row_max = jnp.max(scores, axis=-1, keepdims=True)
        exp_scores = jnp.exp(scores - row_max)
        totals = jnp.sum(exp_scores, axis=-1, keepdims=True)
        probability = (exp_scores / totals).astype(jnp.bfloat16)
        mixed_rows = jnp.einsum(
            "hqk,khd->qhd", probability, value_rows, preferred_element_type=jnp.float32
        )
        return (mixed_rows, (row_max + jnp.log(totals))[..., 0])

    mixed_blocks, log_totals = lax.map(attend, block_starts)
    attended = mixed_blocks.reshape(length, inner_width).astype(jnp.bfloat16)
    middle = residual + jnp.einsum(
        "ti,di->td", attended, attn_set[4], preferred_element_type=jnp.float32
    )
    ffn_set = (
        lax.all_gather(ffn_gain, "shard", axis=0, tiled=True),
        lax.all_gather(w_gate, "shard", axis=0, tiled=True),
        lax.all_gather(w_up, "shard", axis=0, tiled=True),
        lax.all_gather(w_down, "shard", axis=0, tiled=True),
    )
    gain_two = ffn_set[0].astype(jnp.float32)
    normed_two = norm_local(middle, gain_two).astype(jnp.bfloat16)
    gate_values = jnp.dot(normed_two, ffn_set[1], preferred_element_type=jnp.float32)
    up_values = jnp.dot(normed_two, ffn_set[2], preferred_element_type=jnp.float32)
    activated, gelu_pullback = jax.vjp(gelu_tanh, gate_values)
    hidden = (activated * up_values).astype(jnp.bfloat16)
    layer_out = (
        middle + jnp.einsum("tf,df->td", hidden, ffn_set[3], preferred_element_type=jnp.float32)
    ).astype(jnp.bfloat16)
    ffn_set = (
        lax.all_gather(ffn_gain, "shard", axis=0, tiled=True),
        lax.all_gather(w_gate, "shard", axis=0, tiled=True),
        lax.all_gather(w_up, "shard", axis=0, tiled=True),
        lax.all_gather(w_down, "shard", axis=0, tiled=True),
    )
    grad_w_down = jnp.einsum("td,tf->df", cotangent, hidden, preferred_element_type=jnp.float32)
    grad_hidden = jnp.dot(cotangent, ffn_set[3], preferred_element_type=jnp.float32)
    grad_gate = gelu_pullback(grad_hidden * up_values)[0].astype(jnp.bfloat16)
    grad_up = (grad_hidden * activated).astype(jnp.bfloat16)
    grad_w_gate = jnp.einsum("td,tf->df", normed_two, grad_gate, preferred_element_type=jnp.float32)
    grad_w_up = jnp.einsum("td,tf->df", normed_two, grad_up, preferred_element_type=jnp.float32)
    grad_normed_two = jnp.einsum(
        "tf,df->td", grad_gate, ffn_set[1], preferred_element_type=jnp.float32
    )
    grad_normed_two = grad_normed_two + jnp.einsum(
        "tf,df->td", grad_up, ffn_set[2], preferred_element_type=jnp.float32
    )
    middle_part, grad_gain_two = jax.vjp(norm_local, middle, gain_two)[1](grad_normed_two)
    grad_middle = cotangent.astype(jnp.float32) + middle_part
    ffn_shards = (
        lax.psum_scatter(grad_w_gate.astype(jnp.bfloat16), "shard", scatter_dimension=0, tiled=True),
        lax.psum_scatter(grad_w_up.astype(jnp.bfloat16), "shard", scatter_dimension=0, tiled=True),
        lax.psum_scatter(grad_w_down.astype(jnp.bfloat16), "shard", scatter_dimension=0, tiled=True),
    )
    attn_set = (
        lax.all_gather(attn_gain, "shard", axis=0, tiled=True),
        lax.all_gather(w_query, "shard", axis=0, tiled=True),
        lax.all_gather(w_key, "shard", axis=0, tiled=True),
        lax.all_gather(w_value, "shard", axis=0, tiled=True),
        lax.all_gather(w_output, "shard", axis=0, tiled=True),
    )
    grad_branch = grad_middle.astype(jnp.bfloat16)
    grad_w_output = jnp.einsum(
        "td,ti->di", grad_branch, attended, preferred_element_type=jnp.float32
    )
    grad_attended = jnp.einsum(
        "td,di->ti", grad_branch, attn_set[4], preferred_element_type=jnp.float32
    )
    grad_attended = grad_attended.astype(jnp.bfloat16).reshape(length, head_count, head_size)

    def attend_back(carried, block_input):
        grad_keys, grad_values, grad_offsets = carried
        first_row, log_total = block_input
        scores = block_scores(first_row, queries)
        probability = jnp.exp(scores - log_total[..., None])
        grad_probs = jnp.einsum(
            "qhd,khd->hqk", grad_attended, value_rows, preferred_element_type=jnp.float32
        )
        inner_sum = jnp.sum(probability * grad_probs, axis=-1, keepdims=True)
        grad_scores = (probability * (grad_probs - inner_sum)).astype(jnp.bfloat16)
        grad_values = grad_values + jnp.einsum(
            "hqk,qhd->khd",
            probability.astype(jnp.bfloat16),
            grad_attended,
            preferred_element_type=jnp.float32,
        )
        grad_keys = grad_keys + jnp.einsum(
            "hqk,qhd->khd", grad_scores, queries, preferred_element_type=jnp.float32
        )
        grad_queries = jnp.einsum(
            "hqk,khd->qhd", grad_scores, key_rows, preferred_element_type=jnp.float32
        )
        diagonal_sums = diagonal_total(grad_scores.astype(jnp.float32))
        offset_piece = grad_offsets
        grad_offsets = offset_piece + diagonal_sums
        return ((grad_keys, grad_values, grad_offsets), grad_queries)

    zero_rows = jnp.zeros((length, head_count, head_size), jnp.float32)
    zero_offsets = jnp.zeros((head_count, 2 * length - 1), jnp.float32)
    (grad_keys, grad_values, grad_offsets), query_blocks = lax.scan(
        attend_back, (zero_rows, zero_rows, zero_offsets), (block_starts, log_totals)
    )
    grad_queries = query_blocks.reshape(length, inner_width).astype(jnp.bfloat16)
    grad_keys = grad_keys.reshape(length, inner_width).astype(jnp.bfloat16)
    grad_values = grad_values.reshape(length, inner_width).astype(jnp.bfloat16)
    grad_w_query = jnp.einsum(
        "td,ti->di", normed_one, grad_queries, preferred_element_type=jnp.float32
    )
    grad_w_key = jnp.einsum("td,ti->di", normed_one, grad_keys, preferred_element_type=jnp.float32)
    grad_w_value = jnp.einsum(
        "td,ti->di", normed_one, grad_values, preferred_element_type=jnp.float32
    )
    grad_normed_one = jnp.einsum(
        "ti,di->td", grad_queries, attn_set[1], preferred_element_type=jnp.float32
    )
    grad_normed_one = grad_normed_one + jnp.einsum(
        "ti,di->td", grad_keys, attn_set[2], preferred_element_type=jnp.float32
    )
    grad_normed_one = grad_normed_one + jnp.einsum(
        "ti,di->td", grad_values, attn_set[3], preferred_element_type=jnp.float32
    )
    rows_part, grad_gain_one = jax.vjp(norm_local, residual, gain_one)[1](grad_normed_one)
    grad_tokens = (grad_middle + rows_part).astype(jnp.bfloat16)
    grad_table = jnp.dot(grad_offsets, one_hot, precision=highest).T
    owner_start = lax.axis_index("shard") * owner_rows
    attn_shards = (
        lax.psum_scatter(grad_w_query.astype(jnp.bfloat16), "shard", scatter_dimension=0, tiled=True),
        lax.psum_scatter(grad_w_key.astype(jnp.bfloat16), "shard", scatter_dimension=0, tiled=True),
        lax.psum_scatter(grad_w_value.astype(jnp.bfloat16), "shard", scatter_dimension=0, tiled=True),
        lax.psum_scatter(grad_w_output.astype(jnp.bfloat16), "shard", scatter_dimension=0, tiled=True),
    )
    summed = lax.psum(
        (
            attn_shards[0],
            attn_shards[1],
            attn_shards[2],
            attn_shards[3],
            ffn_shards[0],
            ffn_shards[1],
            ffn_shards[2],
        ),
        "rep",
    )
    small_total = lax.psum((grad_gain_one, grad_gain_two, grad_table), ("shard", "rep"))
    gain_one_own = lax.dynamic_slice_in_dim(small_total[0], owner_start, owner_rows, 0)
    gain_two_own = lax.dynamic_slice_in_dim(small_total[1], owner_start, owner_rows, 0)
    return (
        layer_out,
        grad_tokens,
        gain_one_own,
        summed[0].astype(jnp.float32),
        summed[1].astype(jnp.float32),
        summed[2].astype(jnp.float32),
        summed[3].astype(jnp.float32),
        gain_two_own,
        summed[4].astype(jnp.float32),
        summed[5].astype(jnp.float32),
        summed[6].astype(jnp.float32),
        small_total[2],
    )

HEAD_SLOTS = 7
TAIL_SLOTS = 12
HELPED = (1, 2, 3, 4, 5, 6)
SLOTS = {
    "send": (0, 0, 0, 2, 2, 4, 4),
    "forward": (1, 1, 1, 5, 5, 6, 7),
    "swap": (4, 4, 4, 8, 10, 13, 15),
    "get_forward": (3, 5, 5, 11, 12, 14, 16),
    "get_swap": (3, 5, 5, 12, 14, 16, 17),
    "turn": (10, 12, 14, 16, 19, 20, 24, 26, 27),
    "rep": (12, 13, 16, 19, 22, 24, 25, 28, 29),
    "mid": (14, 17, 19, 21, 24, 25, 27, 30, 31),
    "last": (16, 19, 21, 24, 25, 27, 29, 31, 32),
}


def dot_nn(a, b):
    return lax.dot_general(a, b, (((1,), (0,)), ((), ())), preferred_element_type=f32)


def dot_nt(a, b):
    return lax.dot_general(a, b, (((1,), (1,)), ((), ())), preferred_element_type=f32)


def dot_tn(a, b):
    return lax.dot_general(a, b, (((0,), (0,)), ((), ())), preferred_element_type=f32)


def fused_kernel(
    xt_ref,
    ct_ref,
    buckets_ref,
    table_ref,
    gains_ref,
    wq_ref,
    wk_ref,
    wv_ref,
    wo_ref,
    wg_ref,
    wu_ref,
    wd_ref,
    out_ref,
    gtok_ref,
    small_ref,
    gq_ref,
    gk_ref,
    gv_ref,
    go_ref,
    gg_ref,
    gu_ref,
    gd_ref,
    land_ref,
    sum_ref,
    hop_ref,
    turn_ref,
    gland,
    gcol,
    n1t,
    n2t,
    mid,
    acc_o,
    acc_n,
    qt,
    kt,
    vt,
    att,
    dat,
    dqt,
    dkt,
    dvt,
    wq,
    wk,
    wv,
    wo,
    wg2,
    wu2,
    wd2,
    wload,
    g,
    hid,
    dgt,
    dup,
    rc,
    stage_t,
    stage_v,
    vbuf,
    zi,
    zm,
    ubuf,
    revb,
    onehot,
    doff,
    sms,
    smr,
    gain_s,
    gain_r,
    gsend,
    gloc,
    g1r,
    g2r,
    gpr,
    load_sem,
    e0s,
    e0r,
    sum_sem,
    stage_sem,
    e1s,
    e1r,
    e2s,
    e2r,
    zis,
    zir,
    zms,
    zmr,
    us,
    ul,
    ur,
    sss,
    ssr,
    zcredit,
    *,
    chunks,
    heads,
):
    width = xt_ref.shape[0]
    toks = xt_ref.shape[1]
    rows = gains_ref.shape[0]
    fw = land_ref.shape[2]
    sub = fw // 3
    aw = wq_ref.shape[1]
    hs = aw // heads
    total = chunks + 2
    eps = 1e-06
    lanes = revb.shape[1]
    big = 2 * rows
    nbig = width // big

    s = lax.axis_index("shard")
    r = lax.axis_index("rep")
    c = s % 2
    x = (s // 2) % 2
    y = s // 4
    sc = s + 1 - 2 * c
    sx = s + 2 - 4 * x
    sy = s + 4 - 8 * y
    bx = sx - c
    by = sy - c
    bd = (1 - y) * 4 + (1 - x) * 2
    b_own = s - c
    mate = r + 1 - 2 * (r % 2)
    inner = (r == 1) | (r == 2)
    outer = (r == 0) | (r == 3)

    def remote(src, dst, ssem, rsem, dev):
        return pltpu.make_async_remote_copy(
            src_ref=src, dst_ref=dst, send_sem=ssem, recv_sem=rsem, device_id=dev, device_id_type=MESH
        )

    def settle(ref, sem):
        pltpu.make_async_copy(ref, ref, sem).wait()

    barrier = pltpu.get_barrier_semaphore()
    near = [(sc, r), (bx, r), (bx + 1, r), (by, r), (by + 1, r), (bd, r), (bd + 1, r), (s, mate), (sc, mate)]
    for dev in near:
        pl.semaphore_signal(barrier, inc=1, device_id=dev, device_id_type=MESH)

    @pl.when(inner)
    def _():
        pl.semaphore_signal(barrier, inc=1, device_id=(s, 3 - r), device_id_type=MESH)

    @pl.when(inner)
    def _():
        pl.semaphore_wait(barrier, len(near) + 1)

    @pl.when(outer)
    def _():
        pl.semaphore_wait(barrier, len(near))

    def place(chunk, index):
        kind, k = chunk
        if kind == "a":
            return g.at[16 + index, :, pl.ds(k * aw, aw)]
        return land_ref.at[k * 16 + index]

    def places(chunk, count):
        kind, k = chunk
        if kind == "a":
            return g.at[pl.ds(16, count), :, pl.ds(k * aw, aw)]
        return land_ref.at[pl.ds(0, count)]

    def any_of(value, options):
        return functools.reduce(jnp.logical_or, [value == option for option in options], jnp.bool_(False))

    def helped(chunk):
        kind, k = chunk
        return False if kind == "a" else any_of(k, HELPED)

    def active(chunk):
        kind, k = chunk
        return True if kind == "a" else jnp.logical_not(any_of(k, HELPED)) | (r % 2 == k % 2)

    def when(condition, then):
        if condition is True:
            then()
        elif condition is not False:
            pl.when(condition)(then)

    def columns(k, half):
        return pl.ds(pl.multiple_of((2 * k + half) * sub, sub), sub)

    def own_parts(chunk, half):
        kind, k = chunk
        dst = place(chunk, half * 8 + s)
        if kind == "a":
            return [(((wq_ref, wk_ref), (wv_ref, wo_ref))[k][half], dst)]
        return [
            (ref.at[:, columns(k, half)], dst.at[:, pl.ds(j * sub, sub)]) for j, ref in enumerate((wg_ref, wu_ref, wd_ref))
        ]

    def at(chunk):
        kind, k = chunk
        return k if kind == "a" else k + 2

    def gather_send(chunk):
        i = at(chunk)

        def cross():
            for half in (0, 1):
                for src, dst in own_parts(chunk, half):
                    remote(src, dst, gsend.at[i], g1r.at[i], (bx + half, r)).start()
                    remote(src, dst, gsend.at[i], g1r.at[i], (by + half, r)).start()

        when(active(chunk), cross)
        for half in (0, 1):
            for src, dst in own_parts(chunk, half):
                remote(src, dst, gsend.at[i], gpr.at[i], (sc, r)).start()
                pltpu.make_async_copy(src, dst, gloc.at[i]).start()

    def hand_over(chunk, blocks, sem):
        i = at(chunk)

        def hand():
            for b in blocks:
                spot = place(chunk, c * 8 + b)
                remote(spot, spot, gsend.at[i], sem.at[i], (s, mate)).start()

        if chunk[0] == "f":
            pl.when(helped(chunk) & active(chunk))(hand)
        for b in blocks:
            spot = place(chunk, c * 8 + b)
            remote(spot, spot, gsend.at[i], gpr.at[i], (sc, r)).start()

    def gather_forward(chunk):
        i = at(chunk)
        settle(places(chunk, 4), g1r.at[i])

        def cross():
            one = place(chunk, c * 8 + bx)
            two = place(chunk, c * 8 + by + 1)
            remote(one, one, gsend.at[i], g2r.at[i], (sy, r)).start()
            remote(two, two, gsend.at[i], g2r.at[i], (sx, r)).start()

        when(active(chunk), cross)
        hand_over(chunk, (bx, bx + 1, by, by + 1), g1r)

    def gather_swap(chunk):
        settle(places(chunk, 2), g2r.at[at(chunk)])
        hand_over(chunk, (bd, bd + 1), g2r)

    def gather_done(chunk):
        i = at(chunk)
        settle(places(chunk, 8), gpr.at[i])
        settle(places(chunk, 2), gloc.at[i])

    def gather_sent(chunk):
        i = at(chunk)
        does = active(chunk)
        if does is True:
            settle(places(chunk, 14), gsend.at[i])
            return
        pl.when(does & helped(chunk))(lambda: settle(places(chunk, 20), gsend.at[i]))
        pl.when(does & jnp.logical_not(helped(chunk)))(lambda: settle(places(chunk, 14), gsend.at[i]))
        pl.when(jnp.logical_not(does))(lambda: settle(places(chunk, 8), gsend.at[i]))

    def ahead(stage, k, mine):
        chunk = ("f", k)
        does = active(chunk) if mine else jnp.logical_not(active(chunk))
        pl.when((k < chunks) & does)(lambda: stage(chunk))

    def cut(ref, w):
        return ref if w == fw else ref.at[:, :, pl.ds(0, w)]

    def cut1(ref, index, w):
        return ref.at[index] if w == fw else ref.at[index, :, pl.ds(0, w)]

    def span(ref, start, count, w):
        return ref.at[pl.ds(start, count)] if w == fw else ref.at[pl.ds(start, count), :, pl.ds(0, w)]

    def get(ref, index, w):
        return ref[index] if w == fw else ref[index, :, 0:w]

    def put(ref, index, w, value):
        if w == fw:
            ref[index] = value
        else:
            ref[index, :, 0:w] = value

    def add_to(dst, i, src, j, w):
        put(dst, i, w, get(dst, i, w) + get(src, j, w))

    def core_part(n, b, count, w):
        slot = n % 2
        remote(
            span(g, slot * 16 + (1 - c) * 8 + b, count, w), span(rc, slot * 8 + b, count, w), e0s.at[n], e0r.at[n], (sc, r)
        ).start()

    def plane_send(n, w):
        slot = n % 2
        base = slot * 16 + c * 8
        settle(span(rc, slot * 8, 8, w), e0r.at[n])
        order = []
        for k, kx, ky in ((0, 1 - y, 1 - x), (1, y, x)):
            order.append((4 * kx + 2 * (1 - x), sx, 2 * k))
            order.append((4 * (1 - y) + 2 * ky + 1, sy, 2 * k + 1))
        order += [(b, None, None) for b in (4 * (1 - y) + 2 * x, 4 * y + 2 * (1 - x) + 1, b_own, b_own + 1)]

        def store(i):
            b = order[i][0]
            return pltpu.make_async_copy(cut1(g, base + b, w), cut1(sum_ref, n * 8 + b, w), sum_sem.at[n, i])

        for i, (b, _, _) in enumerate(order):
            add_to(g, base + b, rc, slot * 8 + b, w)
            store(i).start()
        for i, (b, dev, spot) in enumerate(order[:4]):
            store(i).wait()
            remote(
                cut1(sum_ref, n * 8 + b, w), cut1(hop_ref, n * 4 + spot, w), e1s.at[n], e1r.at[n, spot // 2], (dev, r)
            ).start()

    def stored(n, w):
        for i in range(4, 8):
            settle(cut1(sum_ref, 0, w), sum_sem.at[n, i])

    def slot_free(n):
        settle(span(g, 0, 8, width_of(n)), e0s.at[n])

    def turn_free(n):
        settle(span(turn_ref, 0, 2, width_of(n)), e2s.at[n])

    def guarded(n, least, then):
        if isinstance(n, int):
            if n >= least:
                then()
        else:
            pl.when(n >= least)(then)

    def turn_loads(n, w):
        base = (n % 2) * 4
        first = n * 8 + 4 * (1 - y) + 2 * x
        second = n * 8 + 4 * y + 2 * (1 - x) + 1
        return [
            pltpu.make_async_copy(cut1(sum_ref, first, w), cut1(stage_t, base, w), stage_sem.at[0]),
            pltpu.make_async_copy(cut1(sum_ref, second, w), cut1(stage_t, base + 1, w), stage_sem.at[1]),
            pltpu.make_async_copy(span(hop_ref, n * 4, 2, w), span(stage_t, base + 2, 2, w), stage_sem.at[2]),
        ]

    def turn_start(n, w):
        guarded(n, 2, lambda: turn_free(n - 2))
        settle(span(hop_ref, 0, 2, w), e1r.at[n, 0])
        for load in turn_loads(n, w):
            load.start()

    def turn_end(n, w):
        base = (n % 2) * 4
        for load in turn_loads(n, w):
            load.wait()
        for j, dev in ((0, sy), (1, sx)):
            add_to(stage_t, base + j, stage_t, base + 2 + j, w)
            remote(cut1(stage_t, base + j, w), cut1(turn_ref, n * 2 + j, w), e2s.at[n], e2r.at[n], (dev, r)).start()

    def rep_loads(n, w):
        return [
            pltpu.make_async_copy(span(sum_ref, n * 8 + b_own, 2, w), span(stage_v, 0, 2, w), stage_sem.at[3]),
            pltpu.make_async_copy(span(hop_ref, n * 4 + 2, 2, w), span(stage_v, 2, 2, w), stage_sem.at[4]),
            pltpu.make_async_copy(span(turn_ref, n * 2, 2, w), span(stage_v, 4, 2, w), stage_sem.at[5]),
        ]

    def rep_start(n, w):
        settle(span(hop_ref, 0, 2, w), e1r.at[n, 1])
        settle(span(turn_ref, 0, 2, w), e2r.at[n])
        for load in rep_loads(n, w):
            load.start()

    def rep_end(n, w):
        slot = n % 2
        if isinstance(n, int):
            if n >= 2:
                pl.when(outer)(functools.partial(rep_free, n))
        else:
            pl.when(outer & (n >= 2))(functools.partial(rep_free, n))
        for load in rep_loads(n, w):
            load.wait()
        for j in (0, 1):
            value = get(stage_v, j, w).astype(f32) + get(stage_v, 2 + j, w).astype(f32)
            value = value + get(stage_v, 4 + j, w).astype(f32)
            put(vbuf, slot * 2 + j, w, value.astype(bf16))

        @pl.when(outer)
        def _():
            remote(
                span(vbuf, slot * 2, 2, w), span(zi, slot * 2, 2, w), zis.at[n], zir.at[n], (s, mate)
            ).start()

    def width_of(n):
        return fw if not isinstance(n, int) or n < chunks else aw

    def rep_free(n):
        earlier = n - 2
        slot = n % 2
        settle(span(vbuf, slot * 2, 2, width_of(earlier)), zis.at[earlier])
        pl.semaphore_wait(zcredit, 1)

    def rep_turn(n, w):
        slot = n % 2

        @pl.when(inner)
        def _():
            settle(span(zi, slot * 2, 2, w), zir.at[n])
            for j in (0, 1):
                add_to(vbuf, slot * 2 + j, zi, slot * 2 + j, w)

            def credit():
                pl.semaphore_signal(zcredit, inc=1, device_id=(s, mate), device_id_type=MESH)

            if isinstance(n, int):
                if n + 2 < total:
                    credit()
            else:
                credit()
            remote(
                span(vbuf, slot * 2, 2, w), span(zm, slot * 2, 2, w), zms.at[n], zmr.at[n], (s, 3 - r)
            ).start()

    def result(n, half, block):
        if isinstance(n, int) and n >= chunks:
            return [(block, ((gv_ref, go_ref), (gq_ref, gk_ref))[n - chunks][half])]
        return [
            (block.at[:, pl.ds(j * sub, sub)], ref.at[:, columns(n, half)])
            for j, ref in enumerate((gg_ref, gu_ref, gd_ref))
        ]

    def u_free(n, w):
        slot = n % 2
        for k in (0, 1, 2):
            settle(cut1(ubuf, slot * 2, w), us.at[n, k])
        settle(cut1(ubuf, slot * 2, w), ul.at[n])

    def rep_last(n, w):
        slot = n % 2

        @pl.when(inner)
        def _():
            settle(span(zm, slot * 2, 2, w), zmr.at[n])
            if isinstance(n, int):
                if n >= 2:
                    u_free(n - 2, width_of(n - 2))
            else:
                pl.when(n >= 2)(lambda: u_free(n - 2, w))
            for j in (0, 1):
                value = get(vbuf, slot * 2 + j, w).astype(f32) + get(zm, slot * 2 + j, w).astype(f32)
                put(ubuf, slot * 2 + j, w, value.astype(bf16))
            keep = cut1(ubuf, slot * 2 + c, w)
            give = cut1(ubuf, slot * 2 + 1 - c, w)

            def finish(half):
                for src, dst in result(n, half, keep):
                    remote(src, dst, us.at[n, 0], ur.at[n, half], (s, mate)).start()
                    pltpu.make_async_copy(src, dst, ul.at[n]).start()
                for src, dst in result(n, half, give):
                    remote(src, dst, us.at[n, 1], ur.at[n, half], (sc, mate)).start()
                    remote(src, dst, us.at[n, 2], ur.at[n, half], (sc, r)).start()

            if w == fw:
                finish(c)
            else:
                pl.when(c == 0)(lambda: finish(0))
                pl.when(c == 1)(lambda: finish(1))
            settle(span(vbuf, slot * 2, 2, w), zms.at[n])

    def gathers(stage, mine):
        return lambda k: ahead(stage, k, mine)

    def reduces(stage):
        return lambda n: stage(n, width_of(n))

    order = (
        ("swap", gathers(gather_swap, True)),
        ("forward", gathers(gather_forward, True)),
        ("send", lambda k: gather_send(("f", k))),
        ("turn", reduces(turn_start)),
        ("rep", reduces(rep_start)),
        ("last", reduces(rep_last)),
        ("mid", reduces(rep_turn)),
        ("turn", reduces(turn_end)),
        ("rep", reduces(rep_end)),
        ("get_forward", gathers(gather_forward, False)),
        ("get_swap", gathers(gather_swap, False)),
    )
    loop_at = HEAD_SLOTS
    tail_at = HEAD_SLOTS + 2 * chunks

    def do(slot):
        for name, stage in order:
            for n, spot in enumerate(SLOTS[name]):
                if spot == slot:
                    stage(n)

    def do_in_loop(t, side):
        for name, stage in order:
            pairs = [
                ((spot - loop_at) // 2, n)
                for n, spot in enumerate(SLOTS[name])
                if loop_at <= spot < tail_at and (spot - loop_at) % 2 == side
            ]
            if pairs:
                n = sum([jnp.where(t == step, number, 0) for step, number in pairs], jnp.int32(0))
                pl.when(any_of(t, [step for step, _ in pairs]))(functools.partial(stage, n))

    def small_send(step):
        if step < 3:
            dev = ((sc, r), (sx, r), (sy, r))[step]
            remote(sms.at[step], smr.at[step], sss.at[step], ssr.at[step], dev).start()
        elif step == 3:

            @pl.when(outer)
            def _():
                remote(sms.at[3], smr.at[3], sss.at[3], ssr.at[3], (s, mate)).start()
        elif step == 4:

            @pl.when(inner)
            def _():
                remote(sms.at[4], smr.at[4], sss.at[4], ssr.at[4], (s, 3 - r)).start()
        else:

            @pl.when(inner)
            def _():
                remote(sms.at[5], smr.at[5], sss.at[5], ssr.at[5], (s, mate)).start()

    def small_step(step):
        def take():
            settle(smr.at[step], ssr.at[step])
            settle(sms.at[step], sss.at[step])
            if step < 2:
                sms[step + 1] = sms[step] + smr[step]
            elif step == 2:
                sms[3] = sms[2] + smr[2]

        if step < 3:
            take()
            small_send(step + 1)
        elif step == 3:

            @pl.when(inner)
            def _():
                settle(smr.at[3], ssr.at[3])
                sms[4] = sms[3] + smr[3]

            @pl.when(outer)
            def _():
                settle(sms.at[3], sss.at[3])

            small_send(4)
        elif step == 4:

            @pl.when(inner)
            def _():
                settle(smr.at[4], ssr.at[4])
                settle(sms.at[4], sss.at[4])
                sms[5] = sms[4] + smr[4]
                small_ref[...] = sms[5]

            small_send(5)
        else:

            @pl.when(inner)
            def _():
                settle(sms.at[5], sss.at[5])

            @pl.when(outer)
            def _():
                settle(smr.at[5], ssr.at[5])
                small_ref[...] = smr[5]

    tile = 64
    tiles = width // tile

    def over_rows(body, start):
        def step(i, carry):
            return body(pl.ds(pl.multiple_of(i * tile, tile), tile), carry)

        return lax.fori_loop(0, tiles, step, start)

    def fold(value):
        return jnp.sum(value.reshape(tile // 8, 8, toks), axis=0)

    zero8 = jnp.zeros((8, toks), f32)

    gather_send(("a", 0))
    gdst = gland.at[s]
    for k, dev in enumerate([(sc, r), (bx, r), (bx + 1, r), (by, r), (by + 1, r), (bd, r), (bd + 1, r)]):
        remote(gains_ref, gdst, gain_s, gain_r, dev).start()
    pltpu.make_async_copy(gains_ref, gdst, load_sem.at[1]).start()
    gather_send(("a", 1))
    do(0)

    def square_sum(sl, acc):
        v = xt_ref[sl, :].astype(f32)
        return acc + fold(v * v)

    ssum = jnp.sum(over_rows(square_sum, zero8), axis=0, keepdims=True)
    r1 = lax.rsqrt(ssum * (1.0 / width) + eps)

    bucket_index = lax.broadcasted_iota(jnp.int32, (table_ref.shape[1], lanes), 0)
    rev_hot = (bucket_index == buckets_ref[0:1, :]).astype(bf16)
    onehot[...] = (bucket_index == buckets_ref[1:2, :]).astype(bf16)
    revb[...] = dot_nn(table_ref[...], rev_hot)

    settle(gland.at[pl.ds(0, 7)], gain_r)
    settle(gland.at[0], load_sem.at[1])
    for b in range(8):
        gcol[rows * b : rows * (b + 1), :] = gland[b].astype(f32)

    def norm_one(sl, carry):
        v = xt_ref[sl, :].astype(f32)
        n1t[sl, :] = (v * r1 * gcol[sl, 0:1]).astype(bf16)
        return carry

    gather_forward(("a", 0))
    do(1)
    over_rows(norm_one, 0)
    gather_swap(("a", 0))
    gather_forward(("a", 1))
    do(2)

    def compact(dst, half, col):
        @pl.loop(0, nbig)
        def _(i):
            both = jnp.concatenate(
                [
                    g[16 + half * 8 + 2 * i, :, col : col + aw].astype(f32),
                    g[16 + half * 8 + 2 * i + 1, :, col : col + aw].astype(f32),
                ],
                axis=0,
            )
            dst[pl.ds(pl.multiple_of(i * 2 * rows, 16), 2 * rows), :] = both.astype(bf16)

    gather_done(("a", 0))
    compact(wq, 0, 0)
    qt[...] = dot_tn(wq[...], n1t[...]).astype(bf16)
    compact(wk, 1, 0)
    kt[...] = dot_tn(wk[...], n1t[...]).astype(bf16)
    gather_swap(("a", 1))
    do(3)
    gather_done(("a", 1))
    compact(wv, 0, aw)
    vt[...] = dot_tn(wv[...], n1t[...]).astype(bf16)
    compact(wo, 1, aw)
    do(4)

    half_tok = toks // 2

    def softmax_block(h, head, block):
        keys = half_tok * (block + 1)
        low = half_tok * block
        row = jnp.broadcast_to(revb[pl.ds(h, 1), :], (half_tok, lanes))
        bias = pltpu.roll(row, (low + 1 - toks) % lanes, 1, stride=1, stride_axis=0)[:, :keys]
        scores = dot_tn(qt[head, low : low + half_tok], kt[head, 0:keys]) + bias
        e = jnp.exp(scores - jnp.max(scores, axis=1, keepdims=True))
        return e * (1.0 / jnp.sum(e, axis=1, keepdims=True)), low, keys

    def attend(h, carry):
        head = pl.ds(pl.multiple_of(h * hs, hs), hs)
        for block in (0, 1):
            p, low, keys = softmax_block(h, head, block)
            att[head, low : low + half_tok] = dot_nt(vt[head, 0:keys], p.astype(bf16)).astype(bf16)
        return carry

    lax.fori_loop(0, heads // 2, attend, 0)
    do(5)
    lax.fori_loop(heads // 2, heads, attend, 0)
    do(6)

    def branch_one(i, acc):
        sl = pl.ds(pl.multiple_of(i * big, 16), big)
        m = xt_ref[sl, :].astype(f32) + dot_nn(wo[sl, :], att[...])
        mid[sl, :] = m
        return acc + jnp.sum((m * m).reshape(big // 8, 8, toks), axis=0)

    ssum = jnp.sum(lax.fori_loop(0, nbig, branch_one, zero8), axis=0, keepdims=True)
    r2n = lax.rsqrt(ssum * (1.0 / width) + eps)

    def norm_two(sl, carry):
        m = mid[sl, :]
        n2t[sl, :] = (m * r2n * gcol[sl, 1:2]).astype(bf16)
        acc_o[sl, :] = m
        acc_n[sl, :] = jnp.zeros((tile, toks), f32)
        return carry

    over_rows(norm_two, 0)

    tok_tile = toks // 2

    parts = [(half, k) for half in (0, 1) for k in (0, 1, 2)]
    depth = 4

    def load(t, p):
        half, k = parts[p]
        return pltpu.make_async_copy(
            land_ref.at[pl.ds(t * 16 + half * 8, 8), :, pl.ds(k * sub, sub)],
            wload.at[pl.ds((p % depth) * 8, 8)],
            load_sem.at[p % depth],
        )

    def ffn_load(t):
        for p in range(depth):
            load(t, p).start()

    def ffn_chunk(t):
        slot = t % 2
        for p, (half, k) in enumerate(parts):
            load(t, p).wait()
            dst = (wg2, wu2, wd2)[k]

            @pl.loop(0, nbig)
            def _(i):
                base = (p % depth) * 8 + 2 * i
                both = jnp.concatenate([wload[base].astype(f32), wload[base + 1].astype(f32)], axis=0)
                sl = pl.ds(pl.multiple_of(i * big, 16), big)
                dst[sl, half * sub : (half + 1) * sub] = both.astype(bf16)

            if p + depth < len(parts):
                load(t, p + depth).start()

        @pl.loop(0, toks // tok_tile)
        def _(m):
            sl = pl.ds(pl.multiple_of(m * tok_tile, tok_tile), tok_tile)
            gate = dot_tn(n2t[:, sl], wg2[...])
            up = dot_tn(n2t[:, sl], wu2[...])
            gh = dot_tn(ct_ref[:, sl], wd2[...])
            k0 = 0.7978845608028654
            k1 = 0.044715
            sq = gate * gate
            th = jnp.tanh(k0 * (gate + k1 * (sq * gate)))
            half_one = 0.5 * (1.0 + th)
            act = gate * half_one
            slope = half_one + 0.5 * gate * (1.0 - th * th) * (k0 * (1.0 + 3.0 * k1 * sq))
            hid[sl, :] = (act * up).astype(bf16)
            dgt[sl, :] = (gh * up * slope).astype(bf16)
            dup[sl, :] = (gh * act).astype(bf16)

        @pl.loop(0, nbig)
        def _(i):
            sl = pl.ds(pl.multiple_of(i * big, 16), big)
            acc_o[sl, :] += dot_nt(wd2[sl, :], hid[...])
            acc_n[sl, :] += dot_nt(wg2[sl, :], dgt[...]) + dot_nt(wu2[sl, :], dup[...])
            for k, value in enumerate(
                (dot_nn(n2t[sl, :], dgt[...]), dot_nn(n2t[sl, :], dup[...]), dot_nn(ct_ref[sl, :], hid[...]))
            ):
                for half in (0, 1):
                    for j in (0, 1):
                        g[slot * 16 + half * 8 + 2 * i + j, :, k * sub : (k + 1) * sub] = value[
                            rows * j : rows * (j + 1), half * sub : (half + 1) * sub
                        ].astype(bf16)
            core_part(t, 2 * i, 2, fw)

    def ffn_step(t, carry):
        gather_done(("f", t))
        ffn_load(t)
        pl.when(t >= 1)(lambda: stored(t - 1, fw))
        do_in_loop(t, 0)
        pl.when(t >= 2)(lambda: slot_free(t - 2))
        ffn_chunk(t)
        do_in_loop(t, 1)
        plane_send(t, fw)
        return carry

    gather_sent(("a", 0))
    gather_sent(("a", 1))
    lax.fori_loop(0, chunks, ffn_step, 0)

    nv = chunks
    nq = chunks + 1
    stored(nv - 1, fw)
    do(tail_at)
    pick = lax.broadcasted_iota(jnp.int32, (8, toks), 0)

    def token_sums(row):
        chosen = (pick == row).astype(bf16)
        return dot_nt(chosen, wg2[...]) + dot_nt(chosen, wu2[...])

    def second_mean(sl, acc):
        return acc + fold(gcol[sl, 1:2] * acc_n[sl, :] * mid[sl, :])

    back = jnp.sum(over_rows(second_mean, zero8), axis=0, keepdims=True) * (1.0 / width)
    back = back * (r2n * r2n * r2n)

    def second_norm(sl, carry):
        m = mid[sl, :]
        gn = acc_n[sl, :]
        out_ref[sl, :] = acc_o[sl, :].astype(bf16)
        v = gn * m * r2n
        hi = v.astype(bf16)
        wg2[sl, :] = hi
        wu2[sl, :] = (v - hi.astype(f32)).astype(bf16)
        gm = ct_ref[sl, :].astype(f32) + r2n * gcol[sl, 1:2] * gn - m * back
        acc_n[sl, :] = gm
        n2t[sl, :] = gm.astype(bf16)
        return carry

    over_rows(second_norm, 0)
    sms[0] = jnp.zeros(sms.shape[1:], f32)
    sms[0, :, 0:width] = token_sums(1)
    do(tail_at + 1)

    dat[...] = dot_tn(wo[...], n2t[...]).astype(bf16)

    def weight_grad(n, half, left, right):
        @pl.loop(0, nbig)
        def _(i):
            sl = pl.ds(pl.multiple_of(i * big, 16), big)
            value = dot_nt(left[sl, :], right[...])
            for j in (0, 1):
                g[(n % 2) * 16 + half * 8 + 2 * i + j, :, 0:aw] = value[rows * j : rows * (j + 1), :].astype(bf16)

    slot_free(5)
    weight_grad(nv, 1, n2t, att)
    do(tail_at + 2)
    flip = (
        lax.broadcasted_iota(jnp.int32, (toks, toks), 0) + lax.broadcasted_iota(jnp.int32, (toks, toks), 1)
        == toks - 1
    )
    hid[...] = flip.astype(bf16)
    doff[...] = jnp.zeros(doff.shape, f32)

    def attend_back(h, carry):
        head = pl.ds(pl.multiple_of(h * hs, hs), hs)
        grad_v = []
        grad_k = []
        offsets = jnp.zeros((1, lanes), f32)
        for block in (0, 1):
            p, low, keys = softmax_block(h, head, block)
            q_rows = qt[head, low : low + half_tok]
            a_rows = dat[head, low : low + half_tok]
            grad_p = dot_tn(a_rows, vt[head, 0:keys])
            ds = (p * (grad_p - jnp.sum(p * grad_p, axis=1, keepdims=True))).astype(bf16)
            grad_v.append(dot_nn(a_rows, p.astype(bf16)))
            grad_k.append(dot_nn(q_rows, ds))
            dqt[head, low : low + half_tok] = dot_nt(kt[head, 0:keys], ds).astype(bf16)
            turned = dot_nn(ds, hid[0:keys, toks - keys : toks])
            padded = jnp.concatenate([turned, jnp.zeros((half_tok, lanes - keys), f32)], axis=1)
            lined = pltpu.roll(padded, half_tok, 1, stride=1, stride_axis=0)
            offsets = offsets + jnp.sum(lined, axis=0, keepdims=True)
        for dst, parts in ((dvt, grad_v), (dkt, grad_k)):
            dst[head, 0:half_tok] = (parts[0] + parts[1][:, 0:half_tok]).astype(bf16)
            dst[head, half_tok:toks] = parts[1][:, half_tok:toks].astype(bf16)
        doff[pl.ds(h, 1), :] = offsets
        return carry

    lax.fori_loop(0, heads // 2, attend_back, 0)
    do(tail_at + 3)
    lax.fori_loop(heads // 2, heads, attend_back, 0)
    weight_grad(nv, 0, n1t, dvt)
    core_part(nv, 0, 8, aw)
    slot_free(6)
    weight_grad(nq, 0, n1t, dqt)
    weight_grad(nq, 1, n1t, dkt)
    plane_send(nv, aw)
    core_part(nq, 0, 8, aw)
    stored(nv, aw)
    do(tail_at + 4)
    plane_send(nq, aw)
    stored(nq, aw)
    do(tail_at + 5)

    def first_back(i, acc):
        sl = pl.ds(pl.multiple_of(i * big, 16), big)
        gn = dot_nn(wq[sl, :], dqt[...]) + dot_nn(wk[sl, :], dkt[...]) + dot_nn(wv[sl, :], dvt[...])
        acc_o[sl, :] = gn
        v = gcol[sl, 0:1] * gn * xt_ref[sl, :].astype(f32)
        return acc + jnp.sum(v.reshape(big // 8, 8, toks), axis=0)

    back = jnp.sum(lax.fori_loop(0, nbig, first_back, zero8), axis=0, keepdims=True) * (1.0 / width)
    back = back * (r1 * r1 * r1)
    do(tail_at + 6)

    def first_norm(sl, carry):
        v = xt_ref[sl, :].astype(f32)
        gn = acc_o[sl, :]
        prod = gn * v * r1
        hi = prod.astype(bf16)
        wg2[sl, :] = hi
        wu2[sl, :] = (prod - hi.astype(f32)).astype(bf16)
        gtok_ref[sl, :] = (acc_n[sl, :] + r1 * gcol[sl, 0:1] * gn - v * back).astype(bf16)
        return carry

    over_rows(first_norm, 0)
    sms[0, :, 0:width] += token_sums(0)
    rest = doff[...]
    table = jnp.zeros((8, onehot.shape[0]), f32)
    for _ in range(3):
        part = rest.astype(bf16)
        table = table + dot_nt(part, onehot[...])
        rest = rest - part.astype(f32)
    sms[0, :, sms.shape[2] - onehot.shape[0] : sms.shape[2]] = table
    small_send(0)
    for k in range(7, TAIL_SLOTS):
        do(tail_at + k)
        for step in {7: (0,), 8: (1,), 9: (2, 3), 10: (4, 5)}.get(k, ()):
            small_step(step)

    settle(gland.at[pl.ds(0, 7)], gain_s)
    slot_free(nv)
    slot_free(nq)
    turn_free(nv)
    turn_free(nq)
    for n in range(total):
        settle(span(hop_ref, 0, 4, width_of(n)), e1s.at[n])
    lax.fori_loop(0, chunks, lambda k, carry: (gather_sent(("f", k)), carry)[1], 0)

    @pl.when(outer)
    def _():
        for n in (nv, nq):
            settle(span(vbuf, (n % 2) * 2, 2, aw), zis.at[n])
        for n in range(total):
            for half in (0, 1):
                settle(cut1(ubuf, 0, width_of(n)), ur.at[n, half])

    @pl.when(inner)
    def _():
        for n in (nv, nq):
            u_free(n, aw)
        for n in range(total):
            settle(cut1(ubuf, 0, width_of(n)), ur.at[n, 1 - c])


def fused(tokens, cotangent, buckets, bias_table, gains, weights):
    toks, width = tokens.shape
    heads = bias_table.shape[1]
    rows, aw = weights[0].shape
    ff = weights[4].shape[1]
    sub = 256
    fw = 3 * sub
    chunks = ff // (2 * sub)
    total = chunks + 2
    lanes = 2 * toks
    small_lanes = (width + 127) // 128 * 128 + 128
    padded = jnp.concatenate([buckets, jnp.full((1,), -1, jnp.int32)])
    turned = jnp.concatenate([buckets[::-1], jnp.full((1,), -1, jnp.int32)])
    bucket_rows = jnp.concatenate([turned[None], padded[None], jnp.full((6, lanes), -1, jnp.int32)])
    table = jnp.pad(bias_table.T, ((0, 8 - heads), (0, 128 - bias_table.shape[0])))
    vm = pl.BlockSpec(memory_space=pltpu.VMEM)
    hbm = pl.BlockSpec(memory_space=pltpu.HBM)
    dma = pltpu.SemaphoreType.DMA
    tok = lambda kind: pltpu.VMEM((width, toks), kind)
    inner_rows = pltpu.VMEM((aw, toks), bf16)
    blocks = lambda count: pltpu.VMEM((count, rows, fw), bf16)
    return pl.pallas_call(
        functools.partial(fused_kernel, chunks=chunks, heads=heads),
        out_shape=(
            jax.ShapeDtypeStruct((width, toks), bf16),
            jax.ShapeDtypeStruct((width, toks), bf16),
            jax.ShapeDtypeStruct((8, small_lanes), f32),
            *([jax.ShapeDtypeStruct((rows, aw), bf16)] * 4),
            *([jax.ShapeDtypeStruct((rows, ff), bf16)] * 3),
            jax.ShapeDtypeStruct((chunks * 16, rows, fw), bf16),
            jax.ShapeDtypeStruct((total * 8, rows, fw), bf16),
            jax.ShapeDtypeStruct((total * 4, rows, fw), bf16),
            jax.ShapeDtypeStruct((total * 2, rows, fw), bf16),
        ),
        in_specs=[vm] * 5 + [hbm] * 7,
        out_specs=[vm] * 3 + [hbm] * 11,
        scratch_shapes=[
            pltpu.VMEM((8, rows, 128), bf16),
            pltpu.VMEM((width, 128), f32),
            tok(bf16),
            tok(bf16),
            tok(f32),
            tok(f32),
            tok(f32),
            *([inner_rows] * 8),
            *([pltpu.VMEM((width, aw), bf16)] * 4),
            *([pltpu.VMEM((width, 2 * sub), bf16)] * 3),
            pltpu.VMEM((32, rows, sub), bf16),
            blocks(32),
            *([pltpu.VMEM((toks, 2 * sub), bf16)] * 3),
            blocks(16),
            blocks(8),
            blocks(6),
            *([blocks(4)] * 4),
            pltpu.VMEM((8, lanes), f32),
            pltpu.VMEM((128, lanes), bf16),
            pltpu.VMEM((8, lanes), f32),
            pltpu.VMEM((6, 8, small_lanes), f32),
            pltpu.VMEM((6, 8, small_lanes), f32),
            dma(()),
            dma(()),
            *([dma((total,))] * 5),
            dma((4,)),
            *([dma((total,))] * 2),
            dma((total, 8)),
            dma((6,)),
            dma((total,)),
            dma((total, 2)),
            *([dma((total,))] * 6),
            dma((total, 3)),
            dma((total,)),
            dma((total, 2)),
            dma((6,)),
            dma((6,)),
            pltpu.SemaphoreType.REGULAR,
        ],
        compiler_params=pltpu.CompilerParams(
            collective_id=0, has_side_effects=True, vmem_limit_bytes=60 * 2**20
        ),
        cost_estimate=pl.CostEstimate(flops=57 * 10**9, bytes_accessed=10**8, transcendentals=10**7),
    )(tokens.T, cotangent.T, bucket_rows, table, gains, *weights)


def fused_body(
    tokens,
    cotangent,
    buckets,
    bias_table,
    attn_gain,
    w_query,
    w_key,
    w_value,
    w_output,
    ffn_gain,
    w_gate,
    w_up,
    w_down,
):
    rows = w_query.shape[0]
    gains = jnp.pad(jnp.stack([attn_gain, ffn_gain], axis=1), ((0, 0), (0, 126)))
    weights = (w_query, w_key, w_value, w_output, w_gate, w_up, w_down)
    out, gtok, small, *grads = fused(tokens, cotangent, buckets, bias_table, gains, weights)
    grads = [grad.astype(f32) for grad in grads[:7]]
    own = lax.dynamic_slice(small, (0, lax.axis_index("shard") * rows), (2, rows))
    table = small[0 : bias_table.shape[1], small.shape[1] - 128 :][:, 0 : bias_table.shape[0]].T
    return (out.T, gtok.T, own[0], *grads[:4], own[1], *grads[4:], table)


def solution(mesh):
    chosen = body
    if mesh.shape["shard"] == 8 and mesh.shape["rep"] == 4:
        chosen = fused_body
    return jax.shard_map(
        chosen,
        mesh=mesh,
        in_specs=(
            P(("shard", "rep"), None),
            P(("shard", "rep"), None),
            P(),
            P(),
            P("shard"),
            P("shard", None),
            P("shard", None),
            P("shard", None),
            P("shard", None),
            P("shard"),
            P("shard", None),
            P("shard", None),
            P("shard", None),
        ),
        out_specs=(
            P(("shard", "rep"), None),
            P(("shard", "rep"), None),
            P("shard"),
            P("shard", None),
            P("shard", None),
            P("shard", None),
            P("shard", None),
            P("shard"),
            P("shard", None),
            P("shard", None),
            P("shard", None),
            P(),
        ),
        check_vma=False,
    )
```

```python
import functools

import jax
import jax.numpy as jnp
from jax import lax
from jax.experimental import pallas as pl
from jax.experimental.pallas import tpu as pltpu
from jax.sharding import PartitionSpec as P

BLOCK = 256
MESH = pl.DeviceIdType.MESH
f32 = jnp.float32
bf16 = jnp.bfloat16


norm_eps = 1e-06
masked_score = -1e30
highest = lax.Precision.HIGHEST


def norm_local(row_values, gain_vector):
    return (
        row_values
        * lax.rsqrt(jnp.mean(row_values * row_values, axis=-1, keepdims=True) + norm_eps)
        * gain_vector
    )


def gelu_tanh(values_in):
    return jax.nn.gelu(values_in, approximate=True)


def diagonal_total(matrix):
    head_count, row_count, key_count = matrix.shape
    flipped = matrix[:, :, ::-1]
    padded = jnp.concatenate(
        [flipped, jnp.zeros((head_count, row_count, row_count), jnp.float32)], axis=2
    )
    flat_rows = padded.reshape(head_count, row_count * (key_count + row_count))
    flat_rows = flat_rows[:, : row_count * (key_count + row_count - 1)]
    return jnp.sum(flat_rows.reshape(head_count, row_count, key_count + row_count - 1), axis=1)


def toeplitz_grid(offset_bias, row_count, length):
    head_count = offset_bias.shape[0]
    span = length + row_count - 1
    flipped = offset_bias[:, ::-1]
    rotated = jnp.concatenate([flipped[:, row_count - 1 :], flipped[:, : row_count - 1]], axis=1)
    tiled = jnp.tile(rotated, (1, row_count))[:, : row_count * (span - 1)]
    return tiled.reshape(head_count, row_count, span - 1)[:, :, :length]


def body(
    tokens,
    cotangent,
    buckets,
    bias_table,
    attn_gain,
    w_query,
    w_key,
    w_value,
    w_output,
    ffn_gain,
    w_gate,
    w_up,
    w_down,
):
    length = tokens.shape[0]
    bucket_count = bias_table.shape[0]
    head_count = bias_table.shape[1]
    inner_width = w_query.shape[1]
    ff_width = w_gate.shape[1]
    owner_rows = w_query.shape[0]
    head_size = inner_width // head_count
    block_rows = min(512, length)
    block_count = length // block_rows
    residual = tokens.astype(jnp.float32)
    attn_set = (
        lax.all_gather(attn_gain, "shard", axis=0, tiled=True),
        lax.all_gather(w_query, "shard", axis=0, tiled=True),
        lax.all_gather(w_key, "shard", axis=0, tiled=True),
        lax.all_gather(w_value, "shard", axis=0, tiled=True),
        lax.all_gather(w_output, "shard", axis=0, tiled=True),
    )
    gain_one = attn_set[0].astype(jnp.float32)
    normed_one = norm_local(residual, gain_one).astype(jnp.bfloat16)

    def project(weight):
        product = jnp.dot(normed_one, weight, preferred_element_type=jnp.float32)
        return product.astype(jnp.bfloat16).reshape(length, head_count, head_size)

    queries = project(attn_set[1])
    key_rows = project(attn_set[2])
    value_rows = project(attn_set[3])
    one_hot = (buckets[:, None] == jnp.arange(bucket_count, dtype=jnp.int32)[None, :]).astype(
        jnp.float32
    )
    offset_bias = jnp.dot(one_hot, bias_table.astype(jnp.float32), precision=highest).T
    block_starts = jnp.arange(block_count, dtype=jnp.int32) * block_rows
    key_index = jnp.arange(length, dtype=jnp.int32)

    def block_scores(first_row, query_block):
        query_index = first_row + jnp.arange(block_rows, dtype=jnp.int32)
        bias_grid = toeplitz_grid(offset_bias, block_rows, length)
        scores = (
            jnp.einsum("qhd,khd->hqk", query_block, key_rows, preferred_element_type=jnp.float32)
            + bias_grid
        )
        allowed = key_index[None, :] // BLOCK <= query_index[:, None] // BLOCK
        return jnp.where(allowed[None], scores, masked_score)

    def attend(first_row):
        scores = block_scores(first_row, queries)
        row_max = jnp.max(scores, axis=-1, keepdims=True)
        exp_scores = jnp.exp(scores - row_max)
        totals = jnp.sum(exp_scores, axis=-1, keepdims=True)
        probability = (exp_scores / totals).astype(jnp.bfloat16)
        mixed_rows = jnp.einsum(
            "hqk,khd->qhd", probability, value_rows, preferred_element_type=jnp.float32
        )
        return (mixed_rows, (row_max + jnp.log(totals))[..., 0])

    mixed_blocks, log_totals = lax.map(attend, block_starts)
    attended = mixed_blocks.reshape(length, inner_width).astype(jnp.bfloat16)
    middle = residual + jnp.einsum(
        "ti,di->td", attended, attn_set[4], preferred_element_type=jnp.float32
    )
    ffn_set = (
        lax.all_gather(ffn_gain, "shard", axis=0, tiled=True),
        lax.all_gather(w_gate, "shard", axis=0, tiled=True),
        lax.all_gather(w_up, "shard", axis=0, tiled=True),
        lax.all_gather(w_down, "shard", axis=0, tiled=True),
    )
    gain_two = ffn_set[0].astype(jnp.float32)
    normed_two = norm_local(middle, gain_two).astype(jnp.bfloat16)
    gate_values = jnp.dot(normed_two, ffn_set[1], preferred_element_type=jnp.float32)
    up_values = jnp.dot(normed_two, ffn_set[2], preferred_element_type=jnp.float32)
    activated, gelu_pullback = jax.vjp(gelu_tanh, gate_values)
    hidden = (activated * up_values).astype(jnp.bfloat16)
    layer_out = (
        middle + jnp.einsum("tf,df->td", hidden, ffn_set[3], preferred_element_type=jnp.float32)
    ).astype(jnp.bfloat16)
    ffn_set = (
        lax.all_gather(ffn_gain, "shard", axis=0, tiled=True),
        lax.all_gather(w_gate, "shard", axis=0, tiled=True),
        lax.all_gather(w_up, "shard", axis=0, tiled=True),
        lax.all_gather(w_down, "shard", axis=0, tiled=True),
    )
    grad_w_down = jnp.einsum("td,tf->df", cotangent, hidden, preferred_element_type=jnp.float32)
    grad_hidden = jnp.dot(cotangent, ffn_set[3], preferred_element_type=jnp.float32)
    grad_gate = gelu_pullback(grad_hidden * up_values)[0].astype(jnp.bfloat16)
    grad_up = (grad_hidden * activated).astype(jnp.bfloat16)
    grad_w_gate = jnp.einsum("td,tf->df", normed_two, grad_gate, preferred_element_type=jnp.float32)
    grad_w_up = jnp.einsum("td,tf->df", normed_two, grad_up, preferred_element_type=jnp.float32)
    grad_normed_two = jnp.einsum(
        "tf,df->td", grad_gate, ffn_set[1], preferred_element_type=jnp.float32
    )
    grad_normed_two = grad_normed_two + jnp.einsum(
        "tf,df->td", grad_up, ffn_set[2], preferred_element_type=jnp.float32
    )
    middle_part, grad_gain_two = jax.vjp(norm_local, middle, gain_two)[1](grad_normed_two)
    grad_middle = cotangent.astype(jnp.float32) + middle_part
    ffn_shards = (
        lax.psum_scatter(grad_w_gate.astype(jnp.bfloat16), "shard", scatter_dimension=0, tiled=True),
        lax.psum_scatter(grad_w_up.astype(jnp.bfloat16), "shard", scatter_dimension=0, tiled=True),
        lax.psum_scatter(grad_w_down.astype(jnp.bfloat16), "shard", scatter_dimension=0, tiled=True),
    )
    attn_set = (
        lax.all_gather(attn_gain, "shard", axis=0, tiled=True),
        lax.all_gather(w_query, "shard", axis=0, tiled=True),
        lax.all_gather(w_key, "shard", axis=0, tiled=True),
        lax.all_gather(w_value, "shard", axis=0, tiled=True),
        lax.all_gather(w_output, "shard", axis=0, tiled=True),
    )
    grad_branch = grad_middle.astype(jnp.bfloat16)
    grad_w_output = jnp.einsum(
        "td,ti->di", grad_branch, attended, preferred_element_type=jnp.float32
    )
    grad_attended = jnp.einsum(
        "td,di->ti", grad_branch, attn_set[4], preferred_element_type=jnp.float32
    )
    grad_attended = grad_attended.astype(jnp.bfloat16).reshape(length, head_count, head_size)

    def attend_back(carried, block_input):
        grad_keys, grad_values, grad_offsets = carried
        first_row, log_total = block_input
        scores = block_scores(first_row, queries)
        probability = jnp.exp(scores - log_total[..., None])
        grad_probs = jnp.einsum(
            "qhd,khd->hqk", grad_attended, value_rows, preferred_element_type=jnp.float32
        )
        inner_sum = jnp.sum(probability * grad_probs, axis=-1, keepdims=True)
        grad_scores = (probability * (grad_probs - inner_sum)).astype(jnp.bfloat16)
        grad_values = grad_values + jnp.einsum(
            "hqk,qhd->khd",
            probability.astype(jnp.bfloat16),
            grad_attended,
            preferred_element_type=jnp.float32,
        )
        grad_keys = grad_keys + jnp.einsum(
            "hqk,qhd->khd", grad_scores, queries, preferred_element_type=jnp.float32
        )
        grad_queries = jnp.einsum(
            "hqk,khd->qhd", grad_scores, key_rows, preferred_element_type=jnp.float32
        )
        diagonal_sums = diagonal_total(grad_scores.astype(jnp.float32))
        offset_piece = grad_offsets
        grad_offsets = offset_piece + diagonal_sums
        return ((grad_keys, grad_values, grad_offsets), grad_queries)

    zero_rows = jnp.zeros((length, head_count, head_size), jnp.float32)
    zero_offsets = jnp.zeros((head_count, 2 * length - 1), jnp.float32)
    (grad_keys, grad_values, grad_offsets), query_blocks = lax.scan(
        attend_back, (zero_rows, zero_rows, zero_offsets), (block_starts, log_totals)
    )
    grad_queries = query_blocks.reshape(length, inner_width).astype(jnp.bfloat16)
    grad_keys = grad_keys.reshape(length, inner_width).astype(jnp.bfloat16)
    grad_values = grad_values.reshape(length, inner_width).astype(jnp.bfloat16)
    grad_w_query = jnp.einsum(
        "td,ti->di", normed_one, grad_queries, preferred_element_type=jnp.float32
    )
    grad_w_key = jnp.einsum("td,ti->di", normed_one, grad_keys, preferred_element_type=jnp.float32)
    grad_w_value = jnp.einsum(
        "td,ti->di", normed_one, grad_values, preferred_element_type=jnp.float32
    )
    grad_normed_one = jnp.einsum(
        "ti,di->td", grad_queries, attn_set[1], preferred_element_type=jnp.float32
    )
    grad_normed_one = grad_normed_one + jnp.einsum(
        "ti,di->td", grad_keys, attn_set[2], preferred_element_type=jnp.float32
    )
    grad_normed_one = grad_normed_one + jnp.einsum(
        "ti,di->td", grad_values, attn_set[3], preferred_element_type=jnp.float32
    )
    rows_part, grad_gain_one = jax.vjp(norm_local, residual, gain_one)[1](grad_normed_one)
    grad_tokens = (grad_middle + rows_part).astype(jnp.bfloat16)
    grad_table = jnp.dot(grad_offsets, one_hot, precision=highest).T
    owner_start = lax.axis_index("shard") * owner_rows
    attn_shards = (
        lax.psum_scatter(grad_w_query.astype(jnp.bfloat16), "shard", scatter_dimension=0, tiled=True),
        lax.psum_scatter(grad_w_key.astype(jnp.bfloat16), "shard", scatter_dimension=0, tiled=True),
        lax.psum_scatter(grad_w_value.astype(jnp.bfloat16), "shard", scatter_dimension=0, tiled=True),
        lax.psum_scatter(grad_w_output.astype(jnp.bfloat16), "shard", scatter_dimension=0, tiled=True),
    )
    summed = lax.psum(
        (
            attn_shards[0],
            attn_shards[1],
            attn_shards[2],
            attn_shards[3],
            ffn_shards[0],
            ffn_shards[1],
            ffn_shards[2],
        ),
        "rep",
    )
    small_total = lax.psum((grad_gain_one, grad_gain_two, grad_table), ("shard", "rep"))
    gain_one_own = lax.dynamic_slice_in_dim(small_total[0], owner_start, owner_rows, 0)
    gain_two_own = lax.dynamic_slice_in_dim(small_total[1], owner_start, owner_rows, 0)
    return (
        layer_out,
        grad_tokens,
        gain_one_own,
        summed[0].astype(jnp.float32),
        summed[1].astype(jnp.float32),
        summed[2].astype(jnp.float32),
        summed[3].astype(jnp.float32),
        gain_two_own,
        summed[4].astype(jnp.float32),
        summed[5].astype(jnp.float32),
        summed[6].astype(jnp.float32),
        small_total[2],
    )

HEAD_SLOTS = 7
TAIL_SLOTS = 14
HELPED = (1, 2, 3, 4, 5, 6)
SLOTS = {
    "send": (0, 0, 0, 2, 2, 2, 2),
    "forward": (1, 1, 1, 6, 7, 8, 11),
    "swap": (2, 3, 4, 8, 10, 11, 17),
    "get_forward": (1, 6, 7, 10, 11, 15, 16),
    "get_swap": (3, 8, 9, 11, 13, 16, 18),
    "turn": (10, 12, 15, 16, 20, 21, 24, 27, 29),
    "rep": (13, 14, 19, 20, 23, 25, 26, 30, 31),
    "mid": (17, 18, 20, 22, 24, 26, 29, 31, 32),
    "last": (18, 21, 23, 24, 25, 28, 30, 32, 33),
}


def dot_nn(a, b):
    return lax.dot_general(a, b, (((1,), (0,)), ((), ())), preferred_element_type=f32)


def dot_nt(a, b):
    return lax.dot_general(a, b, (((1,), (1,)), ((), ())), preferred_element_type=f32)


def dot_tn(a, b):
    return lax.dot_general(a, b, (((0,), (0,)), ((), ())), preferred_element_type=f32)


def fused_kernel(
    xt_ref,
    ct_ref,
    buckets_ref,
    table_ref,
    gains_ref,
    wq_ref,
    wk_ref,
    wv_ref,
    wo_ref,
    wg_ref,
    wu_ref,
    wd_ref,
    out_ref,
    gtok_ref,
    small_ref,
    gq_ref,
    gk_ref,
    gv_ref,
    go_ref,
    gg_ref,
    gu_ref,
    gd_ref,
    land_ref,
    sum_ref,
    hop_ref,
    turn_ref,
    gland,
    gcol,
    n1t,
    n2t,
    mid,
    acc_o,
    acc_n,
    qt,
    kt,
    vt,
    att,
    dat,
    dvt,
    wq,
    wk,
    wv,
    wo,
    wg2,
    wu2,
    wd2,
    wload,
    g,
    hid,
    dgt,
    dup,
    rc,
    stage_t,
    stage_v,
    vbuf,
    zi,
    zm,
    ubuf,
    revb,
    onehot,
    doff,
    sms,
    smr,
    gain_s,
    gain_r,
    gsend,
    gloc,
    g1r,
    g2r,
    gpr,
    load_sem,
    e0s,
    e0r,
    sum_sem,
    stage_sem,
    e1s,
    e1r,
    e2s,
    e2r,
    zis,
    zir,
    zms,
    zmr,
    us,
    ul,
    ur,
    sss,
    ssr,
    zcredit,
    mcredit,
    *,
    chunks,
    heads,
):
    width = xt_ref.shape[0]
    toks = xt_ref.shape[1]
    rows = gains_ref.shape[0]
    fw = land_ref.shape[2]
    sub = fw // 3
    aw = wq_ref.shape[1]
    hs = aw // heads
    total = chunks + 2
    eps = 1e-06
    lanes = revb.shape[1]
    big = 2 * rows
    nbig = width // big

    s = lax.axis_index("shard")
    r = lax.axis_index("rep")
    c = s % 2
    x = (s // 2) % 2
    y = s // 4
    sc = s + 1 - 2 * c
    sx = s + 2 - 4 * x
    sy = s + 4 - 8 * y
    bx = sx - c
    by = sy - c
    bd = (1 - y) * 4 + (1 - x) * 2
    b_own = s - c
    mate = r + 1 - 2 * (r % 2)
    inner = (r == 1) | (r == 2)
    outer = (r == 0) | (r == 3)

    def remote(src, dst, ssem, rsem, dev):
        return pltpu.make_async_remote_copy(
            src_ref=src, dst_ref=dst, send_sem=ssem, recv_sem=rsem, device_id=dev, device_id_type=MESH
        )

    def settle(ref, sem):
        pltpu.make_async_copy(ref, ref, sem).wait()

    barrier = pltpu.get_barrier_semaphore()
    near = [(sc, r), (bx, r), (bx + 1, r), (by, r), (by + 1, r), (bd, r), (bd + 1, r), (s, mate), (sc, mate)]
    for dev in near:
        pl.semaphore_signal(barrier, inc=1, device_id=dev, device_id_type=MESH)

    @pl.when(inner)
    def _():
        pl.semaphore_signal(barrier, inc=1, device_id=(s, 3 - r), device_id_type=MESH)

    @pl.when(inner)
    def _():
        pl.semaphore_wait(barrier, len(near) + 1)

    @pl.when(outer)
    def _():
        pl.semaphore_wait(barrier, len(near))

    def place(chunk, index):
        kind, k = chunk
        if kind == "a":
            return g.at[16 + index, :, pl.ds(k * aw, aw)]
        return land_ref.at[k * 16 + index]

    def places(chunk, count):
        kind, k = chunk
        if kind == "a":
            return g.at[pl.ds(16, count), :, pl.ds(k * aw, aw)]
        return land_ref.at[pl.ds(0, count)]

    def any_of(value, options):
        return functools.reduce(jnp.logical_or, [value == option for option in options], jnp.bool_(False))

    def helped(chunk):
        kind, k = chunk
        return False if kind == "a" else any_of(k, HELPED)

    def active(chunk):
        kind, k = chunk
        return True if kind == "a" else jnp.logical_not(any_of(k, HELPED)) | (r % 2 == k % 2)

    def when(condition, then):
        if condition is True:
            then()
        elif condition is not False:
            pl.when(condition)(then)

    def columns(k, half):
        return pl.ds(pl.multiple_of((2 * k + half) * sub, sub), sub)

    def own_parts(chunk, half):
        kind, k = chunk
        dst = place(chunk, half * 8 + s)
        if kind == "a":
            return [(((wq_ref, wk_ref), (wv_ref, wo_ref))[k][half], dst)]
        return [
            (ref.at[:, columns(k, half)], dst.at[:, pl.ds(j * sub, sub)]) for j, ref in enumerate((wg_ref, wu_ref, wd_ref))
        ]

    def at(chunk):
        kind, k = chunk
        return k if kind == "a" else k + 2

    def gather_send(chunk):
        i = at(chunk)

        def cross():
            for half in (0, 1):
                for src, dst in own_parts(chunk, half):
                    remote(src, dst, gsend.at[i], g1r.at[i], (bx + half, r)).start()
                    remote(src, dst, gsend.at[i], g1r.at[i], (by + half, r)).start()

        when(active(chunk), cross)
        for half in (0, 1):
            for src, dst in own_parts(chunk, half):
                remote(src, dst, gsend.at[i], gpr.at[i], (sc, r)).start()
                pltpu.make_async_copy(src, dst, gloc.at[i]).start()

    def hand_over(chunk, blocks, sem):
        i = at(chunk)

        def hand():
            for b in blocks:
                spot = place(chunk, c * 8 + b)
                remote(spot, spot, gsend.at[i], sem.at[i], (s, mate)).start()

        if chunk[0] == "f":
            pl.when(helped(chunk) & active(chunk))(hand)
        for b in blocks:
            spot = place(chunk, c * 8 + b)
            remote(spot, spot, gsend.at[i], gpr.at[i], (sc, r)).start()

    def gather_forward(chunk):
        i = at(chunk)
        settle(places(chunk, 4), g1r.at[i])

        def cross():
            one = place(chunk, c * 8 + bx)
            two = place(chunk, c * 8 + by + 1)
            remote(one, one, gsend.at[i], g2r.at[i], (sy, r)).start()
            remote(two, two, gsend.at[i], g2r.at[i], (sx, r)).start()

        when(active(chunk), cross)
        hand_over(chunk, (bx, bx + 1, by, by + 1), g1r)

    def gather_swap(chunk):
        settle(places(chunk, 2), g2r.at[at(chunk)])
        hand_over(chunk, (bd, bd + 1), g2r)

    def gather_done(chunk):
        i = at(chunk)
        settle(places(chunk, 8), gpr.at[i])
        settle(places(chunk, 2), gloc.at[i])

    def gather_sent(chunk):
        i = at(chunk)
        does = active(chunk)
        if does is True:
            settle(places(chunk, 14), gsend.at[i])
            return
        pl.when(does & helped(chunk))(lambda: settle(places(chunk, 20), gsend.at[i]))
        pl.when(does & jnp.logical_not(helped(chunk)))(lambda: settle(places(chunk, 14), gsend.at[i]))
        pl.when(jnp.logical_not(does))(lambda: settle(places(chunk, 8), gsend.at[i]))

    def ahead(stage, k, mine):
        chunk = ("f", k)
        does = active(chunk) if mine else jnp.logical_not(active(chunk))
        pl.when((k < chunks) & does)(lambda: stage(chunk))

    def cut(ref, w):
        return ref if w == fw else ref.at[:, :, pl.ds(0, w)]

    def cut1(ref, index, w):
        return ref.at[index] if w == fw else ref.at[index, :, pl.ds(0, w)]

    def span(ref, start, count, w):
        return ref.at[pl.ds(start, count)] if w == fw else ref.at[pl.ds(start, count), :, pl.ds(0, w)]

    def get(ref, index, w):
        return ref[index] if w == fw else ref[index, :, 0:w]

    def put(ref, index, w, value):
        if w == fw:
            ref[index] = value
        else:
            ref[index, :, 0:w] = value

    def add_to(dst, i, src, j, w):
        put(dst, i, w, get(dst, i, w) + get(src, j, w))

    def core_part(n, b, count, w):
        slot = n % 2
        remote(
            span(g, slot * 16 + (1 - c) * 8 + b, count, w), span(rc, slot * 8 + b, count, w), e0s.at[n], e0r.at[n], (sc, r)
        ).start()

    def plane_send(n, w):
        slot = n % 2
        base = slot * 16 + c * 8
        settle(span(rc, slot * 8, 8, w), e0r.at[n])
        order = []
        for k, kx, ky in ((0, 1 - y, 1 - x), (1, y, x)):
            order.append((4 * kx + 2 * (1 - x), sx, 2 * k))
            order.append((4 * (1 - y) + 2 * ky + 1, sy, 2 * k + 1))
        order += [(b, None, None) for b in (4 * (1 - y) + 2 * x, 4 * y + 2 * (1 - x) + 1, b_own, b_own + 1)]

        def store(i):
            b = order[i][0]
            return pltpu.make_async_copy(cut1(g, base + b, w), cut1(sum_ref, n * 8 + b, w), sum_sem.at[n, i])

        for i, (b, _, _) in enumerate(order):
            add_to(g, base + b, rc, slot * 8 + b, w)
            store(i).start()
        for i, (b, dev, spot) in enumerate(order[:4]):
            store(i).wait()
            remote(
                cut1(sum_ref, n * 8 + b, w), cut1(hop_ref, n * 4 + spot, w), e1s.at[n], e1r.at[n, spot // 2], (dev, r)
            ).start()

    def stored(n, w):
        for i in range(4, 8):
            settle(cut1(sum_ref, 0, w), sum_sem.at[n, i])

    def slot_free(n):
        settle(span(g, 0, 8, width_of(n)), e0s.at[n])

    def turn_free(n):
        settle(span(turn_ref, 0, 2, width_of(n)), e2s.at[n])

    def guarded(n, least, then):
        if isinstance(n, int):
            if n >= least:
                then()
        else:
            pl.when(n >= least)(then)

    def turn_loads(n, w):
        base = (n % 2) * 4
        first = n * 8 + 4 * (1 - y) + 2 * x
        second = n * 8 + 4 * y + 2 * (1 - x) + 1
        return [
            pltpu.make_async_copy(cut1(sum_ref, first, w), cut1(stage_t, base, w), stage_sem.at[0]),
            pltpu.make_async_copy(cut1(sum_ref, second, w), cut1(stage_t, base + 1, w), stage_sem.at[1]),
            pltpu.make_async_copy(span(hop_ref, n * 4, 2, w), span(stage_t, base + 2, 2, w), stage_sem.at[2]),
        ]

    def turn_start(n, w):
        guarded(n, 2, lambda: turn_free(n - 2))
        settle(span(hop_ref, 0, 2, w), e1r.at[n, 0])
        for load in turn_loads(n, w):
            load.start()

    def turn_end(n, w):
        base = (n % 2) * 4
        for load in turn_loads(n, w):
            load.wait()
        for j, dev in ((0, sy), (1, sx)):
            add_to(stage_t, base + j, stage_t, base + 2 + j, w)
            remote(cut1(stage_t, base + j, w), cut1(turn_ref, n * 2 + j, w), e2s.at[n], e2r.at[n], (dev, r)).start()

    def rep_loads(n, w):
        return [
            pltpu.make_async_copy(span(sum_ref, n * 8 + b_own, 2, w), span(stage_v, 0, 2, w), stage_sem.at[3]),
            pltpu.make_async_copy(span(hop_ref, n * 4 + 2, 2, w), span(stage_v, 2, 2, w), stage_sem.at[4]),
            pltpu.make_async_copy(span(turn_ref, n * 2, 2, w), span(stage_v, 4, 2, w), stage_sem.at[5]),
        ]

    def rep_start(n, w):
        settle(span(hop_ref, 0, 2, w), e1r.at[n, 1])
        settle(span(turn_ref, 0, 2, w), e2r.at[n])
        for load in rep_loads(n, w):
            load.start()

    def rep_end(n, w):
        third = n % 3

        def outer_room():
            guarded(n, 3, lambda: pl.when(outer)(lambda: sent(vbuf, zis, n - 3)))
            guarded(n, 2, lambda: pl.when(outer)(lambda: pl.semaphore_wait(zcredit, 1)))

        outer_room()
        for load in rep_loads(n, w):
            load.wait()
        for j in (c, 1 - c):
            value = get(stage_v, j, w).astype(f32) + get(stage_v, 2 + j, w).astype(f32)
            value = value + get(stage_v, 4 + j, w).astype(f32)
            put(vbuf, third * 2 + j, w, value.astype(bf16))

            @pl.when(outer)
            def _():
                remote(
                    cut1(vbuf, third * 2 + j, w), cut1(zi, (n % 2) * 2 + j, w), zis.at[n, j], zir.at[n, j], (s, mate)
                ).start()

    def sent(ref, sems, n):
        for j in (0, 1):
            settle(cut1(ref, 0, width_of(n)), sems.at[n, j])

    def width_of(n):
        return fw if not isinstance(n, int) or n < chunks else aw

    def rep_turn(n, w):
        third = n % 3

        @pl.when(inner)
        def _():
            guarded(n, 3, lambda: pl.semaphore_wait(mcredit, 1))
            for j in (c, 1 - c):
                settle(cut1(zi, j, w), zir.at[n, j])
                add_to(vbuf, third * 2 + j, zi, (n % 2) * 2 + j, w)
                remote(
                    cut1(vbuf, third * 2 + j, w), cut1(zm, third * 2 + j, w), zms.at[n, j], zmr.at[n, j], (s, 3 - r)
                ).start()
            guarded(total - 1 - n, 2, lambda: give_credit(zcredit, (s, mate)))

    def give_credit(sem, dev):
        pl.semaphore_signal(sem, inc=1, device_id=dev, device_id_type=MESH)

    def result(n, half, block):
        if isinstance(n, int) and n >= chunks:
            return [(block, ((gv_ref, go_ref), (gq_ref, gk_ref))[n - chunks][half])]
        return [
            (block.at[:, pl.ds(j * sub, sub)], ref.at[:, columns(n, half)])
            for j, ref in enumerate((gg_ref, gu_ref, gd_ref))
        ]

    def u_free(n, w):
        slot = n % 2
        for k in (0, 1, 2):
            settle(cut1(ubuf, slot * 2, w), us.at[n, k])
        settle(cut1(ubuf, slot * 2, w), ul.at[n])

    def rep_last(n, w):
        slot = n % 2
        third = n % 3

        @pl.when(inner)
        def _():
            guarded(n, 2, lambda: u_free(n - 2, width_of(n - 2)))

            def both(j):
                settle(cut1(zm, j, w), zmr.at[n, j])
                value = get(vbuf, third * 2 + j, w).astype(f32) + get(zm, third * 2 + j, w).astype(f32)
                put(ubuf, slot * 2 + j, w, value.astype(bf16))

            def finish_keep(half):
                for src, dst in result(n, half, cut1(ubuf, slot * 2 + c, w)):
                    remote(src, dst, us.at[n, 0], ur.at[n, half], (s, mate)).start()
                    pltpu.make_async_copy(src, dst, ul.at[n]).start()

            def finish_give(half):
                for src, dst in result(n, half, cut1(ubuf, slot * 2 + 1 - c, w)):
                    remote(src, dst, us.at[n, 1], ur.at[n, half], (sc, mate)).start()
                    remote(src, dst, us.at[n, 2], ur.at[n, half], (sc, r)).start()

            for j, finish in ((c, finish_keep), (1 - c, finish_give)):
                both(j)
                if w == fw:
                    finish(c)
                else:
                    pl.when(c == 0)(functools.partial(finish, 0))
                    pl.when(c == 1)(functools.partial(finish, 1))
            guarded(total - 1 - n, 3, lambda: give_credit(mcredit, (s, 3 - r)))
            sent(vbuf, zms, n)

    def gathers(stage, mine):
        return lambda k: ahead(stage, k, mine)

    def reduces(stage):
        return lambda n: stage(n, width_of(n))

    order = (
        ("swap", gathers(gather_swap, True)),
        ("forward", gathers(gather_forward, True)),
        ("send", lambda k: gather_send(("f", k))),
        ("turn", reduces(turn_start)),
        ("rep", reduces(rep_start)),
        ("last", reduces(rep_last)),
        ("mid", reduces(rep_turn)),
        ("turn", reduces(turn_end)),
        ("rep", reduces(rep_end)),
        ("get_forward", gathers(gather_forward, False)),
        ("get_swap", gathers(gather_swap, False)),
    )
    loop_at = HEAD_SLOTS
    tail_at = HEAD_SLOTS + 2 * chunks

    def do(slot):
        for name, stage in order:
            for n, spot in enumerate(SLOTS[name]):
                if spot == slot:
                    stage(n)

    def do_in_loop(t, side):
        for name, stage in order:
            pairs = [
                ((spot - loop_at) // 2, n)
                for n, spot in enumerate(SLOTS[name])
                if loop_at <= spot < tail_at and (spot - loop_at) % 2 == side
            ]
            if pairs:
                n = sum([jnp.where(t == step, number, 0) for step, number in pairs], jnp.int32(0))
                pl.when(any_of(t, [step for step, _ in pairs]))(functools.partial(stage, n))

    def small_send(step):
        if step < 3:
            dev = ((sc, r), (sx, r), (sy, r))[step]
            remote(sms.at[step], smr.at[step], sss.at[step], ssr.at[step], dev).start()
        elif step == 3:

            @pl.when(outer)
            def _():
                remote(sms.at[3], smr.at[3], sss.at[3], ssr.at[3], (s, mate)).start()
        elif step == 4:

            @pl.when(inner)
            def _():
                remote(sms.at[4], smr.at[4], sss.at[4], ssr.at[4], (s, 3 - r)).start()
        else:

            @pl.when(inner)
            def _():
                remote(sms.at[5], smr.at[5], sss.at[5], ssr.at[5], (s, mate)).start()

    def small_step(step):
        def take():
            settle(smr.at[step], ssr.at[step])
            settle(sms.at[step], sss.at[step])
            if step < 2:
                sms[step + 1] = sms[step] + smr[step]
            elif step == 2:
                sms[3] = sms[2] + smr[2]

        if step < 3:
            take()
            small_send(step + 1)
        elif step == 3:

            @pl.when(inner)
            def _():
                settle(smr.at[3], ssr.at[3])
                sms[4] = sms[3] + smr[3]

            @pl.when(outer)
            def _():
                settle(sms.at[3], sss.at[3])

            small_send(4)
        elif step == 4:

            @pl.when(inner)
            def _():
                settle(smr.at[4], ssr.at[4])
                settle(sms.at[4], sss.at[4])
                sms[5] = sms[4] + smr[4]
                small_ref[...] = sms[5]

            small_send(5)
        else:

            @pl.when(inner)
            def _():
                settle(sms.at[5], sss.at[5])

            @pl.when(outer)
            def _():
                settle(smr.at[5], ssr.at[5])
                small_ref[...] = smr[5]

    tile = 64
    tiles = width // tile

    def over_rows(body, start):
        def step(i, carry):
            return body(pl.ds(pl.multiple_of(i * tile, tile), tile), carry)

        return lax.fori_loop(0, tiles, step, start)

    def fold(value):
        return jnp.sum(value.reshape(tile // 8, 8, toks), axis=0)

    zero8 = jnp.zeros((8, toks), f32)

    gather_send(("a", 0))
    gdst = gland.at[s]
    for k, dev in enumerate([(sc, r), (bx, r), (bx + 1, r), (by, r), (by + 1, r), (bd, r), (bd + 1, r)]):
        remote(gains_ref, gdst, gain_s, gain_r, dev).start()
    pltpu.make_async_copy(gains_ref, gdst, load_sem.at[1]).start()
    gather_send(("a", 1))
    do(0)

    def square_sum(sl, acc):
        v = xt_ref[sl, :].astype(f32)
        return acc + fold(v * v)

    ssum = jnp.sum(over_rows(square_sum, zero8), axis=0, keepdims=True)
    r1 = lax.rsqrt(ssum * (1.0 / width) + eps)

    bucket_index = lax.broadcasted_iota(jnp.int32, (table_ref.shape[1], lanes), 0)
    rev_hot = (bucket_index == buckets_ref[0:1, :]).astype(bf16)
    onehot[...] = (bucket_index == buckets_ref[1:2, :]).astype(bf16)
    revb[...] = dot_nn(table_ref[...], rev_hot)

    settle(gland.at[pl.ds(0, 7)], gain_r)
    settle(gland.at[0], load_sem.at[1])
    for b in range(8):
        gcol[rows * b : rows * (b + 1), :] = gland[b].astype(f32)

    def norm_one(sl, carry):
        v = xt_ref[sl, :].astype(f32)
        n1t[sl, :] = (v * r1 * gcol[sl, 0:1]).astype(bf16)
        return carry

    gather_forward(("a", 0))
    do(1)
    over_rows(norm_one, 0)
    gather_swap(("a", 0))
    gather_forward(("a", 1))
    do(2)

    def compact(dst, half, col):
        @pl.loop(0, nbig)
        def _(i):
            both = jnp.concatenate(
                [
                    g[16 + half * 8 + 2 * i, :, col : col + aw].astype(f32),
                    g[16 + half * 8 + 2 * i + 1, :, col : col + aw].astype(f32),
                ],
                axis=0,
            )
            dst[pl.ds(pl.multiple_of(i * 2 * rows, 16), 2 * rows), :] = both.astype(bf16)

    gather_done(("a", 0))
    compact(wq, 0, 0)
    qt[...] = dot_tn(wq[...], n1t[...]).astype(bf16)
    compact(wk, 1, 0)
    kt[...] = dot_tn(wk[...], n1t[...]).astype(bf16)
    gather_swap(("a", 1))
    do(3)
    gather_done(("a", 1))
    compact(wv, 0, aw)
    vt[...] = dot_tn(wv[...], n1t[...]).astype(bf16)
    compact(wo, 1, aw)
    do(4)

    half_tok = toks // 2

    def softmax_block(h, head, block):
        keys = half_tok * (block + 1)
        low = half_tok * block
        row = jnp.broadcast_to(revb[pl.ds(h, 1), :], (half_tok, lanes))
        bias = pltpu.roll(row, (low + 1 - toks) % lanes, 1, stride=1, stride_axis=0)[:, :keys]
        scores = dot_tn(qt[head, low : low + half_tok], kt[head, 0:keys]) + bias
        e = jnp.exp(scores - jnp.max(scores, axis=1, keepdims=True))
        return e * (1.0 / jnp.sum(e, axis=1, keepdims=True)), low, keys

    def attend(h, carry):
        head = pl.ds(pl.multiple_of(h * hs, hs), hs)
        for block in (0, 1):
            p, low, keys = softmax_block(h, head, block)
            att[head, low : low + half_tok] = dot_nt(vt[head, 0:keys], p.astype(bf16)).astype(bf16)
        return carry

    lax.fori_loop(0, heads // 2, attend, 0)
    do(5)
    lax.fori_loop(heads // 2, heads, attend, 0)
    do(6)

    def branch_one(i, acc):
        sl = pl.ds(pl.multiple_of(i * big, 16), big)
        m = xt_ref[sl, :].astype(f32) + dot_nn(wo[sl, :], att[...])
        mid[sl, :] = m
        return acc + jnp.sum((m * m).reshape(big // 8, 8, toks), axis=0)

    ssum = jnp.sum(lax.fori_loop(0, nbig, branch_one, zero8), axis=0, keepdims=True)
    r2n = lax.rsqrt(ssum * (1.0 / width) + eps)

    def norm_two(sl, carry):
        m = mid[sl, :]
        n2t[sl, :] = (m * r2n * gcol[sl, 1:2]).astype(bf16)
        acc_o[sl, :] = m
        acc_n[sl, :] = jnp.zeros((tile, toks), f32)
        return carry

    over_rows(norm_two, 0)

    tok_tile = toks // 2

    parts = [(half, k) for half in (0, 1) for k in (0, 1, 2)]
    depth = 4

    def load(t, p):
        half, k = parts[p]
        return pltpu.make_async_copy(
            land_ref.at[pl.ds(t * 16 + half * 8, 8), :, pl.ds(k * sub, sub)],
            wload.at[pl.ds((p % depth) * 8, 8)],
            load_sem.at[p % depth],
        )

    def ffn_load(t):
        for p in range(depth):
            load(t, p).start()

    def ffn_chunk(t):
        slot = t % 2
        for p, (half, k) in enumerate(parts):
            load(t, p).wait()
            dst = (wg2, wu2, wd2)[k]

            @pl.loop(0, nbig)
            def _(i):
                base = (p % depth) * 8 + 2 * i
                both = jnp.concatenate([wload[base].astype(f32), wload[base + 1].astype(f32)], axis=0)
                sl = pl.ds(pl.multiple_of(i * big, 16), big)
                dst[sl, half * sub : (half + 1) * sub] = both.astype(bf16)

            if p + depth < len(parts):
                load(t, p + depth).start()

        @pl.loop(0, toks // tok_tile)
        def _(m):
            sl = pl.ds(pl.multiple_of(m * tok_tile, tok_tile), tok_tile)
            gate = dot_tn(n2t[:, sl], wg2[...])
            up = dot_tn(n2t[:, sl], wu2[...])
            gh = dot_tn(ct_ref[:, sl], wd2[...])
            k0 = 0.7978845608028654
            k1 = 0.044715
            sq = gate * gate
            th = jnp.tanh(k0 * (gate + k1 * (sq * gate)))
            half_one = 0.5 * (1.0 + th)
            act = gate * half_one
            slope = half_one + 0.5 * gate * (1.0 - th * th) * (k0 * (1.0 + 3.0 * k1 * sq))
            hid[sl, :] = (act * up).astype(bf16)
            dgt[sl, :] = (gh * up * slope).astype(bf16)
            dup[sl, :] = (gh * act).astype(bf16)

        @pl.loop(0, nbig)
        def _(i):
            sl = pl.ds(pl.multiple_of(i * big, 16), big)
            acc_o[sl, :] += dot_nt(wd2[sl, :], hid[...])
            acc_n[sl, :] += dot_nt(wg2[sl, :], dgt[...]) + dot_nt(wu2[sl, :], dup[...])
            for k, value in enumerate(
                (dot_nn(n2t[sl, :], dgt[...]), dot_nn(n2t[sl, :], dup[...]), dot_nn(ct_ref[sl, :], hid[...]))
            ):
                for half in (0, 1):
                    for j in (0, 1):
                        g[slot * 16 + half * 8 + 2 * i + j, :, k * sub : (k + 1) * sub] = value[
                            rows * j : rows * (j + 1), half * sub : (half + 1) * sub
                        ].astype(bf16)
            core_part(t, 2 * i, 2, fw)

    def ffn_step(t, carry):
        gather_done(("f", t))
        ffn_load(t)
        pl.when(t >= 1)(lambda: stored(t - 1, fw))
        do_in_loop(t, 0)
        pl.when(t >= 2)(lambda: slot_free(t - 2))
        ffn_chunk(t)
        do_in_loop(t, 1)
        plane_send(t, fw)
        return carry

    gather_sent(("a", 0))
    gather_sent(("a", 1))
    lax.fori_loop(0, chunks, ffn_step, 0)

    nv = chunks
    nq = chunks + 1
    stored(nv - 1, fw)
    do(tail_at)
    pick = lax.broadcasted_iota(jnp.int32, (8, toks), 0)

    def token_sums(row):
        chosen = (pick == row).astype(bf16)
        return dot_nt(chosen, wg2[...]) + dot_nt(chosen, wu2[...])

    def second_mean(sl, acc):
        return acc + fold(gcol[sl, 1:2] * acc_n[sl, :] * mid[sl, :])

    back = jnp.sum(over_rows(second_mean, zero8), axis=0, keepdims=True) * (1.0 / width)
    back = back * (r2n * r2n * r2n)

    def second_norm(sl, carry):
        m = mid[sl, :]
        gn = acc_n[sl, :]
        out_ref[sl, :] = acc_o[sl, :].astype(bf16)
        v = gn * m * r2n
        hi = v.astype(bf16)
        wg2[sl, :] = hi
        wu2[sl, :] = (v - hi.astype(f32)).astype(bf16)
        gm = ct_ref[sl, :].astype(f32) + r2n * gcol[sl, 1:2] * gn - m * back
        acc_n[sl, :] = gm
        n2t[sl, :] = gm.astype(bf16)
        return carry

    over_rows(second_norm, 0)
    sms[0] = jnp.zeros(sms.shape[1:], f32)
    sms[0, :, 0:width] = token_sums(1)
    do(tail_at + 1)

    dqt = dgt.at[pl.ds(0, aw)]
    dkt = dup.at[pl.ds(0, aw)]
    dat[...] = dot_tn(wo[...], n2t[...]).astype(bf16)

    def weight_grad(n, half, left, right):
        @pl.loop(0, nbig)
        def _(i):
            sl = pl.ds(pl.multiple_of(i * big, 16), big)
            value = dot_nt(left[sl, :], right[...])
            for j in (0, 1):
                g[(n % 2) * 16 + half * 8 + 2 * i + j, :, 0:aw] = value[rows * j : rows * (j + 1), :].astype(bf16)

    slot_free(5)
    weight_grad(nv, 1, n2t, att)
    do(tail_at + 2)
    flip = (
        lax.broadcasted_iota(jnp.int32, (toks, toks), 0) + lax.broadcasted_iota(jnp.int32, (toks, toks), 1)
        == toks - 1
    )
    hid[...] = flip.astype(bf16)
    doff[...] = jnp.zeros(doff.shape, f32)

    def attend_back(h, carry):
        head = pl.ds(pl.multiple_of(h * hs, hs), hs)
        grad_v = []
        grad_k = []
        offsets = jnp.zeros((1, lanes), f32)
        for block in (0, 1):
            p, low, keys = softmax_block(h, head, block)
            q_rows = qt[head, low : low + half_tok]
            a_rows = dat[head, low : low + half_tok]
            grad_p = dot_tn(a_rows, vt[head, 0:keys])
            ds = (p * (grad_p - jnp.sum(p * grad_p, axis=1, keepdims=True))).astype(bf16)
            grad_v.append(dot_nn(a_rows, p.astype(bf16)))
            grad_k.append(dot_nn(q_rows, ds))
            dqt[head, low : low + half_tok] = dot_nt(kt[head, 0:keys], ds).astype(bf16)
            turned = dot_nn(ds, hid[0:keys, toks - keys : toks])
            padded = jnp.concatenate([turned, jnp.zeros((half_tok, lanes - keys), f32)], axis=1)
            lined = pltpu.roll(padded, half_tok, 1, stride=1, stride_axis=0)
            offsets = offsets + jnp.sum(lined, axis=0, keepdims=True)
        for dst, parts in ((dvt, grad_v), (dkt, grad_k)):
            dst[head, 0:half_tok] = (parts[0] + parts[1][:, 0:half_tok]).astype(bf16)
            dst[head, half_tok:toks] = parts[1][:, half_tok:toks].astype(bf16)
        doff[pl.ds(h, 1), :] = offsets
        return carry

    lax.fori_loop(0, heads // 2, attend_back, 0)
    do(tail_at + 3)
    lax.fori_loop(heads // 2, heads, attend_back, 0)
    weight_grad(nv, 0, n1t, dvt)
    core_part(nv, 0, 8, aw)
    slot_free(6)
    weight_grad(nq, 0, n1t, dqt)
    weight_grad(nq, 1, n1t, dkt)
    plane_send(nv, aw)
    core_part(nq, 0, 8, aw)
    stored(nv, aw)
    do(tail_at + 4)
    plane_send(nq, aw)
    stored(nq, aw)
    do(tail_at + 5)

    def first_back(i, acc):
        sl = pl.ds(pl.multiple_of(i * big, 16), big)
        gn = dot_nn(wq[sl, :], dqt[...]) + dot_nn(wk[sl, :], dkt[...]) + dot_nn(wv[sl, :], dvt[...])
        acc_o[sl, :] = gn
        v = gcol[sl, 0:1] * gn * xt_ref[sl, :].astype(f32)
        return acc + jnp.sum(v.reshape(big // 8, 8, toks), axis=0)

    back = jnp.sum(lax.fori_loop(0, nbig, first_back, zero8), axis=0, keepdims=True) * (1.0 / width)
    back = back * (r1 * r1 * r1)
    do(tail_at + 6)

    def first_norm(sl, carry):
        v = xt_ref[sl, :].astype(f32)
        gn = acc_o[sl, :]
        prod = gn * v * r1
        hi = prod.astype(bf16)
        wg2[sl, :] = hi
        wu2[sl, :] = (prod - hi.astype(f32)).astype(bf16)
        gtok_ref[sl, :] = (acc_n[sl, :] + r1 * gcol[sl, 0:1] * gn - v * back).astype(bf16)
        return carry

    over_rows(first_norm, 0)
    sms[0, :, 0:width] += token_sums(0)
    rest = doff[...]
    table = jnp.zeros((8, onehot.shape[0]), f32)
    for _ in range(3):
        part = rest.astype(bf16)
        table = table + dot_nt(part, onehot[...])
        rest = rest - part.astype(f32)
    sms[0, :, sms.shape[2] - onehot.shape[0] : sms.shape[2]] = table
    small_send(0)
    for k in range(7, TAIL_SLOTS):
        do(tail_at + k)
        if k < 13:
            small_step(k - 7)

    settle(gland.at[pl.ds(0, 7)], gain_s)
    slot_free(nv)
    slot_free(nq)
    turn_free(nv)
    turn_free(nq)
    for n in range(total):
        settle(span(hop_ref, 0, 4, width_of(n)), e1s.at[n])
    lax.fori_loop(0, chunks, lambda k, carry: (gather_sent(("f", k)), carry)[1], 0)

    @pl.when(outer)
    def _():
        for n in (nv - 1, nv, nq):
            sent(vbuf, zis, n)
        for n in range(total):
            for half in (0, 1):
                settle(cut1(ubuf, 0, width_of(n)), ur.at[n, half])

    @pl.when(inner)
    def _():
        for n in (nv, nq):
            u_free(n, aw)
        for n in range(total):
            settle(cut1(ubuf, 0, width_of(n)), ur.at[n, 1 - c])


def fused(tokens, cotangent, buckets, bias_table, gains, weights):
    toks, width = tokens.shape
    heads = bias_table.shape[1]
    rows, aw = weights[0].shape
    ff = weights[4].shape[1]
    sub = 256
    fw = 3 * sub
    chunks = ff // (2 * sub)
    total = chunks + 2
    lanes = 2 * toks
    small_lanes = (width + 127) // 128 * 128 + 128
    padded = jnp.concatenate([buckets, jnp.full((1,), -1, jnp.int32)])
    turned = jnp.concatenate([buckets[::-1], jnp.full((1,), -1, jnp.int32)])
    bucket_rows = jnp.concatenate([turned[None], padded[None], jnp.full((6, lanes), -1, jnp.int32)])
    table = jnp.pad(bias_table.T, ((0, 8 - heads), (0, 128 - bias_table.shape[0])))
    vm = pl.BlockSpec(memory_space=pltpu.VMEM)
    hbm = pl.BlockSpec(memory_space=pltpu.HBM)
    dma = pltpu.SemaphoreType.DMA
    tok = lambda kind: pltpu.VMEM((width, toks), kind)
    inner_rows = pltpu.VMEM((aw, toks), bf16)
    blocks = lambda count: pltpu.VMEM((count, rows, fw), bf16)
    return pl.pallas_call(
        functools.partial(fused_kernel, chunks=chunks, heads=heads),
        out_shape=(
            jax.ShapeDtypeStruct((width, toks), bf16),
            jax.ShapeDtypeStruct((width, toks), bf16),
            jax.ShapeDtypeStruct((8, small_lanes), f32),
            *([jax.ShapeDtypeStruct((rows, aw), bf16)] * 4),
            *([jax.ShapeDtypeStruct((rows, ff), bf16)] * 3),
            jax.ShapeDtypeStruct((chunks * 16, rows, fw), bf16),
            jax.ShapeDtypeStruct((total * 8, rows, fw), bf16),
            jax.ShapeDtypeStruct((total * 4, rows, fw), bf16),
            jax.ShapeDtypeStruct((total * 2, rows, fw), bf16),
        ),
        in_specs=[vm] * 5 + [hbm] * 7,
        out_specs=[vm] * 3 + [hbm] * 11,
        scratch_shapes=[
            pltpu.VMEM((8, rows, 128), bf16),
            pltpu.VMEM((width, 128), f32),
            tok(bf16),
            tok(bf16),
            tok(f32),
            tok(f32),
            tok(f32),
            *([inner_rows] * 6),
            *([pltpu.VMEM((width, aw), bf16)] * 4),
            *([pltpu.VMEM((width, 2 * sub), bf16)] * 3),
            pltpu.VMEM((32, rows, sub), bf16),
            blocks(32),
            *([pltpu.VMEM((toks, 2 * sub), bf16)] * 3),
            blocks(16),
            blocks(8),
            blocks(6),
            blocks(6),
            blocks(4),
            blocks(6),
            blocks(4),
            pltpu.VMEM((8, lanes), f32),
            pltpu.VMEM((128, lanes), bf16),
            pltpu.VMEM((8, lanes), f32),
            pltpu.VMEM((6, 8, small_lanes), f32),
            pltpu.VMEM((6, 8, small_lanes), f32),
            dma(()),
            dma(()),
            *([dma((total,))] * 5),
            dma((4,)),
            *([dma((total,))] * 2),
            dma((total, 8)),
            dma((6,)),
            dma((total,)),
            dma((total, 2)),
            *([dma((total,))] * 2),
            *([dma((total, 2))] * 4),
            dma((total, 3)),
            dma((total,)),
            dma((total, 2)),
            dma((6,)),
            dma((6,)),
            pltpu.SemaphoreType.REGULAR,
            pltpu.SemaphoreType.REGULAR,
        ],
        compiler_params=pltpu.CompilerParams(
            collective_id=0, has_side_effects=True, vmem_limit_bytes=60 * 2**20
        ),
        cost_estimate=pl.CostEstimate(flops=57 * 10**9, bytes_accessed=10**8, transcendentals=10**7),
    )(tokens.T, cotangent.T, bucket_rows, table, gains, *weights)


def fused_body(
    tokens,
    cotangent,
    buckets,
    bias_table,
    attn_gain,
    w_query,
    w_key,
    w_value,
    w_output,
    ffn_gain,
    w_gate,
    w_up,
    w_down,
):
    rows = w_query.shape[0]
    gains = jnp.pad(jnp.stack([attn_gain, ffn_gain], axis=1), ((0, 0), (0, 126)))
    weights = (w_query, w_key, w_value, w_output, w_gate, w_up, w_down)
    out, gtok, small, *grads = fused(tokens, cotangent, buckets, bias_table, gains, weights)
    grads = [grad.astype(f32) for grad in grads[:7]]
    own = lax.dynamic_slice(small, (0, lax.axis_index("shard") * rows), (2, rows))
    table = small[0 : bias_table.shape[1], small.shape[1] - 128 :][:, 0 : bias_table.shape[0]].T
    return (out.T, gtok.T, own[0], *grads[:4], own[1], *grads[4:], table)


def solution(mesh):
    chosen = body
    if mesh.shape["shard"] == 8 and mesh.shape["rep"] == 4:
        chosen = fused_body
    return jax.shard_map(
        chosen,
        mesh=mesh,
        in_specs=(
            P(("shard", "rep"), None),
            P(("shard", "rep"), None),
            P(),
            P(),
            P("shard"),
            P("shard", None),
            P("shard", None),
            P("shard", None),
            P("shard", None),
            P("shard"),
            P("shard", None),
            P("shard", None),
            P("shard", None),
        ),
        out_specs=(
            P(("shard", "rep"), None),
            P(("shard", "rep"), None),
            P("shard"),
            P("shard", None),
            P("shard", None),
            P("shard", None),
            P("shard", None),
            P("shard"),
            P("shard", None),
            P("shard", None),
            P("shard", None),
            P(),
        ),
        check_vma=False,
    )
```

```python
import functools

import jax
import jax.numpy as jnp
from jax import lax
from jax.experimental import pallas as pl
from jax.experimental.pallas import tpu as pltpu
from jax.sharding import PartitionSpec as P

BLOCK = 256
MESH = pl.DeviceIdType.MESH
f32 = jnp.float32
bf16 = jnp.bfloat16


norm_eps = 1e-06
masked_score = -1e30
highest = lax.Precision.HIGHEST


def norm_local(row_values, gain_vector):
    return (
        row_values
        * lax.rsqrt(jnp.mean(row_values * row_values, axis=-1, keepdims=True) + norm_eps)
        * gain_vector
    )


def gelu_tanh(values_in):
    return jax.nn.gelu(values_in, approximate=True)


def diagonal_total(matrix):
    head_count, row_count, key_count = matrix.shape
    flipped = matrix[:, :, ::-1]
    padded = jnp.concatenate(
        [flipped, jnp.zeros((head_count, row_count, row_count), jnp.float32)], axis=2
    )
    flat_rows = padded.reshape(head_count, row_count * (key_count + row_count))
    flat_rows = flat_rows[:, : row_count * (key_count + row_count - 1)]
    return jnp.sum(flat_rows.reshape(head_count, row_count, key_count + row_count - 1), axis=1)


def toeplitz_grid(offset_bias, row_count, length):
    head_count = offset_bias.shape[0]
    span = length + row_count - 1
    flipped = offset_bias[:, ::-1]
    rotated = jnp.concatenate([flipped[:, row_count - 1 :], flipped[:, : row_count - 1]], axis=1)
    tiled = jnp.tile(rotated, (1, row_count))[:, : row_count * (span - 1)]
    return tiled.reshape(head_count, row_count, span - 1)[:, :, :length]


def body(
    tokens,
    cotangent,
    buckets,
    bias_table,
    attn_gain,
    w_query,
    w_key,
    w_value,
    w_output,
    ffn_gain,
    w_gate,
    w_up,
    w_down,
):
    length = tokens.shape[0]
    bucket_count = bias_table.shape[0]
    head_count = bias_table.shape[1]
    inner_width = w_query.shape[1]
    ff_width = w_gate.shape[1]
    owner_rows = w_query.shape[0]
    head_size = inner_width // head_count
    block_rows = min(512, length)
    block_count = length // block_rows
    residual = tokens.astype(jnp.float32)
    attn_set = (
        lax.all_gather(attn_gain, "shard", axis=0, tiled=True),
        lax.all_gather(w_query, "shard", axis=0, tiled=True),
        lax.all_gather(w_key, "shard", axis=0, tiled=True),
        lax.all_gather(w_value, "shard", axis=0, tiled=True),
        lax.all_gather(w_output, "shard", axis=0, tiled=True),
    )
    gain_one = attn_set[0].astype(jnp.float32)
    normed_one = norm_local(residual, gain_one).astype(jnp.bfloat16)

    def project(weight):
        product = jnp.dot(normed_one, weight, preferred_element_type=jnp.float32)
        return product.astype(jnp.bfloat16).reshape(length, head_count, head_size)

    queries = project(attn_set[1])
    key_rows = project(attn_set[2])
    value_rows = project(attn_set[3])
    one_hot = (buckets[:, None] == jnp.arange(bucket_count, dtype=jnp.int32)[None, :]).astype(
        jnp.float32
    )
    offset_bias = jnp.dot(one_hot, bias_table.astype(jnp.float32), precision=highest).T
    block_starts = jnp.arange(block_count, dtype=jnp.int32) * block_rows
    key_index = jnp.arange(length, dtype=jnp.int32)

    def block_scores(first_row, query_block):
        query_index = first_row + jnp.arange(block_rows, dtype=jnp.int32)
        bias_grid = toeplitz_grid(offset_bias, block_rows, length)
        scores = (
            jnp.einsum("qhd,khd->hqk", query_block, key_rows, preferred_element_type=jnp.float32)
            + bias_grid
        )
        allowed = key_index[None, :] // BLOCK <= query_index[:, None] // BLOCK
        return jnp.where(allowed[None], scores, masked_score)

    def attend(first_row):
        scores = block_scores(first_row, queries)
        row_max = jnp.max(scores, axis=-1, keepdims=True)
        exp_scores = jnp.exp(scores - row_max)
        totals = jnp.sum(exp_scores, axis=-1, keepdims=True)
        probability = (exp_scores / totals).astype(jnp.bfloat16)
        mixed_rows = jnp.einsum(
            "hqk,khd->qhd", probability, value_rows, preferred_element_type=jnp.float32
        )
        return (mixed_rows, (row_max + jnp.log(totals))[..., 0])

    mixed_blocks, log_totals = lax.map(attend, block_starts)
    attended = mixed_blocks.reshape(length, inner_width).astype(jnp.bfloat16)
    middle = residual + jnp.einsum(
        "ti,di->td", attended, attn_set[4], preferred_element_type=jnp.float32
    )
    ffn_set = (
        lax.all_gather(ffn_gain, "shard", axis=0, tiled=True),
        lax.all_gather(w_gate, "shard", axis=0, tiled=True),
        lax.all_gather(w_up, "shard", axis=0, tiled=True),
        lax.all_gather(w_down, "shard", axis=0, tiled=True),
    )
    gain_two = ffn_set[0].astype(jnp.float32)
    normed_two = norm_local(middle, gain_two).astype(jnp.bfloat16)
    gate_values = jnp.dot(normed_two, ffn_set[1], preferred_element_type=jnp.float32)
    up_values = jnp.dot(normed_two, ffn_set[2], preferred_element_type=jnp.float32)
    activated, gelu_pullback = jax.vjp(gelu_tanh, gate_values)
    hidden = (activated * up_values).astype(jnp.bfloat16)
    layer_out = (
        middle + jnp.einsum("tf,df->td", hidden, ffn_set[3], preferred_element_type=jnp.float32)
    ).astype(jnp.bfloat16)
    ffn_set = (
        lax.all_gather(ffn_gain, "shard", axis=0, tiled=True),
        lax.all_gather(w_gate, "shard", axis=0, tiled=True),
        lax.all_gather(w_up, "shard", axis=0, tiled=True),
        lax.all_gather(w_down, "shard", axis=0, tiled=True),
    )
    grad_w_down = jnp.einsum("td,tf->df", cotangent, hidden, preferred_element_type=jnp.float32)
    grad_hidden = jnp.dot(cotangent, ffn_set[3], preferred_element_type=jnp.float32)
    grad_gate = gelu_pullback(grad_hidden * up_values)[0].astype(jnp.bfloat16)
    grad_up = (grad_hidden * activated).astype(jnp.bfloat16)
    grad_w_gate = jnp.einsum("td,tf->df", normed_two, grad_gate, preferred_element_type=jnp.float32)
    grad_w_up = jnp.einsum("td,tf->df", normed_two, grad_up, preferred_element_type=jnp.float32)
    grad_normed_two = jnp.einsum(
        "tf,df->td", grad_gate, ffn_set[1], preferred_element_type=jnp.float32
    )
    grad_normed_two = grad_normed_two + jnp.einsum(
        "tf,df->td", grad_up, ffn_set[2], preferred_element_type=jnp.float32
    )
    middle_part, grad_gain_two = jax.vjp(norm_local, middle, gain_two)[1](grad_normed_two)
    grad_middle = cotangent.astype(jnp.float32) + middle_part
    ffn_shards = (
        lax.psum_scatter(grad_w_gate.astype(jnp.bfloat16), "shard", scatter_dimension=0, tiled=True),
        lax.psum_scatter(grad_w_up.astype(jnp.bfloat16), "shard", scatter_dimension=0, tiled=True),
        lax.psum_scatter(grad_w_down.astype(jnp.bfloat16), "shard", scatter_dimension=0, tiled=True),
    )
    attn_set = (
        lax.all_gather(attn_gain, "shard", axis=0, tiled=True),
        lax.all_gather(w_query, "shard", axis=0, tiled=True),
        lax.all_gather(w_key, "shard", axis=0, tiled=True),
        lax.all_gather(w_value, "shard", axis=0, tiled=True),
        lax.all_gather(w_output, "shard", axis=0, tiled=True),
    )
    grad_branch = grad_middle.astype(jnp.bfloat16)
    grad_w_output = jnp.einsum(
        "td,ti->di", grad_branch, attended, preferred_element_type=jnp.float32
    )
    grad_attended = jnp.einsum(
        "td,di->ti", grad_branch, attn_set[4], preferred_element_type=jnp.float32
    )
    grad_attended = grad_attended.astype(jnp.bfloat16).reshape(length, head_count, head_size)

    def attend_back(carried, block_input):
        grad_keys, grad_values, grad_offsets = carried
        first_row, log_total = block_input
        scores = block_scores(first_row, queries)
        probability = jnp.exp(scores - log_total[..., None])
        grad_probs = jnp.einsum(
            "qhd,khd->hqk", grad_attended, value_rows, preferred_element_type=jnp.float32
        )
        inner_sum = jnp.sum(probability * grad_probs, axis=-1, keepdims=True)
        grad_scores = (probability * (grad_probs - inner_sum)).astype(jnp.bfloat16)
        grad_values = grad_values + jnp.einsum(
            "hqk,qhd->khd",
            probability.astype(jnp.bfloat16),
            grad_attended,
            preferred_element_type=jnp.float32,
        )
        grad_keys = grad_keys + jnp.einsum(
            "hqk,qhd->khd", grad_scores, queries, preferred_element_type=jnp.float32
        )
        grad_queries = jnp.einsum(
            "hqk,khd->qhd", grad_scores, key_rows, preferred_element_type=jnp.float32
        )
        diagonal_sums = diagonal_total(grad_scores.astype(jnp.float32))
        offset_piece = grad_offsets
        grad_offsets = offset_piece + diagonal_sums
        return ((grad_keys, grad_values, grad_offsets), grad_queries)

    zero_rows = jnp.zeros((length, head_count, head_size), jnp.float32)
    zero_offsets = jnp.zeros((head_count, 2 * length - 1), jnp.float32)
    (grad_keys, grad_values, grad_offsets), query_blocks = lax.scan(
        attend_back, (zero_rows, zero_rows, zero_offsets), (block_starts, log_totals)
    )
    grad_queries = query_blocks.reshape(length, inner_width).astype(jnp.bfloat16)
    grad_keys = grad_keys.reshape(length, inner_width).astype(jnp.bfloat16)
    grad_values = grad_values.reshape(length, inner_width).astype(jnp.bfloat16)
    grad_w_query = jnp.einsum(
        "td,ti->di", normed_one, grad_queries, preferred_element_type=jnp.float32
    )
    grad_w_key = jnp.einsum("td,ti->di", normed_one, grad_keys, preferred_element_type=jnp.float32)
    grad_w_value = jnp.einsum(
        "td,ti->di", normed_one, grad_values, preferred_element_type=jnp.float32
    )
    grad_normed_one = jnp.einsum(
        "ti,di->td", grad_queries, attn_set[1], preferred_element_type=jnp.float32
    )
    grad_normed_one = grad_normed_one + jnp.einsum(
        "ti,di->td", grad_keys, attn_set[2], preferred_element_type=jnp.float32
    )
    grad_normed_one = grad_normed_one + jnp.einsum(
        "ti,di->td", grad_values, attn_set[3], preferred_element_type=jnp.float32
    )
    rows_part, grad_gain_one = jax.vjp(norm_local, residual, gain_one)[1](grad_normed_one)
    grad_tokens = (grad_middle + rows_part).astype(jnp.bfloat16)
    grad_table = jnp.dot(grad_offsets, one_hot, precision=highest).T
    owner_start = lax.axis_index("shard") * owner_rows
    attn_shards = (
        lax.psum_scatter(grad_w_query.astype(jnp.bfloat16), "shard", scatter_dimension=0, tiled=True),
        lax.psum_scatter(grad_w_key.astype(jnp.bfloat16), "shard", scatter_dimension=0, tiled=True),
        lax.psum_scatter(grad_w_value.astype(jnp.bfloat16), "shard", scatter_dimension=0, tiled=True),
        lax.psum_scatter(grad_w_output.astype(jnp.bfloat16), "shard", scatter_dimension=0, tiled=True),
    )
    summed = lax.psum(
        (
            attn_shards[0],
            attn_shards[1],
            attn_shards[2],
            attn_shards[3],
            ffn_shards[0],
            ffn_shards[1],
            ffn_shards[2],
        ),
        "rep",
    )
    small_total = lax.psum((grad_gain_one, grad_gain_two, grad_table), ("shard", "rep"))
    gain_one_own = lax.dynamic_slice_in_dim(small_total[0], owner_start, owner_rows, 0)
    gain_two_own = lax.dynamic_slice_in_dim(small_total[1], owner_start, owner_rows, 0)
    return (
        layer_out,
        grad_tokens,
        gain_one_own,
        summed[0].astype(jnp.float32),
        summed[1].astype(jnp.float32),
        summed[2].astype(jnp.float32),
        summed[3].astype(jnp.float32),
        gain_two_own,
        summed[4].astype(jnp.float32),
        summed[5].astype(jnp.float32),
        summed[6].astype(jnp.float32),
        small_total[2],
    )

HEAD_SLOTS = 7
TAIL_SLOTS = 14
HELPED = (1, 2, 3, 4, 5, 6)
SLOTS = {
    "send": (0, 0, 0, 2, 2, 2, 2),
    "forward": (1, 1, 1, 6, 7, 8, 11),
    "swap": (2, 3, 4, 8, 10, 11, 17),
    "get_forward": (1, 6, 7, 10, 11, 15, 16),
    "get_swap": (3, 8, 9, 11, 13, 16, 18),
    "turn": (10, 12, 15, 16, 20, 21, 24, 27, 29),
    "rep": (13, 14, 19, 20, 23, 25, 26, 30, 31),
    "mid": (17, 18, 20, 22, 24, 26, 29, 31, 32),
    "last": (18, 21, 23, 24, 25, 28, 30, 32, 33),
}


def dot_nn(a, b):
    return lax.dot_general(a, b, (((1,), (0,)), ((), ())), preferred_element_type=f32)


def dot_nt(a, b):
    return lax.dot_general(a, b, (((1,), (1,)), ((), ())), preferred_element_type=f32)


def dot_tn(a, b):
    return lax.dot_general(a, b, (((0,), (0,)), ((), ())), preferred_element_type=f32)


def fused_kernel(
    xt_ref,
    ct_ref,
    buckets_ref,
    table_ref,
    gains_ref,
    wq_ref,
    wk_ref,
    wv_ref,
    wo_ref,
    wg_ref,
    wu_ref,
    wd_ref,
    out_ref,
    gtok_ref,
    small_ref,
    gq_ref,
    gk_ref,
    gv_ref,
    go_ref,
    gg_ref,
    gu_ref,
    gd_ref,
    land_ref,
    sum_ref,
    hop_ref,
    turn_ref,
    gland,
    gcol,
    n1t,
    n2t,
    mid,
    acc_o,
    acc_n,
    qt,
    kt,
    vt,
    att,
    dat,
    dvt,
    wq,
    wk,
    wv,
    wo,
    wg2,
    wu2,
    wd2,
    wload,
    g,
    hid,
    dgt,
    dup,
    rc,
    stage_t,
    stage_v,
    vbuf,
    zi,
    zm,
    ubuf,
    revb,
    onehot,
    doff,
    sms,
    smr,
    gain_s,
    gain_r,
    gsend,
    gloc,
    g1r,
    g2r,
    gpr,
    load_sem,
    e0s,
    e0r,
    sum_sem,
    stage_sem,
    e1s,
    e1r,
    e2s,
    e2r,
    zis,
    zir,
    zms,
    zmr,
    us,
    ul,
    ur,
    sss,
    ssr,
    zcredit,
    mcredit,
    *,
    chunks,
    heads,
):
    width = xt_ref.shape[0]
    toks = xt_ref.shape[1]
    rows = gains_ref.shape[0]
    fw = land_ref.shape[2]
    sub = fw // 3
    aw = wq_ref.shape[1]
    hs = aw // heads
    total = chunks + 2
    eps = 1e-06
    lanes = revb.shape[1]
    big = 2 * rows
    nbig = width // big

    s = lax.axis_index("shard")
    r = lax.axis_index("rep")
    c = s % 2
    x = (s // 2) % 2
    y = s // 4
    sc = s + 1 - 2 * c
    sx = s + 2 - 4 * x
    sy = s + 4 - 8 * y
    bx = sx - c
    by = sy - c
    bd = (1 - y) * 4 + (1 - x) * 2
    b_own = s - c
    mate = r + 1 - 2 * (r % 2)
    inner = (r == 1) | (r == 2)
    outer = (r == 0) | (r == 3)

    def remote(src, dst, ssem, rsem, dev):
        return pltpu.make_async_remote_copy(
            src_ref=src, dst_ref=dst, send_sem=ssem, recv_sem=rsem, device_id=dev, device_id_type=MESH
        )

    def settle(ref, sem):
        pltpu.make_async_copy(ref, ref, sem).wait()

    barrier = pltpu.get_barrier_semaphore()
    near = [(sc, r), (bx, r), (bx + 1, r), (by, r), (by + 1, r), (bd, r), (bd + 1, r), (s, mate), (sc, mate)]
    for dev in near:
        pl.semaphore_signal(barrier, inc=1, device_id=dev, device_id_type=MESH)

    @pl.when(inner)
    def _():
        pl.semaphore_signal(barrier, inc=1, device_id=(s, 3 - r), device_id_type=MESH)

    @pl.when(inner)
    def _():
        pl.semaphore_wait(barrier, len(near) + 1)

    @pl.when(outer)
    def _():
        pl.semaphore_wait(barrier, len(near))

    def place(chunk, index):
        kind, k = chunk
        if kind == "a":
            return g.at[16 + index, :, pl.ds(k * aw, aw)]
        return land_ref.at[k * 16 + index]

    def places(chunk, count):
        kind, k = chunk
        if kind == "a":
            return g.at[pl.ds(16, count), :, pl.ds(k * aw, aw)]
        return land_ref.at[pl.ds(0, count)]

    def any_of(value, options):
        return functools.reduce(jnp.logical_or, [value == option for option in options], jnp.bool_(False))

    def helped(chunk):
        kind, k = chunk
        return False if kind == "a" else any_of(k, HELPED)

    def active(chunk):
        kind, k = chunk
        return True if kind == "a" else jnp.logical_not(any_of(k, HELPED)) | (r % 2 == k % 2)

    def when(condition, then):
        if condition is True:
            then()
        elif condition is not False:
            pl.when(condition)(then)

    def columns(k, half):
        return pl.ds(pl.multiple_of((2 * k + half) * sub, sub), sub)

    def own_parts(chunk, half):
        kind, k = chunk
        dst = place(chunk, half * 8 + s)
        if kind == "a":
            return [(((wq_ref, wk_ref), (wv_ref, wo_ref))[k][half], dst)]
        return [
            (ref.at[:, columns(k, half)], dst.at[:, pl.ds(j * sub, sub)]) for j, ref in enumerate((wg_ref, wu_ref, wd_ref))
        ]

    def at(chunk):
        kind, k = chunk
        return k if kind == "a" else k + 2

    def gather_send(chunk):
        i = at(chunk)

        def cross():
            for half in (0, 1):
                for src, dst in own_parts(chunk, half):
                    remote(src, dst, gsend.at[i], g1r.at[i], (bx + half, r)).start()
                    remote(src, dst, gsend.at[i], g1r.at[i], (by + half, r)).start()

        when(active(chunk), cross)
        for half in (0, 1):
            for src, dst in own_parts(chunk, half):
                remote(src, dst, gsend.at[i], gpr.at[i], (sc, r)).start()
                pltpu.make_async_copy(src, dst, gloc.at[i]).start()

    def hand_over(chunk, blocks, sem):
        i = at(chunk)

        def hand():
            for b in blocks:
                spot = place(chunk, c * 8 + b)
                remote(spot, spot, gsend.at[i], sem.at[i], (s, mate)).start()

        if chunk[0] == "f":
            pl.when(helped(chunk) & active(chunk))(hand)
        for b in blocks:
            spot = place(chunk, c * 8 + b)
            remote(spot, spot, gsend.at[i], gpr.at[i], (sc, r)).start()

    def gather_forward(chunk):
        i = at(chunk)
        settle(places(chunk, 4), g1r.at[i])

        def cross():
            one = place(chunk, c * 8 + bx)
            two = place(chunk, c * 8 + by + 1)
            remote(one, one, gsend.at[i], g2r.at[i], (sy, r)).start()
            remote(two, two, gsend.at[i], g2r.at[i], (sx, r)).start()

        when(active(chunk), cross)
        hand_over(chunk, (bx, bx + 1, by, by + 1), g1r)

    def gather_swap(chunk):
        settle(places(chunk, 2), g2r.at[at(chunk)])
        hand_over(chunk, (bd, bd + 1), g2r)

    def gather_done(chunk):
        i = at(chunk)
        settle(places(chunk, 8), gpr.at[i])
        settle(places(chunk, 2), gloc.at[i])

    def gather_sent(chunk):
        i = at(chunk)
        does = active(chunk)
        if does is True:
            settle(places(chunk, 14), gsend.at[i])
            return
        pl.when(does & helped(chunk))(lambda: settle(places(chunk, 20), gsend.at[i]))
        pl.when(does & jnp.logical_not(helped(chunk)))(lambda: settle(places(chunk, 14), gsend.at[i]))
        pl.when(jnp.logical_not(does))(lambda: settle(places(chunk, 8), gsend.at[i]))

    def ahead(stage, k, mine):
        chunk = ("f", k)
        does = active(chunk) if mine else jnp.logical_not(active(chunk))
        pl.when((k < chunks) & does)(lambda: stage(chunk))

    def cut(ref, w):
        return ref if w == fw else ref.at[:, :, pl.ds(0, w)]

    def cut1(ref, index, w):
        return ref.at[index] if w == fw else ref.at[index, :, pl.ds(0, w)]

    def span(ref, start, count, w):
        return ref.at[pl.ds(start, count)] if w == fw else ref.at[pl.ds(start, count), :, pl.ds(0, w)]

    def get(ref, index, w):
        return ref[index] if w == fw else ref[index, :, 0:w]

    def put(ref, index, w, value):
        if w == fw:
            ref[index] = value
        else:
            ref[index, :, 0:w] = value

    def add_to(dst, i, src, j, w):
        put(dst, i, w, get(dst, i, w) + get(src, j, w))

    def core_part(n, b, count, w):
        slot = n % 2
        remote(
            span(g, slot * 16 + (1 - c) * 8 + b, count, w), span(rc, slot * 8 + b, count, w), e0s.at[n], e0r.at[n], (sc, r)
        ).start()

    def plane_send(n, w):
        slot = n % 2
        base = slot * 16 + c * 8
        settle(span(rc, slot * 8, 8, w), e0r.at[n])
        order = []
        for k, kx, ky in ((0, 1 - y, 1 - x), (1, y, x)):
            order.append((4 * kx + 2 * (1 - x), sx, 2 * k))
            order.append((4 * (1 - y) + 2 * ky + 1, sy, 2 * k + 1))
        order += [(b, None, None) for b in (4 * (1 - y) + 2 * x, 4 * y + 2 * (1 - x) + 1, b_own, b_own + 1)]

        def store(i):
            b = order[i][0]
            return pltpu.make_async_copy(cut1(g, base + b, w), cut1(sum_ref, n * 8 + b, w), sum_sem.at[n, i])

        for i, (b, _, _) in enumerate(order):
            add_to(g, base + b, rc, slot * 8 + b, w)
            store(i).start()
        for i, (b, dev, spot) in enumerate(order[:4]):
            store(i).wait()
            remote(
                cut1(sum_ref, n * 8 + b, w), cut1(hop_ref, n * 4 + spot, w), e1s.at[n], e1r.at[n, spot // 2], (dev, r)
            ).start()

    def stored(n, w):
        for i in range(4, 8):
            settle(cut1(sum_ref, 0, w), sum_sem.at[n, i])

    def slot_free(n):
        settle(span(g, 0, 8, width_of(n)), e0s.at[n])

    def turn_free(n):
        settle(span(turn_ref, 0, 2, width_of(n)), e2s.at[n])

    def guarded(n, least, then):
        if isinstance(n, int):
            if n >= least:
                then()
        else:
            pl.when(n >= least)(then)

    def turn_loads(n, w):
        base = (n % 2) * 4
        first = n * 8 + 4 * (1 - y) + 2 * x
        second = n * 8 + 4 * y + 2 * (1 - x) + 1
        return [
            pltpu.make_async_copy(cut1(sum_ref, first, w), cut1(stage_t, base, w), stage_sem.at[0]),
            pltpu.make_async_copy(cut1(sum_ref, second, w), cut1(stage_t, base + 1, w), stage_sem.at[1]),
            pltpu.make_async_copy(span(hop_ref, n * 4, 2, w), span(stage_t, base + 2, 2, w), stage_sem.at[2]),
        ]

    def turn_start(n, w):
        guarded(n, 2, lambda: turn_free(n - 2))
        settle(span(hop_ref, 0, 2, w), e1r.at[n, 0])
        for load in turn_loads(n, w):
            load.start()

    def turn_end(n, w):
        base = (n % 2) * 4
        for load in turn_loads(n, w):
            load.wait()
        for j, dev in ((0, sy), (1, sx)):
            add_to(stage_t, base + j, stage_t, base + 2 + j, w)
            remote(cut1(stage_t, base + j, w), cut1(turn_ref, n * 2 + j, w), e2s.at[n], e2r.at[n], (dev, r)).start()

    def rep_loads(n, w):
        return [
            pltpu.make_async_copy(span(sum_ref, n * 8 + b_own, 2, w), span(stage_v, 0, 2, w), stage_sem.at[3]),
            pltpu.make_async_copy(span(hop_ref, n * 4 + 2, 2, w), span(stage_v, 2, 2, w), stage_sem.at[4]),
            pltpu.make_async_copy(span(turn_ref, n * 2, 2, w), span(stage_v, 4, 2, w), stage_sem.at[5]),
        ]

    def rep_start(n, w):
        settle(span(hop_ref, 0, 2, w), e1r.at[n, 1])
        settle(span(turn_ref, 0, 2, w), e2r.at[n])
        for load in rep_loads(n, w):
            load.start()

    def rep_end(n, w):
        third = n % 3

        def outer_room():
            guarded(n, 3, lambda: pl.when(outer)(lambda: sent(vbuf, zis, n - 3)))
            guarded(n, 2, lambda: pl.when(outer)(lambda: pl.semaphore_wait(zcredit, 1)))

        outer_room()
        for load in rep_loads(n, w):
            load.wait()
        for j in (c, 1 - c):
            value = get(stage_v, j, w).astype(f32) + get(stage_v, 2 + j, w).astype(f32)
            value = value + get(stage_v, 4 + j, w).astype(f32)
            put(vbuf, third * 2 + j, w, value.astype(bf16))

            @pl.when(outer)
            def _():
                remote(
                    cut1(vbuf, third * 2 + j, w), cut1(zi, (n % 2) * 2 + j, w), zis.at[n, j], zir.at[n, j], (s, mate)
                ).start()

    def sent(ref, sems, n):
        for j in (0, 1):
            settle(cut1(ref, 0, width_of(n)), sems.at[n, j])

    def width_of(n):
        return fw if not isinstance(n, int) or n < chunks else aw

    def rep_turn(n, w):
        third = n % 3

        @pl.when(inner)
        def _():
            guarded(n, 3, lambda: pl.semaphore_wait(mcredit, 1))
            for j in (c, 1 - c):
                settle(cut1(zi, j, w), zir.at[n, j])
                add_to(vbuf, third * 2 + j, zi, (n % 2) * 2 + j, w)
                remote(
                    cut1(vbuf, third * 2 + j, w), cut1(zm, third * 2 + j, w), zms.at[n, j], zmr.at[n, j], (s, 3 - r)
                ).start()
            guarded(total - 1 - n, 2, lambda: give_credit(zcredit, (s, mate)))

    def give_credit(sem, dev):
        pl.semaphore_signal(sem, inc=1, device_id=dev, device_id_type=MESH)

    def result(n, half, block):
        if isinstance(n, int) and n >= chunks:
            return [(block, ((gv_ref, go_ref), (gq_ref, gk_ref))[n - chunks][half])]
        return [
            (block.at[:, pl.ds(j * sub, sub)], ref.at[:, columns(n, half)])
            for j, ref in enumerate((gg_ref, gu_ref, gd_ref))
        ]

    def u_free(n, w):
        slot = n % 2
        for k in (0, 1, 2):
            settle(cut1(ubuf, slot * 2, w), us.at[n, k])
        settle(cut1(ubuf, slot * 2, w), ul.at[n])

    def rep_last(n, w):
        slot = n % 2
        third = n % 3

        @pl.when(inner)
        def _():
            guarded(n, 2, lambda: u_free(n - 2, width_of(n - 2)))

            def both(j):
                settle(cut1(zm, j, w), zmr.at[n, j])
                value = get(vbuf, third * 2 + j, w).astype(f32) + get(zm, third * 2 + j, w).astype(f32)
                put(ubuf, slot * 2 + j, w, value.astype(bf16))

            def finish_keep(half):
                for src, dst in result(n, half, cut1(ubuf, slot * 2 + c, w)):
                    remote(src, dst, us.at[n, 0], ur.at[n, half], (s, mate)).start()
                    pltpu.make_async_copy(src, dst, ul.at[n]).start()

            def finish_give(half):
                for src, dst in result(n, half, cut1(ubuf, slot * 2 + 1 - c, w)):
                    remote(src, dst, us.at[n, 1], ur.at[n, half], (sc, mate)).start()
                    remote(src, dst, us.at[n, 2], ur.at[n, half], (sc, r)).start()

            for j, finish in ((c, finish_keep), (1 - c, finish_give)):
                both(j)
                if w == fw:
                    finish(c)
                else:
                    pl.when(c == 0)(functools.partial(finish, 0))
                    pl.when(c == 1)(functools.partial(finish, 1))
            guarded(total - 1 - n, 3, lambda: give_credit(mcredit, (s, 3 - r)))
            sent(vbuf, zms, n)

    def gathers(stage, mine):
        return lambda k: ahead(stage, k, mine)

    def reduces(stage):
        return lambda n: stage(n, width_of(n))

    order = (
        ("swap", gathers(gather_swap, True)),
        ("forward", gathers(gather_forward, True)),
        ("send", lambda k: gather_send(("f", k))),
        ("turn", reduces(turn_start)),
        ("rep", reduces(rep_start)),
        ("last", reduces(rep_last)),
        ("mid", reduces(rep_turn)),
        ("turn", reduces(turn_end)),
        ("rep", reduces(rep_end)),
        ("get_forward", gathers(gather_forward, False)),
        ("get_swap", gathers(gather_swap, False)),
    )
    loop_at = HEAD_SLOTS
    tail_at = HEAD_SLOTS + 2 * chunks

    def do(slot):
        for name, stage in order:
            for n, spot in enumerate(SLOTS[name]):
                if spot == slot:
                    stage(n)

    def do_in_loop(t, side):
        for name, stage in order:
            pairs = [
                ((spot - loop_at) // 2, n)
                for n, spot in enumerate(SLOTS[name])
                if loop_at <= spot < tail_at and (spot - loop_at) % 2 == side
            ]
            if pairs:
                n = sum([jnp.where(t == step, number, 0) for step, number in pairs], jnp.int32(0))
                pl.when(any_of(t, [step for step, _ in pairs]))(functools.partial(stage, n))

    def small_send(step):
        if step < 3:
            dev = ((sc, r), (sx, r), (sy, r))[step]
            remote(sms.at[step], smr.at[step], sss.at[step], ssr.at[step], dev).start()
        elif step == 3:

            @pl.when(outer)
            def _():
                remote(sms.at[3], smr.at[3], sss.at[3], ssr.at[3], (s, mate)).start()
        elif step == 4:

            @pl.when(inner)
            def _():
                remote(sms.at[4], smr.at[4], sss.at[4], ssr.at[4], (s, 3 - r)).start()
        else:

            @pl.when(inner)
            def _():
                remote(sms.at[5], smr.at[5], sss.at[5], ssr.at[5], (s, mate)).start()

    def small_step(step):
        def take():
            settle(smr.at[step], ssr.at[step])
            settle(sms.at[step], sss.at[step])
            if step < 2:
                sms[step + 1] = sms[step] + smr[step]
            elif step == 2:
                sms[3] = sms[2] + smr[2]

        if step < 3:
            take()
            small_send(step + 1)
        elif step == 3:

            @pl.when(inner)
            def _():
                settle(smr.at[3], ssr.at[3])
                sms[4] = sms[3] + smr[3]

            @pl.when(outer)
            def _():
                settle(sms.at[3], sss.at[3])

            small_send(4)
        elif step == 4:

            @pl.when(inner)
            def _():
                settle(smr.at[4], ssr.at[4])
                settle(sms.at[4], sss.at[4])
                sms[5] = sms[4] + smr[4]
                small_ref[...] = sms[5]

            small_send(5)
        else:

            @pl.when(inner)
            def _():
                settle(sms.at[5], sss.at[5])

            @pl.when(outer)
            def _():
                settle(smr.at[5], ssr.at[5])
                small_ref[...] = smr[5]

    tile = 64
    tiles = width // tile

    def over_rows(body, start):
        def step(i, carry):
            return body(pl.ds(pl.multiple_of(i * tile, tile), tile), carry)

        return lax.fori_loop(0, tiles, step, start)

    def fold(value):
        return jnp.sum(value.reshape(tile // 8, 8, toks), axis=0)

    zero8 = jnp.zeros((8, toks), f32)

    gather_send(("a", 0))
    gdst = gland.at[s]
    for k, dev in enumerate([(sc, r), (bx, r), (bx + 1, r), (by, r), (by + 1, r), (bd, r), (bd + 1, r)]):
        remote(gains_ref, gdst, gain_s, gain_r, dev).start()
    pltpu.make_async_copy(gains_ref, gdst, load_sem.at[1]).start()
    gather_send(("a", 1))
    do(0)

    def square_sum(sl, acc):
        v = xt_ref[sl, :].astype(f32)
        return acc + fold(v * v)

    ssum = jnp.sum(over_rows(square_sum, zero8), axis=0, keepdims=True)
    r1 = lax.rsqrt(ssum * (1.0 / width) + eps)

    bucket_index = lax.broadcasted_iota(jnp.int32, onehot.shape, 0)
    onehot[...] = (bucket_index == buckets_ref[...]).astype(bf16)
    turn_index = lax.broadcasted_iota(jnp.int32, (toks, toks), 0) + lax.broadcasted_iota(jnp.int32, (toks, toks), 1)
    flip = (turn_index == toks - 1).astype(bf16)
    offset_bias = dot_nn(table_ref[...], onehot[0 : table_ref.shape[1], :]).astype(bf16)
    revb[0:heads, 0:toks] = dot_nn(offset_bias[:, toks:lanes], flip)
    revb[0:heads, toks:lanes] = dot_nn(offset_bias[:, 0:toks], flip)

    settle(gland.at[pl.ds(0, 7)], gain_r)
    settle(gland.at[0], load_sem.at[1])
    for b in range(8):
        gcol[rows * b : rows * (b + 1), :] = gland[b].astype(f32)

    def norm_one(sl, carry):
        v = xt_ref[sl, :].astype(f32)
        n1t[sl, :] = (v * r1 * gcol[sl, 0:1]).astype(bf16)
        return carry

    gather_forward(("a", 0))
    do(1)
    over_rows(norm_one, 0)
    gather_swap(("a", 0))
    gather_forward(("a", 1))
    do(2)

    def compact(dst, half, col):
        @pl.loop(0, nbig)
        def _(i):
            both = jnp.concatenate(
                [
                    g[16 + half * 8 + 2 * i, :, col : col + aw].astype(f32),
                    g[16 + half * 8 + 2 * i + 1, :, col : col + aw].astype(f32),
                ],
                axis=0,
            )
            dst[pl.ds(pl.multiple_of(i * 2 * rows, 16), 2 * rows), :] = both.astype(bf16)

    gather_done(("a", 0))
    compact(wq, 0, 0)
    qt[...] = dot_tn(wq[...], n1t[...]).astype(bf16)
    compact(wk, 1, 0)
    kt[...] = dot_tn(wk[...], n1t[...]).astype(bf16)
    gather_swap(("a", 1))
    do(3)
    gather_done(("a", 1))
    compact(wv, 0, aw)
    vt[...] = dot_tn(wv[...], n1t[...]).astype(bf16)
    compact(wo, 1, aw)
    do(4)

    half_tok = toks // 2

    def softmax_block(h, head, block):
        keys = half_tok * (block + 1)
        low = half_tok * block
        row = jnp.broadcast_to(revb[pl.ds(h, 1), :], (half_tok, lanes))
        bias = pltpu.roll(row, (low - toks) % lanes, 1, stride=1, stride_axis=0)[:, :keys]
        scores = dot_tn(qt[head, low : low + half_tok], kt[head, 0:keys]) + bias
        e = jnp.exp(scores - jnp.max(scores, axis=1, keepdims=True))
        return e * (1.0 / jnp.sum(e, axis=1, keepdims=True)), low, keys

    def attend(h, carry):
        head = pl.ds(pl.multiple_of(h * hs, hs), hs)
        for block in (0, 1):
            p, low, keys = softmax_block(h, head, block)
            att[head, low : low + half_tok] = dot_nt(vt[head, 0:keys], p.astype(bf16)).astype(bf16)
        return carry

    lax.fori_loop(0, heads // 2, attend, 0)
    do(5)
    lax.fori_loop(heads // 2, heads, attend, 0)
    do(6)

    def branch_one(i, acc):
        sl = pl.ds(pl.multiple_of(i * big, 16), big)
        m = xt_ref[sl, :].astype(f32) + dot_nn(wo[sl, :], att[...])
        mid[sl, :] = m
        return acc + jnp.sum((m * m).reshape(big // 8, 8, toks), axis=0)

    ssum = jnp.sum(lax.fori_loop(0, nbig, branch_one, zero8), axis=0, keepdims=True)
    r2n = lax.rsqrt(ssum * (1.0 / width) + eps)

    def norm_two(sl, carry):
        m = mid[sl, :]
        n2t[sl, :] = (m * r2n * gcol[sl, 1:2]).astype(bf16)
        acc_o[sl, :] = m
        acc_n[sl, :] = jnp.zeros((tile, toks), f32)
        return carry

    over_rows(norm_two, 0)

    tok_tile = toks // 2

    parts = [(half, k) for half in (0, 1) for k in (0, 1, 2)]
    depth = 4

    def load(t, p):
        half, k = parts[p]
        return pltpu.make_async_copy(
            land_ref.at[pl.ds(t * 16 + half * 8, 8), :, pl.ds(k * sub, sub)],
            wload.at[pl.ds((p % depth) * 8, 8)],
            load_sem.at[p % depth],
        )

    def ffn_load(t):
        for p in range(depth):
            load(t, p).start()

    def ffn_chunk(t):
        slot = t % 2
        for p, (half, k) in enumerate(parts):
            load(t, p).wait()
            dst = (wg2, wu2, wd2)[k]

            @pl.loop(0, nbig)
            def _(i):
                base = (p % depth) * 8 + 2 * i
                both = jnp.concatenate([wload[base].astype(f32), wload[base + 1].astype(f32)], axis=0)
                sl = pl.ds(pl.multiple_of(i * big, 16), big)
                dst[sl, half * sub : (half + 1) * sub] = both.astype(bf16)

            if p + depth < len(parts):
                load(t, p + depth).start()

        @pl.loop(0, toks // tok_tile)
        def _(m):
            sl = pl.ds(pl.multiple_of(m * tok_tile, tok_tile), tok_tile)
            gate = dot_tn(n2t[:, sl], wg2[...])
            up = dot_tn(n2t[:, sl], wu2[...])
            gh = dot_tn(ct_ref[:, sl], wd2[...])
            k0 = 0.7978845608028654
            k1 = 0.044715
            sq = gate * gate
            th = jnp.tanh(k0 * (gate + k1 * (sq * gate)))
            half_one = 0.5 * (1.0 + th)
            act = gate * half_one
            slope = half_one + 0.5 * gate * (1.0 - th * th) * (k0 * (1.0 + 3.0 * k1 * sq))
            hid[sl, :] = (act * up).astype(bf16)
            dgt[sl, :] = (gh * up * slope).astype(bf16)
            dup[sl, :] = (gh * act).astype(bf16)

        @pl.loop(0, nbig)
        def _(i):
            sl = pl.ds(pl.multiple_of(i * big, 16), big)
            acc_o[sl, :] += dot_nt(wd2[sl, :], hid[...])
            acc_n[sl, :] += dot_nt(wg2[sl, :], dgt[...]) + dot_nt(wu2[sl, :], dup[...])
            for k, value in enumerate(
                (dot_nn(n2t[sl, :], dgt[...]), dot_nn(n2t[sl, :], dup[...]), dot_nn(ct_ref[sl, :], hid[...]))
            ):
                for half in (0, 1):
                    for j in (0, 1):
                        g[slot * 16 + half * 8 + 2 * i + j, :, k * sub : (k + 1) * sub] = value[
                            rows * j : rows * (j + 1), half * sub : (half + 1) * sub
                        ].astype(bf16)
            core_part(t, 2 * i, 2, fw)

    def ffn_step(t, carry):
        gather_done(("f", t))
        ffn_load(t)
        pl.when(t >= 1)(lambda: stored(t - 1, fw))
        do_in_loop(t, 0)
        pl.when(t >= 2)(lambda: slot_free(t - 2))
        ffn_chunk(t)
        do_in_loop(t, 1)
        plane_send(t, fw)
        return carry

    gather_sent(("a", 0))
    gather_sent(("a", 1))
    lax.fori_loop(0, chunks, ffn_step, 0)

    nv = chunks
    nq = chunks + 1
    stored(nv - 1, fw)
    do(tail_at)
    pick = lax.broadcasted_iota(jnp.int32, (8, toks), 0)

    def token_sums(row):
        chosen = (pick == row).astype(bf16)
        return dot_nt(chosen, wg2[...]) + dot_nt(chosen, wu2[...])

    def second_mean(sl, acc):
        return acc + fold(gcol[sl, 1:2] * acc_n[sl, :] * mid[sl, :])

    back = jnp.sum(over_rows(second_mean, zero8), axis=0, keepdims=True) * (1.0 / width)
    back = back * (r2n * r2n * r2n)

    def second_norm(sl, carry):
        m = mid[sl, :]
        gn = acc_n[sl, :]
        out_ref[sl, :] = acc_o[sl, :].astype(bf16)
        v = gn * m * r2n
        hi = v.astype(bf16)
        wg2[sl, :] = hi
        wu2[sl, :] = (v - hi.astype(f32)).astype(bf16)
        gm = ct_ref[sl, :].astype(f32) + r2n * gcol[sl, 1:2] * gn - m * back
        acc_n[sl, :] = gm
        n2t[sl, :] = gm.astype(bf16)
        return carry

    over_rows(second_norm, 0)
    sms[0] = jnp.zeros(sms.shape[1:], f32)
    sms[0, :, 0:width] = token_sums(1)
    do(tail_at + 1)

    dqt = dgt.at[pl.ds(0, aw)]
    dkt = dup.at[pl.ds(0, aw)]
    dat[...] = dot_tn(wo[...], n2t[...]).astype(bf16)

    def weight_grad(n, half, left, right):
        @pl.loop(0, nbig)
        def _(i):
            sl = pl.ds(pl.multiple_of(i * big, 16), big)
            value = dot_nt(left[sl, :], right[...])
            for j in (0, 1):
                g[(n % 2) * 16 + half * 8 + 2 * i + j, :, 0:aw] = value[rows * j : rows * (j + 1), :].astype(bf16)

    slot_free(5)
    weight_grad(nv, 1, n2t, att)
    do(tail_at + 2)
    hid[...] = (turn_index == toks - 1).astype(bf16)
    doff[...] = jnp.zeros(doff.shape, f32)

    def attend_back(h, carry):
        head = pl.ds(pl.multiple_of(h * hs, hs), hs)
        grad_v = []
        grad_k = []
        offsets = jnp.zeros((1, lanes), f32)
        for block in (0, 1):
            p, low, keys = softmax_block(h, head, block)
            q_rows = qt[head, low : low + half_tok]
            a_rows = dat[head, low : low + half_tok]
            grad_p = dot_tn(a_rows, vt[head, 0:keys])
            ds = (p * (grad_p - jnp.sum(p * grad_p, axis=1, keepdims=True))).astype(bf16)
            grad_v.append(dot_nn(a_rows, p.astype(bf16)))
            grad_k.append(dot_nn(q_rows, ds))
            dqt[head, low : low + half_tok] = dot_nt(kt[head, 0:keys], ds).astype(bf16)
            turned = dot_nn(ds, hid[0:keys, toks - keys : toks])
            padded = jnp.concatenate([turned, jnp.zeros((half_tok, lanes - keys), f32)], axis=1)
            lined = pltpu.roll(padded, half_tok, 1, stride=1, stride_axis=0)
            offsets = offsets + jnp.sum(lined, axis=0, keepdims=True)
        for dst, parts in ((dvt, grad_v), (dkt, grad_k)):
            dst[head, 0:half_tok] = (parts[0] + parts[1][:, 0:half_tok]).astype(bf16)
            dst[head, half_tok:toks] = parts[1][:, half_tok:toks].astype(bf16)
        doff[pl.ds(h, 1), :] = offsets
        return carry

    lax.fori_loop(0, heads // 2, attend_back, 0)
    do(tail_at + 3)
    lax.fori_loop(heads // 2, heads, attend_back, 0)
    weight_grad(nv, 0, n1t, dvt)
    core_part(nv, 0, 8, aw)
    slot_free(6)
    weight_grad(nq, 0, n1t, dqt)
    weight_grad(nq, 1, n1t, dkt)
    plane_send(nv, aw)
    core_part(nq, 0, 8, aw)
    stored(nv, aw)
    do(tail_at + 4)
    plane_send(nq, aw)
    stored(nq, aw)
    do(tail_at + 5)

    def first_back(i, acc):
        sl = pl.ds(pl.multiple_of(i * big, 16), big)
        gn = dot_nn(wq[sl, :], dqt[...]) + dot_nn(wk[sl, :], dkt[...]) + dot_nn(wv[sl, :], dvt[...])
        acc_o[sl, :] = gn
        v = gcol[sl, 0:1] * gn * xt_ref[sl, :].astype(f32)
        return acc + jnp.sum(v.reshape(big // 8, 8, toks), axis=0)

    back = jnp.sum(lax.fori_loop(0, nbig, first_back, zero8), axis=0, keepdims=True) * (1.0 / width)
    back = back * (r1 * r1 * r1)
    do(tail_at + 6)

    def first_norm(sl, carry):
        v = xt_ref[sl, :].astype(f32)
        gn = acc_o[sl, :]
        prod = gn * v * r1
        hi = prod.astype(bf16)
        wg2[sl, :] = hi
        wu2[sl, :] = (prod - hi.astype(f32)).astype(bf16)
        gtok_ref[sl, :] = (acc_n[sl, :] + r1 * gcol[sl, 0:1] * gn - v * back).astype(bf16)
        return carry

    over_rows(first_norm, 0)
    sms[0, :, 0:width] += token_sums(0)
    rest = doff[...]
    table = jnp.zeros((8, onehot.shape[0]), f32)
    for _ in range(3):
        part = rest.astype(bf16)
        table = table + dot_nt(part, onehot[...])
        rest = rest - part.astype(f32)
    sms[0, :, sms.shape[2] - onehot.shape[0] : sms.shape[2]] = table
    small_send(0)
    for k in range(7, TAIL_SLOTS):
        do(tail_at + k)
        if k < 13:
            small_step(k - 7)

    settle(gland.at[pl.ds(0, 7)], gain_s)
    slot_free(nv)
    slot_free(nq)
    turn_free(nv)
    turn_free(nq)
    for n in range(total):
        settle(span(hop_ref, 0, 4, width_of(n)), e1s.at[n])
    lax.fori_loop(0, chunks, lambda k, carry: (gather_sent(("f", k)), carry)[1], 0)

    @pl.when(outer)
    def _():
        for n in (nv - 1, nv, nq):
            sent(vbuf, zis, n)
        for n in range(total):
            for half in (0, 1):
                settle(cut1(ubuf, 0, width_of(n)), ur.at[n, half])

    @pl.when(inner)
    def _():
        for n in (nv, nq):
            u_free(n, aw)
        for n in range(total):
            settle(cut1(ubuf, 0, width_of(n)), ur.at[n, 1 - c])


def fused(tokens, cotangent, buckets, bias_table, gains, weights):
    toks, width = tokens.shape
    heads = bias_table.shape[1]
    rows, aw = weights[0].shape
    ff = weights[4].shape[1]
    sub = 256
    fw = 3 * sub
    chunks = ff // (2 * sub)
    total = chunks + 2
    lanes = 2 * toks
    small_lanes = (width + 127) // 128 * 128 + 128
    bucket_rows = jnp.pad(buckets, (0, 1), constant_values=-1)[None]
    vm = pl.BlockSpec(memory_space=pltpu.VMEM)
    hbm = pl.BlockSpec(memory_space=pltpu.HBM)
    dma = pltpu.SemaphoreType.DMA
    tok = lambda kind: pltpu.VMEM((width, toks), kind)
    inner_rows = pltpu.VMEM((aw, toks), bf16)
    blocks = lambda count: pltpu.VMEM((count, rows, fw), bf16)
    return pl.pallas_call(
        functools.partial(fused_kernel, chunks=chunks, heads=heads),
        out_shape=(
            jax.ShapeDtypeStruct((width, toks), bf16),
            jax.ShapeDtypeStruct((width, toks), bf16),
            jax.ShapeDtypeStruct((8, small_lanes), f32),
            *([jax.ShapeDtypeStruct((rows, aw), bf16)] * 4),
            *([jax.ShapeDtypeStruct((rows, ff), bf16)] * 3),
            jax.ShapeDtypeStruct((chunks * 16, rows, fw), bf16),
            jax.ShapeDtypeStruct((total * 8, rows, fw), bf16),
            jax.ShapeDtypeStruct((total * 4, rows, fw), bf16),
            jax.ShapeDtypeStruct((total * 2, rows, fw), bf16),
        ),
        in_specs=[vm] * 5 + [hbm] * 7,
        out_specs=[vm] * 3 + [hbm] * 11,
        scratch_shapes=[
            pltpu.VMEM((8, rows, 128), bf16),
            pltpu.VMEM((width, 128), f32),
            tok(bf16),
            tok(bf16),
            tok(f32),
            tok(f32),
            tok(f32),
            *([inner_rows] * 6),
            *([pltpu.VMEM((width, aw), bf16)] * 4),
            *([pltpu.VMEM((width, 2 * sub), bf16)] * 3),
            pltpu.VMEM((32, rows, sub), bf16),
            blocks(32),
            *([pltpu.VMEM((toks, 2 * sub), bf16)] * 3),
            blocks(16),
            blocks(8),
            blocks(6),
            blocks(6),
            blocks(4),
            blocks(6),
            blocks(4),
            pltpu.VMEM((8, lanes), f32),
            pltpu.VMEM((128, lanes), bf16),
            pltpu.VMEM((8, lanes), f32),
            pltpu.VMEM((6, 8, small_lanes), f32),
            pltpu.VMEM((6, 8, small_lanes), f32),
            dma(()),
            dma(()),
            *([dma((total,))] * 5),
            dma((4,)),
            *([dma((total,))] * 2),
            dma((total, 8)),
            dma((6,)),
            dma((total,)),
            dma((total, 2)),
            *([dma((total,))] * 2),
            *([dma((total, 2))] * 4),
            dma((total, 3)),
            dma((total,)),
            dma((total, 2)),
            dma((6,)),
            dma((6,)),
            pltpu.SemaphoreType.REGULAR,
            pltpu.SemaphoreType.REGULAR,
        ],
        compiler_params=pltpu.CompilerParams(
            collective_id=0, has_side_effects=True, vmem_limit_bytes=60 * 2**20
        ),
        cost_estimate=pl.CostEstimate(flops=57 * 10**9, bytes_accessed=10**8, transcendentals=10**7),
    )(tokens.T, cotangent.T, bucket_rows, bias_table.T, gains, *weights)


def widen_kernel(*refs):
    count = len(refs) // 2
    for src, dst in zip(refs[:count], refs[count:]):
        dst[...] = src[...].astype(dst.dtype)


def widen(out, gtok, grads):
    steps = 4
    width, toks = out.shape
    rows, ff = grads[-1].shape
    act = pl.BlockSpec((width // steps, toks), lambda i: (i, 0))
    small = pl.BlockSpec(grads[0].shape, lambda i: (0, 0))
    large = pl.BlockSpec((rows, ff // steps), lambda i: (0, i))
    specs = [act] * 2 + [small] * 4 + [large] * 3
    return pl.pallas_call(
        widen_kernel,
        grid=(steps,),
        out_shape=[jax.ShapeDtypeStruct(v.shape, bf16) for v in (out, gtok)]
        + [jax.ShapeDtypeStruct(v.shape, f32) for v in grads],
        in_specs=specs,
        out_specs=specs,
        compiler_params=pltpu.CompilerParams(vmem_limit_bytes=60 * 2**20),
        cost_estimate=pl.CostEstimate(flops=10**7, bytes_accessed=2 * 10**7, transcendentals=0),
    )(out, gtok, *grads)


def fused_body(
    tokens,
    cotangent,
    buckets,
    bias_table,
    attn_gain,
    w_query,
    w_key,
    w_value,
    w_output,
    ffn_gain,
    w_gate,
    w_up,
    w_down,
):
    rows = w_query.shape[0]
    lane = lax.broadcasted_iota(jnp.int32, (rows, 128), 1)
    gains = jnp.where(lane == 0, attn_gain[:, None], ffn_gain[:, None])
    weights = (w_query, w_key, w_value, w_output, w_gate, w_up, w_down)
    out, gtok, small, *grads = fused(tokens, cotangent, buckets, bias_table, gains, weights)
    out, gtok, *grads = widen(out, gtok, grads[:7])
    own = lax.dynamic_slice(small, (0, lax.axis_index("shard") * rows), (2, rows))
    table = small[0 : bias_table.shape[1], small.shape[1] - 128 :][:, 0 : bias_table.shape[0]].T
    return (out.T, gtok.T, own[0], *grads[:4], own[1], *grads[4:], table)


def solution(mesh):
    chosen = body
    if mesh.shape["shard"] == 8 and mesh.shape["rep"] == 4:
        chosen = fused_body
    return jax.shard_map(
        chosen,
        mesh=mesh,
        in_specs=(
            P(("shard", "rep"), None),
            P(("shard", "rep"), None),
            P(),
            P(),
            P("shard"),
            P("shard", None),
            P("shard", None),
            P("shard", None),
            P("shard", None),
            P("shard"),
            P("shard", None),
            P("shard", None),
            P("shard", None),
        ),
        out_specs=(
            P(("shard", "rep"), None),
            P(("shard", "rep"), None),
            P("shard"),
            P("shard", None),
            P("shard", None),
            P("shard", None),
            P("shard", None),
            P("shard"),
            P("shard", None),
            P("shard", None),
            P("shard", None),
            P(),
        ),
        check_vma=False,
    )
```

```python
import functools

import jax
import jax.numpy as jnp
from jax import lax
from jax.experimental import pallas as pl
from jax.experimental.pallas import tpu as pltpu
from jax.sharding import PartitionSpec as P

BLOCK = 256
MESH = pl.DeviceIdType.MESH
f32 = jnp.float32
bf16 = jnp.bfloat16


norm_eps = 1e-06
masked_score = -1e30
highest = lax.Precision.HIGHEST


def norm_local(row_values, gain_vector):
    return (
        row_values
        * lax.rsqrt(jnp.mean(row_values * row_values, axis=-1, keepdims=True) + norm_eps)
        * gain_vector
    )


def gelu_tanh(values_in):
    return jax.nn.gelu(values_in, approximate=True)


def diagonal_total(matrix):
    head_count, row_count, key_count = matrix.shape
    flipped = matrix[:, :, ::-1]
    padded = jnp.concatenate(
        [flipped, jnp.zeros((head_count, row_count, row_count), jnp.float32)], axis=2
    )
    flat_rows = padded.reshape(head_count, row_count * (key_count + row_count))
    flat_rows = flat_rows[:, : row_count * (key_count + row_count - 1)]
    return jnp.sum(flat_rows.reshape(head_count, row_count, key_count + row_count - 1), axis=1)


def toeplitz_grid(offset_bias, row_count, length):
    head_count = offset_bias.shape[0]
    span = length + row_count - 1
    flipped = offset_bias[:, ::-1]
    rotated = jnp.concatenate([flipped[:, row_count - 1 :], flipped[:, : row_count - 1]], axis=1)
    tiled = jnp.tile(rotated, (1, row_count))[:, : row_count * (span - 1)]
    return tiled.reshape(head_count, row_count, span - 1)[:, :, :length]


def body(
    tokens,
    cotangent,
    buckets,
    bias_table,
    attn_gain,
    w_query,
    w_key,
    w_value,
    w_output,
    ffn_gain,
    w_gate,
    w_up,
    w_down,
):
    length = tokens.shape[0]
    bucket_count = bias_table.shape[0]
    head_count = bias_table.shape[1]
    inner_width = w_query.shape[1]
    ff_width = w_gate.shape[1]
    owner_rows = w_query.shape[0]
    head_size = inner_width // head_count
    block_rows = min(512, length)
    block_count = length // block_rows
    residual = tokens.astype(jnp.float32)
    attn_set = (
        lax.all_gather(attn_gain, "shard", axis=0, tiled=True),
        lax.all_gather(w_query, "shard", axis=0, tiled=True),
        lax.all_gather(w_key, "shard", axis=0, tiled=True),
        lax.all_gather(w_value, "shard", axis=0, tiled=True),
        lax.all_gather(w_output, "shard", axis=0, tiled=True),
    )
    gain_one = attn_set[0].astype(jnp.float32)
    normed_one = norm_local(residual, gain_one).astype(jnp.bfloat16)

    def project(weight):
        product = jnp.dot(normed_one, weight, preferred_element_type=jnp.float32)
        return product.astype(jnp.bfloat16).reshape(length, head_count, head_size)

    queries = project(attn_set[1])
    key_rows = project(attn_set[2])
    value_rows = project(attn_set[3])
    one_hot = (buckets[:, None] == jnp.arange(bucket_count, dtype=jnp.int32)[None, :]).astype(
        jnp.float32
    )
    offset_bias = jnp.dot(one_hot, bias_table.astype(jnp.float32), precision=highest).T
    block_starts = jnp.arange(block_count, dtype=jnp.int32) * block_rows
    key_index = jnp.arange(length, dtype=jnp.int32)

    def block_scores(first_row, query_block):
        query_index = first_row + jnp.arange(block_rows, dtype=jnp.int32)
        bias_grid = toeplitz_grid(offset_bias, block_rows, length)
        scores = (
            jnp.einsum("qhd,khd->hqk", query_block, key_rows, preferred_element_type=jnp.float32)
            + bias_grid
        )
        allowed = key_index[None, :] // BLOCK <= query_index[:, None] // BLOCK
        return jnp.where(allowed[None], scores, masked_score)

    def attend(first_row):
        scores = block_scores(first_row, queries)
        row_max = jnp.max(scores, axis=-1, keepdims=True)
        exp_scores = jnp.exp(scores - row_max)
        totals = jnp.sum(exp_scores, axis=-1, keepdims=True)
        probability = (exp_scores / totals).astype(jnp.bfloat16)
        mixed_rows = jnp.einsum(
            "hqk,khd->qhd", probability, value_rows, preferred_element_type=jnp.float32
        )
        return (mixed_rows, (row_max + jnp.log(totals))[..., 0])

    mixed_blocks, log_totals = lax.map(attend, block_starts)
    attended = mixed_blocks.reshape(length, inner_width).astype(jnp.bfloat16)
    middle = residual + jnp.einsum(
        "ti,di->td", attended, attn_set[4], preferred_element_type=jnp.float32
    )
    ffn_set = (
        lax.all_gather(ffn_gain, "shard", axis=0, tiled=True),
        lax.all_gather(w_gate, "shard", axis=0, tiled=True),
        lax.all_gather(w_up, "shard", axis=0, tiled=True),
        lax.all_gather(w_down, "shard", axis=0, tiled=True),
    )
    gain_two = ffn_set[0].astype(jnp.float32)
    normed_two = norm_local(middle, gain_two).astype(jnp.bfloat16)
    gate_values = jnp.dot(normed_two, ffn_set[1], preferred_element_type=jnp.float32)
    up_values = jnp.dot(normed_two, ffn_set[2], preferred_element_type=jnp.float32)
    activated, gelu_pullback = jax.vjp(gelu_tanh, gate_values)
    hidden = (activated * up_values).astype(jnp.bfloat16)
    layer_out = (
        middle + jnp.einsum("tf,df->td", hidden, ffn_set[3], preferred_element_type=jnp.float32)
    ).astype(jnp.bfloat16)
    ffn_set = (
        lax.all_gather(ffn_gain, "shard", axis=0, tiled=True),
        lax.all_gather(w_gate, "shard", axis=0, tiled=True),
        lax.all_gather(w_up, "shard", axis=0, tiled=True),
        lax.all_gather(w_down, "shard", axis=0, tiled=True),
    )
    grad_w_down = jnp.einsum("td,tf->df", cotangent, hidden, preferred_element_type=jnp.float32)
    grad_hidden = jnp.dot(cotangent, ffn_set[3], preferred_element_type=jnp.float32)
    grad_gate = gelu_pullback(grad_hidden * up_values)[0].astype(jnp.bfloat16)
    grad_up = (grad_hidden * activated).astype(jnp.bfloat16)
    grad_w_gate = jnp.einsum("td,tf->df", normed_two, grad_gate, preferred_element_type=jnp.float32)
    grad_w_up = jnp.einsum("td,tf->df", normed_two, grad_up, preferred_element_type=jnp.float32)
    grad_normed_two = jnp.einsum(
        "tf,df->td", grad_gate, ffn_set[1], preferred_element_type=jnp.float32
    )
    grad_normed_two = grad_normed_two + jnp.einsum(
        "tf,df->td", grad_up, ffn_set[2], preferred_element_type=jnp.float32
    )
    middle_part, grad_gain_two = jax.vjp(norm_local, middle, gain_two)[1](grad_normed_two)
    grad_middle = cotangent.astype(jnp.float32) + middle_part
    ffn_shards = (
        lax.psum_scatter(grad_w_gate.astype(jnp.bfloat16), "shard", scatter_dimension=0, tiled=True),
        lax.psum_scatter(grad_w_up.astype(jnp.bfloat16), "shard", scatter_dimension=0, tiled=True),
        lax.psum_scatter(grad_w_down.astype(jnp.bfloat16), "shard", scatter_dimension=0, tiled=True),
    )
    attn_set = (
        lax.all_gather(attn_gain, "shard", axis=0, tiled=True),
        lax.all_gather(w_query, "shard", axis=0, tiled=True),
        lax.all_gather(w_key, "shard", axis=0, tiled=True),
        lax.all_gather(w_value, "shard", axis=0, tiled=True),
        lax.all_gather(w_output, "shard", axis=0, tiled=True),
    )
    grad_branch = grad_middle.astype(jnp.bfloat16)
    grad_w_output = jnp.einsum(
        "td,ti->di", grad_branch, attended, preferred_element_type=jnp.float32
    )
    grad_attended = jnp.einsum(
        "td,di->ti", grad_branch, attn_set[4], preferred_element_type=jnp.float32
    )
    grad_attended = grad_attended.astype(jnp.bfloat16).reshape(length, head_count, head_size)

    def attend_back(carried, block_input):
        grad_keys, grad_values, grad_offsets = carried
        first_row, log_total = block_input
        scores = block_scores(first_row, queries)
        probability = jnp.exp(scores - log_total[..., None])
        grad_probs = jnp.einsum(
            "qhd,khd->hqk", grad_attended, value_rows, preferred_element_type=jnp.float32
        )
        inner_sum = jnp.sum(probability * grad_probs, axis=-1, keepdims=True)
        grad_scores = (probability * (grad_probs - inner_sum)).astype(jnp.bfloat16)
        grad_values = grad_values + jnp.einsum(
            "hqk,qhd->khd",
            probability.astype(jnp.bfloat16),
            grad_attended,
            preferred_element_type=jnp.float32,
        )
        grad_keys = grad_keys + jnp.einsum(
            "hqk,qhd->khd", grad_scores, queries, preferred_element_type=jnp.float32
        )
        grad_queries = jnp.einsum(
            "hqk,khd->qhd", grad_scores, key_rows, preferred_element_type=jnp.float32
        )
        diagonal_sums = diagonal_total(grad_scores.astype(jnp.float32))
        offset_piece = grad_offsets
        grad_offsets = offset_piece + diagonal_sums
        return ((grad_keys, grad_values, grad_offsets), grad_queries)

    zero_rows = jnp.zeros((length, head_count, head_size), jnp.float32)
    zero_offsets = jnp.zeros((head_count, 2 * length - 1), jnp.float32)
    (grad_keys, grad_values, grad_offsets), query_blocks = lax.scan(
        attend_back, (zero_rows, zero_rows, zero_offsets), (block_starts, log_totals)
    )
    grad_queries = query_blocks.reshape(length, inner_width).astype(jnp.bfloat16)
    grad_keys = grad_keys.reshape(length, inner_width).astype(jnp.bfloat16)
    grad_values = grad_values.reshape(length, inner_width).astype(jnp.bfloat16)
    grad_w_query = jnp.einsum(
        "td,ti->di", normed_one, grad_queries, preferred_element_type=jnp.float32
    )
    grad_w_key = jnp.einsum("td,ti->di", normed_one, grad_keys, preferred_element_type=jnp.float32)
    grad_w_value = jnp.einsum(
        "td,ti->di", normed_one, grad_values, preferred_element_type=jnp.float32
    )
    grad_normed_one = jnp.einsum(
        "ti,di->td", grad_queries, attn_set[1], preferred_element_type=jnp.float32
    )
    grad_normed_one = grad_normed_one + jnp.einsum(
        "ti,di->td", grad_keys, attn_set[2], preferred_element_type=jnp.float32
    )
    grad_normed_one = grad_normed_one + jnp.einsum(
        "ti,di->td", grad_values, attn_set[3], preferred_element_type=jnp.float32
    )
    rows_part, grad_gain_one = jax.vjp(norm_local, residual, gain_one)[1](grad_normed_one)
    grad_tokens = (grad_middle + rows_part).astype(jnp.bfloat16)
    grad_table = jnp.dot(grad_offsets, one_hot, precision=highest).T
    owner_start = lax.axis_index("shard") * owner_rows
    attn_shards = (
        lax.psum_scatter(grad_w_query.astype(jnp.bfloat16), "shard", scatter_dimension=0, tiled=True),
        lax.psum_scatter(grad_w_key.astype(jnp.bfloat16), "shard", scatter_dimension=0, tiled=True),
        lax.psum_scatter(grad_w_value.astype(jnp.bfloat16), "shard", scatter_dimension=0, tiled=True),
        lax.psum_scatter(grad_w_output.astype(jnp.bfloat16), "shard", scatter_dimension=0, tiled=True),
    )
    summed = lax.psum(
        (
            attn_shards[0],
            attn_shards[1],
            attn_shards[2],
            attn_shards[3],
            ffn_shards[0],
            ffn_shards[1],
            ffn_shards[2],
        ),
        "rep",
    )
    small_total = lax.psum((grad_gain_one, grad_gain_two, grad_table), ("shard", "rep"))
    gain_one_own = lax.dynamic_slice_in_dim(small_total[0], owner_start, owner_rows, 0)
    gain_two_own = lax.dynamic_slice_in_dim(small_total[1], owner_start, owner_rows, 0)
    return (
        layer_out,
        grad_tokens,
        gain_one_own,
        summed[0].astype(jnp.float32),
        summed[1].astype(jnp.float32),
        summed[2].astype(jnp.float32),
        summed[3].astype(jnp.float32),
        gain_two_own,
        summed[4].astype(jnp.float32),
        summed[5].astype(jnp.float32),
        summed[6].astype(jnp.float32),
        small_total[2],
    )

HEAD_SLOTS = 7
TAIL_SLOTS = 14
HELPED = (1, 2, 3, 4, 5, 6)
SLOTS = {
    "send": (0, 0, 0, 2, 2, 2, 2),
    "forward": (1, 1, 1, 6, 7, 8, 11),
    "swap": (2, 3, 4, 8, 10, 11, 17),
    "get_forward": (1, 6, 7, 10, 11, 15, 16),
    "get_swap": (3, 8, 9, 11, 13, 16, 18),
    "turn": (10, 12, 15, 16, 20, 21, 24, 27, 29),
    "rep": (13, 14, 19, 20, 23, 25, 26, 30, 31),
    "mid": (17, 18, 20, 22, 24, 26, 29, 31, 32),
    "last": (18, 21, 23, 24, 25, 28, 30, 32, 33),
}


def dot_nn(a, b):
    return lax.dot_general(a, b, (((1,), (0,)), ((), ())), preferred_element_type=f32)


def dot_nt(a, b):
    return lax.dot_general(a, b, (((1,), (1,)), ((), ())), preferred_element_type=f32)


def dot_tn(a, b):
    return lax.dot_general(a, b, (((0,), (0,)), ((), ())), preferred_element_type=f32)


def fused_kernel(
    xt_ref,
    ct_ref,
    buckets_ref,
    table_ref,
    gains_ref,
    wq_ref,
    wk_ref,
    wv_ref,
    wo_ref,
    wg_ref,
    wu_ref,
    wd_ref,
    out_ref,
    gtok_ref,
    small_ref,
    gq_ref,
    gk_ref,
    gv_ref,
    go_ref,
    gg_ref,
    gu_ref,
    gd_ref,
    land_ref,
    sum_ref,
    hop_ref,
    turn_ref,
    gland,
    gcol,
    n1t,
    n2t,
    mid,
    acc_o,
    acc_n,
    qt,
    kt,
    vt,
    att,
    dat,
    dvt,
    wq,
    wk,
    wv,
    wo,
    wg2,
    wu2,
    wd2,
    wload,
    g,
    hid,
    dgt,
    dup,
    rc,
    stage_t,
    stage_v,
    vbuf,
    zi,
    zm,
    ubuf,
    revb,
    onehot,
    doff,
    sms,
    smr,
    gain_s,
    gain_r,
    gsend,
    gloc,
    g1r,
    g2r,
    gpr,
    load_sem,
    e0s,
    e0r,
    sum_sem,
    stage_sem,
    e1s,
    e1r,
    e2s,
    e2r,
    zis,
    zir,
    zms,
    zmr,
    us,
    ul,
    ur,
    sss,
    ssr,
    zcredit,
    mcredit,
    *,
    chunks,
    heads,
):
    width = xt_ref.shape[0]
    toks = xt_ref.shape[1]
    rows = gains_ref.shape[0]
    fw = land_ref.shape[2]
    sub = fw // 3
    aw = wq_ref.shape[1]
    hs = aw // heads
    total = chunks + 2
    eps = 1e-06
    lanes = revb.shape[1]
    big = 2 * rows
    nbig = width // big

    s = lax.axis_index("shard")
    r = lax.axis_index("rep")
    c = s % 2
    x = (s // 2) % 2
    y = s // 4
    sc = s + 1 - 2 * c
    sx = s + 2 - 4 * x
    sy = s + 4 - 8 * y
    bx = sx - c
    by = sy - c
    bd = (1 - y) * 4 + (1 - x) * 2
    b_own = s - c
    mate = r + 1 - 2 * (r % 2)
    inner = (r == 1) | (r == 2)
    outer = (r == 0) | (r == 3)

    def remote(src, dst, ssem, rsem, dev):
        return pltpu.make_async_remote_copy(
            src_ref=src, dst_ref=dst, send_sem=ssem, recv_sem=rsem, device_id=dev, device_id_type=MESH
        )

    def settle(ref, sem):
        pltpu.make_async_copy(ref, ref, sem).wait()

    barrier = pltpu.get_barrier_semaphore()
    near = [(sc, r), (bx, r), (bx + 1, r), (by, r), (by + 1, r), (bd, r), (bd + 1, r), (s, mate), (sc, mate)]
    for dev in near:
        pl.semaphore_signal(barrier, inc=1, device_id=dev, device_id_type=MESH)

    @pl.when(inner)
    def _():
        pl.semaphore_signal(barrier, inc=1, device_id=(s, 3 - r), device_id_type=MESH)

    @pl.when(inner)
    def _():
        pl.semaphore_wait(barrier, len(near) + 1)

    @pl.when(outer)
    def _():
        pl.semaphore_wait(barrier, len(near))

    def place(chunk, index):
        kind, k = chunk
        if kind == "a":
            return g.at[16 + index, :, pl.ds(k * aw, aw)]
        return land_ref.at[k * 16 + index]

    def places(chunk, count):
        kind, k = chunk
        if kind == "a":
            return g.at[pl.ds(16, count), :, pl.ds(k * aw, aw)]
        return land_ref.at[pl.ds(0, count)]

    def any_of(value, options):
        return functools.reduce(jnp.logical_or, [value == option for option in options], jnp.bool_(False))

    def helped(chunk):
        kind, k = chunk
        return False if kind == "a" else any_of(k, HELPED)

    def active(chunk):
        kind, k = chunk
        return True if kind == "a" else jnp.logical_not(any_of(k, HELPED)) | (r % 2 == k % 2)

    def when(condition, then):
        if condition is True:
            then()
        elif condition is not False:
            pl.when(condition)(then)

    def columns(k, half):
        return pl.ds(pl.multiple_of((2 * k + half) * sub, sub), sub)

    def own_parts(chunk, half):
        kind, k = chunk
        dst = place(chunk, half * 8 + s)
        if kind == "a":
            return [(((wq_ref, wk_ref), (wv_ref, wo_ref))[k][half], dst)]
        return [
            (ref.at[:, columns(k, half)], dst.at[:, pl.ds(j * sub, sub)]) for j, ref in enumerate((wg_ref, wu_ref, wd_ref))
        ]

    def at(chunk):
        kind, k = chunk
        return k if kind == "a" else k + 2

    def gather_send(chunk):
        i = at(chunk)

        def cross():
            for half in (0, 1):
                for src, dst in own_parts(chunk, half):
                    remote(src, dst, gsend.at[i], g1r.at[i], (bx + half, r)).start()
                    remote(src, dst, gsend.at[i], g1r.at[i], (by + half, r)).start()

        when(active(chunk), cross)
        for half in (0, 1):
            for src, dst in own_parts(chunk, half):
                remote(src, dst, gsend.at[i], gpr.at[i], (sc, r)).start()
                pltpu.make_async_copy(src, dst, gloc.at[i]).start()

    def hand_over(chunk, blocks, sem):
        i = at(chunk)

        def hand():
            for b in blocks:
                spot = place(chunk, c * 8 + b)
                remote(spot, spot, gsend.at[i], sem.at[i], (s, mate)).start()

        if chunk[0] == "f":
            pl.when(helped(chunk) & active(chunk))(hand)
        for b in blocks:
            spot = place(chunk, c * 8 + b)
            remote(spot, spot, gsend.at[i], gpr.at[i], (sc, r)).start()

    def gather_forward(chunk):
        i = at(chunk)
        settle(places(chunk, 4), g1r.at[i])

        def cross():
            one = place(chunk, c * 8 + bx)
            two = place(chunk, c * 8 + by + 1)
            remote(one, one, gsend.at[i], g2r.at[i], (sy, r)).start()
            remote(two, two, gsend.at[i], g2r.at[i], (sx, r)).start()

        when(active(chunk), cross)
        hand_over(chunk, (bx, bx + 1, by, by + 1), g1r)

    def gather_swap(chunk):
        settle(places(chunk, 2), g2r.at[at(chunk)])
        hand_over(chunk, (bd, bd + 1), g2r)

    def gather_done(chunk):
        i = at(chunk)
        settle(places(chunk, 8), gpr.at[i])
        settle(places(chunk, 2), gloc.at[i])

    def gather_sent(chunk):
        i = at(chunk)
        does = active(chunk)
        if does is True:
            settle(places(chunk, 14), gsend.at[i])
            return
        pl.when(does & helped(chunk))(lambda: settle(places(chunk, 20), gsend.at[i]))
        pl.when(does & jnp.logical_not(helped(chunk)))(lambda: settle(places(chunk, 14), gsend.at[i]))
        pl.when(jnp.logical_not(does))(lambda: settle(places(chunk, 8), gsend.at[i]))

    def ahead(stage, k, mine):
        chunk = ("f", k)
        does = active(chunk) if mine else jnp.logical_not(active(chunk))
        pl.when((k < chunks) & does)(lambda: stage(chunk))

    def cut(ref, w):
        return ref if w == fw else ref.at[:, :, pl.ds(0, w)]

    def cut1(ref, index, w):
        return ref.at[index] if w == fw else ref.at[index, :, pl.ds(0, w)]

    def span(ref, start, count, w):
        return ref.at[pl.ds(start, count)] if w == fw else ref.at[pl.ds(start, count), :, pl.ds(0, w)]

    def get(ref, index, w):
        return ref[index] if w == fw else ref[index, :, 0:w]

    def put(ref, index, w, value):
        if w == fw:
            ref[index] = value
        else:
            ref[index, :, 0:w] = value

    def add_to(dst, i, src, j, w):
        put(dst, i, w, get(dst, i, w) + get(src, j, w))

    def core_part(n, b, count, w):
        slot = n % 2
        remote(
            span(g, slot * 16 + (1 - c) * 8 + b, count, w), span(rc, slot * 8 + b, count, w), e0s.at[n], e0r.at[n], (sc, r)
        ).start()

    def plane_send(n, w):
        slot = n % 2
        base = slot * 16 + c * 8
        settle(span(rc, slot * 8, 8, w), e0r.at[n])
        order = []
        for k, kx, ky in ((0, 1 - y, 1 - x), (1, y, x)):
            order.append((4 * kx + 2 * (1 - x), sx, 2 * k))
            order.append((4 * (1 - y) + 2 * ky + 1, sy, 2 * k + 1))
        order += [(b, None, None) for b in (4 * (1 - y) + 2 * x, 4 * y + 2 * (1 - x) + 1, b_own, b_own + 1)]

        def store(i):
            b = order[i][0]
            return pltpu.make_async_copy(cut1(g, base + b, w), cut1(sum_ref, n * 8 + b, w), sum_sem.at[n, i])

        for i, (b, _, _) in enumerate(order):
            add_to(g, base + b, rc, slot * 8 + b, w)
            store(i).start()
        for i, (b, dev, spot) in enumerate(order[:4]):
            store(i).wait()
            remote(
                cut1(sum_ref, n * 8 + b, w), cut1(hop_ref, n * 4 + spot, w), e1s.at[n], e1r.at[n, spot // 2], (dev, r)
            ).start()

    def stored(n, w):
        for i in range(4, 8):
            settle(cut1(sum_ref, 0, w), sum_sem.at[n, i])

    def slot_free(n):
        settle(span(g, 0, 8, width_of(n)), e0s.at[n])

    def turn_free(n):
        settle(span(turn_ref, 0, 2, width_of(n)), e2s.at[n])

    def guarded(n, least, then):
        if isinstance(n, int):
            if n >= least:
                then()
        else:
            pl.when(n >= least)(then)

    def turn_loads(n, w):
        base = (n % 2) * 4
        first = n * 8 + 4 * (1 - y) + 2 * x
        second = n * 8 + 4 * y + 2 * (1 - x) + 1
        return [
            pltpu.make_async_copy(cut1(sum_ref, first, w), cut1(stage_t, base, w), stage_sem.at[0]),
            pltpu.make_async_copy(cut1(sum_ref, second, w), cut1(stage_t, base + 1, w), stage_sem.at[1]),
            pltpu.make_async_copy(span(hop_ref, n * 4, 2, w), span(stage_t, base + 2, 2, w), stage_sem.at[2]),
        ]

    def turn_start(n, w):
        guarded(n, 2, lambda: turn_free(n - 2))
        settle(span(hop_ref, 0, 2, w), e1r.at[n, 0])
        for load in turn_loads(n, w):
            load.start()

    def turn_end(n, w):
        base = (n % 2) * 4
        for load in turn_loads(n, w):
            load.wait()
        for j, dev in ((0, sy), (1, sx)):
            add_to(stage_t, base + j, stage_t, base + 2 + j, w)
            remote(cut1(stage_t, base + j, w), cut1(turn_ref, n * 2 + j, w), e2s.at[n], e2r.at[n], (dev, r)).start()

    def rep_loads(n, w):
        return [
            pltpu.make_async_copy(span(sum_ref, n * 8 + b_own, 2, w), span(stage_v, 0, 2, w), stage_sem.at[3]),
            pltpu.make_async_copy(span(hop_ref, n * 4 + 2, 2, w), span(stage_v, 2, 2, w), stage_sem.at[4]),
            pltpu.make_async_copy(span(turn_ref, n * 2, 2, w), span(stage_v, 4, 2, w), stage_sem.at[5]),
        ]

    def rep_start(n, w):
        settle(span(hop_ref, 0, 2, w), e1r.at[n, 1])
        settle(span(turn_ref, 0, 2, w), e2r.at[n])
        for load in rep_loads(n, w):
            load.start()

    def rep_end(n, w):
        third = n % 3

        def outer_room():
            guarded(n, 3, lambda: pl.when(outer)(lambda: sent(vbuf, zis, n - 3)))
            guarded(n, 2, lambda: pl.when(outer)(lambda: pl.semaphore_wait(zcredit, 1)))

        outer_room()
        for load in rep_loads(n, w):
            load.wait()
        for j in (c, 1 - c):
            value = get(stage_v, j, w).astype(f32) + get(stage_v, 2 + j, w).astype(f32)
            value = value + get(stage_v, 4 + j, w).astype(f32)
            put(vbuf, third * 2 + j, w, value.astype(bf16))

            @pl.when(outer)
            def _():
                remote(
                    cut1(vbuf, third * 2 + j, w), cut1(zi, (n % 2) * 2 + j, w), zis.at[n, j], zir.at[n, j], (s, mate)
                ).start()

    def sent(ref, sems, n):
        for j in (0, 1):
            settle(cut1(ref, 0, width_of(n)), sems.at[n, j])

    def width_of(n):
        return fw if not isinstance(n, int) or n < chunks else aw

    def rep_turn(n, w):
        third = n % 3

        @pl.when(inner)
        def _():
            guarded(n, 3, lambda: pl.semaphore_wait(mcredit, 1))
            for j in (c, 1 - c):
                settle(cut1(zi, j, w), zir.at[n, j])
                add_to(vbuf, third * 2 + j, zi, (n % 2) * 2 + j, w)
                remote(
                    cut1(vbuf, third * 2 + j, w), cut1(zm, third * 2 + j, w), zms.at[n, j], zmr.at[n, j], (s, 3 - r)
                ).start()
            guarded(total - 1 - n, 2, lambda: give_credit(zcredit, (s, mate)))

    def give_credit(sem, dev):
        pl.semaphore_signal(sem, inc=1, device_id=dev, device_id_type=MESH)

    def result(n, half, block):
        if isinstance(n, int) and n >= chunks:
            return [(block, ((gv_ref, go_ref), (gq_ref, gk_ref))[n - chunks][half])]
        return [
            (block.at[:, pl.ds(j * sub, sub)], ref.at[:, columns(n, half)])
            for j, ref in enumerate((gg_ref, gu_ref, gd_ref))
        ]

    def u_free(n, w):
        slot = n % 2
        for k in (0, 1, 2):
            settle(cut1(ubuf, slot * 2, w), us.at[n, k])
        settle(cut1(ubuf, slot * 2, w), ul.at[n])

    def rep_last(n, w):
        slot = n % 2
        third = n % 3

        @pl.when(inner)
        def _():
            guarded(n, 2, lambda: u_free(n - 2, width_of(n - 2)))

            def both(j):
                settle(cut1(zm, j, w), zmr.at[n, j])
                value = get(vbuf, third * 2 + j, w).astype(f32) + get(zm, third * 2 + j, w).astype(f32)
                put(ubuf, slot * 2 + j, w, value.astype(bf16))

            def finish_keep(half):
                for src, dst in result(n, half, cut1(ubuf, slot * 2 + c, w)):
                    remote(src, dst, us.at[n, 0], ur.at[n, half], (s, mate)).start()
                    pltpu.make_async_copy(src, dst, ul.at[n]).start()

            def finish_give(half):
                for src, dst in result(n, half, cut1(ubuf, slot * 2 + 1 - c, w)):
                    remote(src, dst, us.at[n, 1], ur.at[n, half], (sc, mate)).start()
                    remote(src, dst, us.at[n, 2], ur.at[n, half], (sc, r)).start()

            for j, finish in ((c, finish_keep), (1 - c, finish_give)):
                both(j)
                if w == fw:
                    finish(c)
                else:
                    pl.when(c == 0)(functools.partial(finish, 0))
                    pl.when(c == 1)(functools.partial(finish, 1))
            guarded(total - 1 - n, 3, lambda: give_credit(mcredit, (s, 3 - r)))
            sent(vbuf, zms, n)

    def gathers(stage, mine):
        return lambda k: ahead(stage, k, mine)

    def reduces(stage):
        return lambda n: stage(n, width_of(n))

    order = (
        ("swap", gathers(gather_swap, True)),
        ("forward", gathers(gather_forward, True)),
        ("send", lambda k: gather_send(("f", k))),
        ("turn", reduces(turn_start)),
        ("rep", reduces(rep_start)),
        ("last", reduces(rep_last)),
        ("mid", reduces(rep_turn)),
        ("turn", reduces(turn_end)),
        ("rep", reduces(rep_end)),
        ("get_forward", gathers(gather_forward, False)),
        ("get_swap", gathers(gather_swap, False)),
    )
    loop_at = HEAD_SLOTS
    tail_at = HEAD_SLOTS + 2 * chunks

    def do(slot):
        for name, stage in order:
            for n, spot in enumerate(SLOTS[name]):
                if spot == slot:
                    stage(n)

    def do_in_loop(t, side):
        for name, stage in order:
            pairs = [
                ((spot - loop_at) // 2, n)
                for n, spot in enumerate(SLOTS[name])
                if loop_at <= spot < tail_at and (spot - loop_at) % 2 == side
            ]
            if pairs:
                n = sum([jnp.where(t == step, number, 0) for step, number in pairs], jnp.int32(0))
                pl.when(any_of(t, [step for step, _ in pairs]))(functools.partial(stage, n))

    def small_send(step):
        if step < 3:
            dev = ((sc, r), (sx, r), (sy, r))[step]
            remote(sms.at[step], smr.at[step], sss.at[step], ssr.at[step], dev).start()
        elif step == 3:

            @pl.when(outer)
            def _():
                remote(sms.at[3], smr.at[3], sss.at[3], ssr.at[3], (s, mate)).start()
        elif step == 4:

            @pl.when(inner)
            def _():
                remote(sms.at[4], smr.at[4], sss.at[4], ssr.at[4], (s, 3 - r)).start()
        else:

            @pl.when(inner)
            def _():
                remote(sms.at[5], smr.at[5], sss.at[5], ssr.at[5], (s, mate)).start()

    def small_step(step):
        def take():
            settle(smr.at[step], ssr.at[step])
            settle(sms.at[step], sss.at[step])
            if step < 2:
                sms[step + 1] = sms[step] + smr[step]
            elif step == 2:
                sms[3] = sms[2] + smr[2]

        if step < 3:
            take()
            small_send(step + 1)
        elif step == 3:

            @pl.when(inner)
            def _():
                settle(smr.at[3], ssr.at[3])
                sms[4] = sms[3] + smr[3]

            @pl.when(outer)
            def _():
                settle(sms.at[3], sss.at[3])

            small_send(4)
        elif step == 4:

            @pl.when(inner)
            def _():
                settle(smr.at[4], ssr.at[4])
                settle(sms.at[4], sss.at[4])
                sms[5] = sms[4] + smr[4]
                small_ref[...] = sms[5]

            small_send(5)
        else:

            @pl.when(inner)
            def _():
                settle(sms.at[5], sss.at[5])

            @pl.when(outer)
            def _():
                settle(smr.at[5], ssr.at[5])
                small_ref[...] = smr[5]

    tile = 64
    tiles = width // tile

    def over_rows(body, start):
        def step(i, carry):
            return body(pl.ds(pl.multiple_of(i * tile, tile), tile), carry)

        return lax.fori_loop(0, tiles, step, start)

    def fold(value):
        return jnp.sum(value.reshape(tile // 8, 8, toks), axis=0)

    zero8 = jnp.zeros((8, toks), f32)

    gather_send(("a", 0))
    gdst = gland.at[s]
    for k, dev in enumerate([(sc, r), (bx, r), (bx + 1, r), (by, r), (by + 1, r), (bd, r), (bd + 1, r)]):
        remote(gains_ref, gdst, gain_s, gain_r, dev).start()
    pltpu.make_async_copy(gains_ref, gdst, load_sem.at[1]).start()
    gather_send(("a", 1))
    do(0)

    def square_sum(sl, acc):
        v = xt_ref[sl, :].astype(f32)
        return acc + fold(v * v)

    ssum = jnp.sum(over_rows(square_sum, zero8), axis=0, keepdims=True)
    r1 = lax.rsqrt(ssum * (1.0 / width) + eps)

    bucket_index = lax.broadcasted_iota(jnp.int32, onehot.shape, 0)
    onehot[...] = (bucket_index == buckets_ref[...]).astype(bf16)
    turn_index = lax.broadcasted_iota(jnp.int32, (toks, toks), 0) + lax.broadcasted_iota(jnp.int32, (toks, toks), 1)
    flip = (turn_index == toks - 1).astype(bf16)
    offset_bias = dot_nn(table_ref[...], onehot[0 : table_ref.shape[1], :]).astype(bf16)
    revb[0:heads, 0:toks] = dot_nn(offset_bias[:, toks:lanes], flip)
    revb[0:heads, toks:lanes] = dot_nn(offset_bias[:, 0:toks], flip)

    settle(gland.at[pl.ds(0, 7)], gain_r)
    settle(gland.at[0], load_sem.at[1])
    for b in range(8):
        gcol[rows * b : rows * (b + 1), :] = gland[b].astype(f32)

    def norm_one(sl, carry):
        v = xt_ref[sl, :].astype(f32)
        n1t[sl, :] = (v * r1 * gcol[sl, 0:1]).astype(bf16)
        return carry

    gather_forward(("a", 0))
    do(1)
    over_rows(norm_one, 0)
    gather_swap(("a", 0))
    gather_forward(("a", 1))
    do(2)

    def compact(dst, half, col):
        @pl.loop(0, nbig)
        def _(i):
            both = jnp.concatenate(
                [
                    g[16 + half * 8 + 2 * i, :, col : col + aw].astype(f32),
                    g[16 + half * 8 + 2 * i + 1, :, col : col + aw].astype(f32),
                ],
                axis=0,
            )
            dst[pl.ds(pl.multiple_of(i * 2 * rows, 16), 2 * rows), :] = both.astype(bf16)

    gather_done(("a", 0))
    compact(wq, 0, 0)
    qt[...] = dot_tn(wq[...], n1t[...]).astype(bf16)
    compact(wk, 1, 0)
    kt[...] = dot_tn(wk[...], n1t[...]).astype(bf16)
    gather_swap(("a", 1))
    do(3)
    gather_done(("a", 1))
    compact(wv, 0, aw)
    vt[...] = dot_tn(wv[...], n1t[...]).astype(bf16)
    compact(wo, 1, aw)
    do(4)

    half_tok = toks // 2

    def softmax_block(h, head, block):
        keys = half_tok * (block + 1)
        low = half_tok * block
        row = jnp.broadcast_to(revb[pl.ds(h, 1), :], (half_tok, lanes))
        bias = pltpu.roll(row, (low - toks) % lanes, 1, stride=1, stride_axis=0)[:, :keys]
        scores = dot_tn(qt[head, low : low + half_tok], kt[head, 0:keys]) + bias
        e = jnp.exp(scores - jnp.max(scores, axis=1, keepdims=True))
        return e * (1.0 / jnp.sum(e, axis=1, keepdims=True)), low, keys

    def attend(h, carry):
        head = pl.ds(pl.multiple_of(h * hs, hs), hs)
        for block in (0, 1):
            p, low, keys = softmax_block(h, head, block)
            att[head, low : low + half_tok] = dot_nt(vt[head, 0:keys], p.astype(bf16)).astype(bf16)
        return carry

    lax.fori_loop(0, heads // 2, attend, 0)
    do(5)
    lax.fori_loop(heads // 2, heads, attend, 0)
    do(6)

    def branch_one(i, acc):
        sl = pl.ds(pl.multiple_of(i * big, 16), big)
        m = xt_ref[sl, :].astype(f32) + dot_nn(wo[sl, :], att[...])
        mid[sl, :] = m
        return acc + jnp.sum((m * m).reshape(big // 8, 8, toks), axis=0)

    ssum = jnp.sum(lax.fori_loop(0, nbig, branch_one, zero8), axis=0, keepdims=True)
    r2n = lax.rsqrt(ssum * (1.0 / width) + eps)

    def norm_two(sl, carry):
        m = mid[sl, :]
        n2t[sl, :] = (m * r2n * gcol[sl, 1:2]).astype(bf16)
        acc_o[sl, :] = m
        acc_n[sl, :] = jnp.zeros((tile, toks), f32)
        return carry

    over_rows(norm_two, 0)

    tok_tile = toks // 2

    parts = [(half, k) for half in (0, 1) for k in (0, 1, 2)]
    depth = 4

    def load(t, p):
        half, k = parts[p]
        return pltpu.make_async_copy(
            land_ref.at[pl.ds(t * 16 + half * 8, 8), :, pl.ds(k * sub, sub)],
            wload.at[pl.ds((p % depth) * 8, 8)],
            load_sem.at[p % depth],
        )

    def ffn_load(t):
        for p in range(depth):
            load(t, p).start()

    def ffn_chunk(t):
        slot = t % 2
        for p, (half, k) in enumerate(parts):
            load(t, p).wait()
            dst = (wg2, wu2, wd2)[k]

            @pl.loop(0, nbig)
            def _(i):
                base = (p % depth) * 8 + 2 * i
                both = jnp.concatenate([wload[base].astype(f32), wload[base + 1].astype(f32)], axis=0)
                sl = pl.ds(pl.multiple_of(i * big, 16), big)
                dst[sl, half * sub : (half + 1) * sub] = both.astype(bf16)

            if p + depth < len(parts):
                load(t, p + depth).start()

        @pl.loop(0, toks // tok_tile)
        def _(m):
            sl = pl.ds(pl.multiple_of(m * tok_tile, tok_tile), tok_tile)
            gate = dot_tn(n2t[:, sl], wg2[...])
            up = dot_tn(n2t[:, sl], wu2[...])
            gh = dot_tn(ct_ref[:, sl], wd2[...])
            k0 = 0.7978845608028654
            k1 = 0.044715
            sq = gate * gate
            th = jnp.tanh(k0 * (gate + k1 * (sq * gate)))
            half_one = 0.5 * (1.0 + th)
            act = gate * half_one
            slope = half_one + 0.5 * gate * (1.0 - th * th) * (k0 * (1.0 + 3.0 * k1 * sq))
            hid[sl, :] = (act * up).astype(bf16)
            dgt[sl, :] = (gh * up * slope).astype(bf16)
            dup[sl, :] = (gh * act).astype(bf16)

        @pl.loop(0, nbig)
        def _(i):
            sl = pl.ds(pl.multiple_of(i * big, 16), big)
            acc_o[sl, :] += dot_nt(wd2[sl, :], hid[...])
            acc_n[sl, :] += dot_nt(wg2[sl, :], dgt[...]) + dot_nt(wu2[sl, :], dup[...])
            for k, value in enumerate(
                (dot_nn(n2t[sl, :], dgt[...]), dot_nn(n2t[sl, :], dup[...]), dot_nn(ct_ref[sl, :], hid[...]))
            ):
                for half in (0, 1):
                    for j in (0, 1):
                        g[slot * 16 + half * 8 + 2 * i + j, :, k * sub : (k + 1) * sub] = value[
                            rows * j : rows * (j + 1), half * sub : (half + 1) * sub
                        ].astype(bf16)
            core_part(t, 2 * i, 2, fw)

    def ffn_step(t, carry):
        gather_done(("f", t))
        ffn_load(t)
        pl.when(t >= 1)(lambda: stored(t - 1, fw))
        do_in_loop(t, 0)
        pl.when(t >= 2)(lambda: slot_free(t - 2))
        ffn_chunk(t)
        do_in_loop(t, 1)
        plane_send(t, fw)
        return carry

    gather_sent(("a", 0))
    gather_sent(("a", 1))
    lax.fori_loop(0, chunks, ffn_step, 0)

    nv = chunks
    nq = chunks + 1
    stored(nv - 1, fw)
    do(tail_at)
    pick = lax.broadcasted_iota(jnp.int32, (8, toks), 0)

    def token_sums(row):
        chosen = (pick == row).astype(bf16)
        return dot_nt(chosen, wg2[...]) + dot_nt(chosen, wu2[...])

    def second_mean(sl, acc):
        return acc + fold(gcol[sl, 1:2] * acc_n[sl, :] * mid[sl, :])

    back = jnp.sum(over_rows(second_mean, zero8), axis=0, keepdims=True) * (1.0 / width)
    back = back * (r2n * r2n * r2n)

    def second_norm(sl, carry):
        m = mid[sl, :]
        gn = acc_n[sl, :]
        out_ref[sl, :] = acc_o[sl, :].astype(bf16)
        v = gn * m * r2n
        hi = v.astype(bf16)
        wg2[sl, :] = hi
        wu2[sl, :] = (v - hi.astype(f32)).astype(bf16)
        gm = ct_ref[sl, :].astype(f32) + r2n * gcol[sl, 1:2] * gn - m * back
        acc_n[sl, :] = gm
        n2t[sl, :] = gm.astype(bf16)
        return carry

    over_rows(second_norm, 0)
    sms[0] = jnp.zeros(sms.shape[1:], f32)
    sms[0, :, 0:width] = token_sums(1)
    do(tail_at + 1)

    dqt = dgt.at[pl.ds(0, aw)]
    dkt = dup.at[pl.ds(0, aw)]
    dat[...] = dot_tn(wo[...], n2t[...]).astype(bf16)

    def weight_grad(n, half, left, right):
        @pl.loop(0, nbig)
        def _(i):
            sl = pl.ds(pl.multiple_of(i * big, 16), big)
            value = dot_nt(left[sl, :], right[...])
            for j in (0, 1):
                g[(n % 2) * 16 + half * 8 + 2 * i + j, :, 0:aw] = value[rows * j : rows * (j + 1), :].astype(bf16)

    slot_free(5)
    weight_grad(nv, 1, n2t, att)
    do(tail_at + 2)
    hid[...] = (turn_index == toks - 1).astype(bf16)
    doff[...] = jnp.zeros(doff.shape, f32)

    def attend_back(h, carry):
        head = pl.ds(pl.multiple_of(h * hs, hs), hs)
        grad_v = []
        grad_k = []
        offsets = jnp.zeros((1, lanes), f32)
        for block in (0, 1):
            p, low, keys = softmax_block(h, head, block)
            q_rows = qt[head, low : low + half_tok]
            a_rows = dat[head, low : low + half_tok]
            grad_p = dot_tn(a_rows, vt[head, 0:keys])
            ds = (p * (grad_p - jnp.sum(p * grad_p, axis=1, keepdims=True))).astype(bf16)
            grad_v.append(dot_nn(a_rows, p.astype(bf16)))
            grad_k.append(dot_nn(q_rows, ds))
            dqt[head, low : low + half_tok] = dot_nt(kt[head, 0:keys], ds).astype(bf16)
            turned = dot_nn(ds, hid[0:keys, toks - keys : toks])
            padded = jnp.concatenate([turned, jnp.zeros((half_tok, lanes - keys), f32)], axis=1)
            lined = pltpu.roll(padded, half_tok, 1, stride=1, stride_axis=0)
            offsets = offsets + jnp.sum(lined, axis=0, keepdims=True)
        for dst, parts in ((dvt, grad_v), (dkt, grad_k)):
            dst[head, 0:half_tok] = (parts[0] + parts[1][:, 0:half_tok]).astype(bf16)
            dst[head, half_tok:toks] = parts[1][:, half_tok:toks].astype(bf16)
        doff[pl.ds(h, 1), :] = offsets
        return carry

    lax.fori_loop(0, heads // 2, attend_back, 0)
    do(tail_at + 3)
    lax.fori_loop(heads // 2, heads, attend_back, 0)
    weight_grad(nv, 0, n1t, dvt)
    core_part(nv, 0, 8, aw)
    slot_free(6)
    weight_grad(nq, 0, n1t, dqt)
    weight_grad(nq, 1, n1t, dkt)
    plane_send(nv, aw)
    core_part(nq, 0, 8, aw)
    stored(nv, aw)
    do(tail_at + 4)
    plane_send(nq, aw)
    stored(nq, aw)
    do(tail_at + 5)

    def first_back(i, acc):
        sl = pl.ds(pl.multiple_of(i * big, 16), big)
        gn = dot_nn(wq[sl, :], dqt[...]) + dot_nn(wk[sl, :], dkt[...]) + dot_nn(wv[sl, :], dvt[...])
        acc_o[sl, :] = gn
        v = gcol[sl, 0:1] * gn * xt_ref[sl, :].astype(f32)
        return acc + jnp.sum(v.reshape(big // 8, 8, toks), axis=0)

    back = jnp.sum(lax.fori_loop(0, nbig, first_back, zero8), axis=0, keepdims=True) * (1.0 / width)
    back = back * (r1 * r1 * r1)
    do(tail_at + 6)

    def first_norm(sl, carry):
        v = xt_ref[sl, :].astype(f32)
        gn = acc_o[sl, :]
        prod = gn * v * r1
        hi = prod.astype(bf16)
        wg2[sl, :] = hi
        wu2[sl, :] = (prod - hi.astype(f32)).astype(bf16)
        gtok_ref[sl, :] = (acc_n[sl, :] + r1 * gcol[sl, 0:1] * gn - v * back).astype(bf16)
        return carry

    over_rows(first_norm, 0)
    sms[0, :, 0:width] += token_sums(0)
    rest = doff[...]
    table = jnp.zeros((8, onehot.shape[0]), f32)
    for _ in range(3):
        part = rest.astype(bf16)
        table = table + dot_nt(part, onehot[...])
        rest = rest - part.astype(f32)
    sms[0, :, sms.shape[2] - onehot.shape[0] : sms.shape[2]] = table
    small_send(0)
    for k in range(7, TAIL_SLOTS):
        do(tail_at + k)
        if k < 13:
            small_step(k - 7)

    settle(gland.at[pl.ds(0, 7)], gain_s)
    slot_free(nv)
    slot_free(nq)
    turn_free(nv)
    turn_free(nq)
    for n in range(total):
        settle(span(hop_ref, 0, 4, width_of(n)), e1s.at[n])
    lax.fori_loop(0, chunks, lambda k, carry: (gather_sent(("f", k)), carry)[1], 0)

    @pl.when(outer)
    def _():
        for n in (nv - 1, nv, nq):
            sent(vbuf, zis, n)
        for n in range(total):
            for half in (0, 1):
                settle(cut1(ubuf, 0, width_of(n)), ur.at[n, half])

    @pl.when(inner)
    def _():
        for n in (nv, nq):
            u_free(n, aw)
        for n in range(total):
            settle(cut1(ubuf, 0, width_of(n)), ur.at[n, 1 - c])


def fused(tokens, cotangent, buckets, bias_table, gains, weights):
    toks, width = tokens.shape
    heads = bias_table.shape[1]
    rows, aw = weights[0].shape
    ff = weights[4].shape[1]
    sub = 256
    fw = 3 * sub
    chunks = ff // (2 * sub)
    total = chunks + 2
    lanes = 2 * toks
    small_lanes = (width + 127) // 128 * 128 + 128
    bucket_rows = jnp.pad(buckets, (0, 1), constant_values=-1)[None]
    vm = pl.BlockSpec(memory_space=pltpu.VMEM)
    hbm = pl.BlockSpec(memory_space=pltpu.HBM)
    dma = pltpu.SemaphoreType.DMA
    tok = lambda kind: pltpu.VMEM((width, toks), kind)
    inner_rows = pltpu.VMEM((aw, toks), bf16)
    blocks = lambda count: pltpu.VMEM((count, rows, fw), bf16)
    return pl.pallas_call(
        functools.partial(fused_kernel, chunks=chunks, heads=heads),
        out_shape=(
            jax.ShapeDtypeStruct((width, toks), bf16),
            jax.ShapeDtypeStruct((width, toks), bf16),
            jax.ShapeDtypeStruct((8, small_lanes), f32),
            *([jax.ShapeDtypeStruct((rows, aw), bf16)] * 4),
            *([jax.ShapeDtypeStruct((rows, ff), bf16)] * 3),
            jax.ShapeDtypeStruct((chunks * 16, rows, fw), bf16),
            jax.ShapeDtypeStruct((total * 8, rows, fw), bf16),
            jax.ShapeDtypeStruct((total * 4, rows, fw), bf16),
            jax.ShapeDtypeStruct((total * 2, rows, fw), bf16),
        ),
        in_specs=[vm] * 5 + [hbm] * 7,
        out_specs=[vm] * 3 + [hbm] * 11,
        scratch_shapes=[
            pltpu.VMEM((8, rows, 128), bf16),
            pltpu.VMEM((width, 128), f32),
            tok(bf16),
            tok(bf16),
            tok(f32),
            tok(f32),
            tok(f32),
            *([inner_rows] * 6),
            *([pltpu.VMEM((width, aw), bf16)] * 4),
            *([pltpu.VMEM((width, 2 * sub), bf16)] * 3),
            pltpu.VMEM((32, rows, sub), bf16),
            blocks(32),
            *([pltpu.VMEM((toks, 2 * sub), bf16)] * 3),
            blocks(16),
            blocks(8),
            blocks(6),
            blocks(6),
            blocks(4),
            blocks(6),
            blocks(4),
            pltpu.VMEM((8, lanes), f32),
            pltpu.VMEM((128, lanes), bf16),
            pltpu.VMEM((8, lanes), f32),
            pltpu.VMEM((6, 8, small_lanes), f32),
            pltpu.VMEM((6, 8, small_lanes), f32),
            dma(()),
            dma(()),
            *([dma((total,))] * 5),
            dma((4,)),
            *([dma((total,))] * 2),
            dma((total, 8)),
            dma((6,)),
            dma((total,)),
            dma((total, 2)),
            *([dma((total,))] * 2),
            *([dma((total, 2))] * 4),
            dma((total, 3)),
            dma((total,)),
            dma((total, 2)),
            dma((6,)),
            dma((6,)),
            pltpu.SemaphoreType.REGULAR,
            pltpu.SemaphoreType.REGULAR,
        ],
        compiler_params=pltpu.CompilerParams(
            collective_id=0, has_side_effects=True, vmem_limit_bytes=60 * 2**20
        ),
        cost_estimate=pl.CostEstimate(flops=57 * 10**9, bytes_accessed=10**8, transcendentals=10**7),
    )(tokens.T, cotangent.T, bucket_rows, bias_table.T, gains, *weights)


def widen_kernel(*refs):
    count = len(refs) // 2
    for src, dst in zip(refs[: count - 1], refs[count:-1]):
        dst[...] = src[...].astype(dst.dtype)
    sums, table = refs[count - 1], refs[-1]
    lane = sums.shape[1] - 128
    table[...] = sums[0 : table.shape[0], lane : lane + table.shape[1]]


def widen(out, gtok, grads, sums, table_shape):
    steps = 4
    width, toks = out.shape
    rows, ff = grads[-1].shape
    act = pl.BlockSpec((width // steps, toks), lambda i: (i, 0))
    small = pl.BlockSpec(grads[0].shape, lambda i: (0, 0))
    large = pl.BlockSpec((rows, ff // steps), lambda i: (0, i))
    specs = [act] * 2 + [small] * 4 + [large] * 3
    whole = lambda shape: pl.BlockSpec(shape, lambda i: (0, 0))
    return pl.pallas_call(
        widen_kernel,
        grid=(steps,),
        out_shape=[jax.ShapeDtypeStruct(v.shape, bf16) for v in (out, gtok)]
        + [jax.ShapeDtypeStruct(v.shape, f32) for v in grads]
        + [jax.ShapeDtypeStruct(table_shape, f32)],
        in_specs=specs + [whole(sums.shape)],
        out_specs=specs + [whole(table_shape)],
        compiler_params=pltpu.CompilerParams(vmem_limit_bytes=60 * 2**20),
        cost_estimate=pl.CostEstimate(flops=10**7, bytes_accessed=2 * 10**7, transcendentals=0),
    )(out, gtok, *grads, sums)


def fused_body(
    tokens,
    cotangent,
    buckets,
    bias_table,
    attn_gain,
    w_query,
    w_key,
    w_value,
    w_output,
    ffn_gain,
    w_gate,
    w_up,
    w_down,
):
    rows = w_query.shape[0]
    lane = lax.broadcasted_iota(jnp.int32, (rows, 128), 1)
    gains = jnp.where(lane == 0, attn_gain[:, None], ffn_gain[:, None])
    weights = (w_query, w_key, w_value, w_output, w_gate, w_up, w_down)
    out, gtok, small, *grads = fused(tokens, cotangent, buckets, bias_table, gains, weights)
    out, gtok, *grads, table = widen(out, gtok, grads[:7], small, bias_table.shape[::-1])
    own = lax.dynamic_slice(small, (0, lax.axis_index("shard") * rows), (2, rows))
    return (out.T, gtok.T, own[0], *grads[:4], own[1], *grads[4:], table.T)


def solution(mesh):
    chosen = body
    if mesh.shape["shard"] == 8 and mesh.shape["rep"] == 4:
        chosen = fused_body
    return jax.shard_map(
        chosen,
        mesh=mesh,
        in_specs=(
            P(("shard", "rep"), None),
            P(("shard", "rep"), None),
            P(),
            P(),
            P("shard"),
            P("shard", None),
            P("shard", None),
            P("shard", None),
            P("shard", None),
            P("shard"),
            P("shard", None),
            P("shard", None),
            P("shard", None),
        ),
        out_specs=(
            P(("shard", "rep"), None),
            P(("shard", "rep"), None),
            P("shard"),
            P("shard", None),
            P("shard", None),
            P("shard", None),
            P("shard", None),
            P("shard"),
            P("shard", None),
            P("shard", None),
            P("shard", None),
            P(),
        ),
        check_vma=False,
    )
```
